32 devices in a mesh: list: 4 (over z), fsdp: 8 (over y, x, core).
Axes of the slice: x: 2, y: 2, z: 4, core: 2. Of those that a mesh axis runs over, the one named last changes fastest.
Arguments:
- hidden: bfloat16 [512, 64, 2048], P(('list', 'fsdp')), may hold values from -6 to 6
- norm_gain: float32 [2048], replicated, may hold values from 0.5 to 1.5
- w_qkv: bfloat16 [2048, 1536], P('fsdp'), may hold values from -0.125 to 0.125
- w_out: bfloat16 [1024, 2048], P('fsdp'), may hold values from -0.1875 to 0.1875
- final_gain: float32 [2048], replicated, may hold values from 0.5 to 1.5
- w_score: float32 [2048], replicated, may hold values from -0.125 to 0.125
- prior: float32 [512], P(('list', 'fsdp')), may hold values from -8 to 400
- labels: int32 [512], P(('list', 'fsdp')), may hold values from 0 to 3
- lengths: int32 [16], replicated, may hold values from 1 to 48, 512 in all
Outputs:
- loss: float32 [], replicated
- grad_qkv: float32 [2048, 1536], P('fsdp', 'list')
- grad_out: float32 [1024, 2048], P('fsdp', 'list')
The draws below stay inside these ranges and needn't reach their ends.
Inputs may be any that keep to these rules, and one draw needn't show every extreme that they name: `lengths`: the longest list holds exactly 48 passages.
All inputs are finite; a program needn't handle non-finite values.
Results may differ from the reference program's by a relative error of at most 0.025.
Values may be sent and summed in bfloat16 or wider, within the bound.
No kernel may reach another device: no remote copies, remote signals or barrier semaphores. Data moves between devices by JAX's collectives and lax.ppermute only.
A program may use at most 128 MiB of HBM per device.

```python
import math
import jax
import jax.numpy as jnp
import numpy as np
from jax import lax

D = 2048
HEADS = 16
KV_HEADS = 4
HEAD_DIM = 64
PASSAGE_LEN = 64
LONGEST = 48
PASSAGES_DEV = 16
PASSAGES = 512
QUERIES = 16
N_LIST = 4
N_FSDP = 8


def draw_prior(key, part):
    second_key = jax.random.fold_in(jax.random.fold_in(key, 17), 1)
    return jnp.clip(jax.random.normal(second_key, (PASSAGES,), jnp.float32), -6.0, 6.0)


def plant(result, rng, low, high):
    spot = [jax.random.randint(jax.random.fold_in(rng, axis), (), 0, length) for axis, length in enumerate(result.shape)]
    longest = result.shape.index(max(result.shape))
    next_to = spot[:longest] + [(spot[longest] + 1) % result.shape[longest]] + spot[longest + 1:]
    return result.at[tuple(spot)].set(low).at[tuple(next_to)].set(high)


def block_scale(rng, extent, cuts, least, top_value):
    factor_of = 1.0
    for axis_at, shards_of in cuts:
        steps = jax.random.uniform(jax.random.fold_in(jax.random.fold_in(rng, 6), axis_at), (shards_of,), jnp.float32, least / len(cuts), top_value / len(cuts))
        factor_of = factor_of * jnp.repeat(jnp.exp(steps), extent[axis_at] // shards_of).reshape((-1,) + (1,) * (len(extent) - 1 - axis_at))
    return factor_of


def profile(number_of, total, reach, skew):
    portions = [(1 << 20) // math.isqrt(standing ** skew) + 1 for standing in range(2, number_of + 1)]
    spare, given = total - reach - (number_of - 1), [1] * (number_of - 1)
    while spare > 0:
        free = [i for i in range(number_of - 1) if given[i] < reach]
        pool, left = sum([portions[i] for i in free]), spare
        for i in free:
            addition = min(reach - given[i], max(1, left * portions[i] // pool), spare)
            given[i] = given[i] + addition
            spare = spare - addition
    return np.array([reach] + given)


def uneven(rng, amount, total, bound, slope):
    if amount == 2:
        one = jax.random.randint(rng, (), max(1, total - bound), min(bound, total - 1) + 1)
        return jnp.stack([one, total - one])
    sizes = jnp.asarray(profile(amount, total, bound, slope), jnp.int32)
    twos = (amount - 1) // 2
    donor, taker = sizes[1:1 + 2 * twos:2], sizes[2:2 + 2 * twos:2]
    slack = jnp.minimum(donor - 1, bound - taker)
    moved = jax.random.randint(jax.random.fold_in(rng, 1), (twos,), 0, 1 << 20) % (slack + 1)
    sizes = sizes.at[1:1 + 2 * twos:2].set(donor - moved).at[2:2 + 2 * twos:2].set(taker + moved)
    return sizes[jax.random.permutation(jax.random.fold_in(rng, 2), amount)]


def scatter_about(own_key, extent, deviation, bound, shards=(), kind=jnp.bfloat16):
    drawn = deviation * jax.random.normal(own_key, extent, jnp.float32)
    if shards:
        drawn = drawn * block_scale(own_key, extent, shards, -0.22, 0.18)
    return jnp.clip(drawn, -bound, bound).astype(kind)


def setup_inputs(seed: int = 0) -> dict:
    seeds = jax.random.split(jax.random.key(seed), 10)
    return {
        "hidden": scatter_about(seeds[0], (PASSAGES, PASSAGE_LEN, D), 1.0, 6.0, ((0, 32),)),
        "norm_gain": jnp.clip(1.0 + 0.1 * jax.random.normal(seeds[1], (D,), jnp.float32), 0.5, 1.5),
        "w_qkv": scatter_about(seeds[2], (D, HEADS * HEAD_DIM + 2 * KV_HEADS * HEAD_DIM), D ** -0.5, 0.125, ((0, 8),)),
        "w_out": scatter_about(seeds[3], (HEADS * HEAD_DIM, D), (HEADS * HEAD_DIM) ** -0.5, 0.1875, ((0, 8),)),
        "final_gain": jnp.clip(1.0 + 0.1 * jax.random.normal(seeds[4], (D,), jnp.float32), 0.5, 1.5),
        "w_score": scatter_about(seeds[5], (D,), D ** -0.5, 0.125, (), jnp.float32),
        "prior": draw_prior(jax.random.fold_in(seeds[9], 71), 0),
        "labels": plant(jax.random.randint(seeds[7], (PASSAGES,), 0, 4), jax.random.fold_in(seeds[7], 1), 0, 3).astype(jnp.int32),
        "lengths": uneven(seeds[8], QUERIES, PASSAGES, LONGEST, 1).astype(jnp.int32),
    }


epsilon = 1e-05
loss_scale = 64.0

def forward_block(block, prior_part, norm_gain, w_qkv, w_out, final_gain, w_score):
    passages = block.shape[0]
    width_q = HEADS * HEAD_DIM
    width_k = KV_HEADS * HEAD_DIM
    ratio = HEADS // KV_HEADS
    values = block.astype(jnp.float32)
    mean_square = lax.optimization_barrier(jnp.mean(values * values, -1, keepdims=True))
    normal_rows = (values * lax.rsqrt(mean_square + epsilon) * norm_gain).astype(jnp.bfloat16)
    normal_rows = normal_rows.reshape(passages * PASSAGE_LEN, D)
    projected = jnp.dot(normal_rows, w_qkv, preferred_element_type=jnp.float32).astype(jnp.bfloat16)
    query_part = projected[:, :width_q].reshape(passages, PASSAGE_LEN, KV_HEADS, ratio, HEAD_DIM)
    key_part = projected[:, width_q:width_q + width_k].reshape(passages, PASSAGE_LEN, KV_HEADS, HEAD_DIM)
    value_part = projected[:, width_q + width_k:].reshape(passages, PASSAGE_LEN, KV_HEADS, HEAD_DIM)
    scores = jnp.einsum('bqgre,bkge->bgrqk', query_part.astype(jnp.float32), key_part.astype(jnp.float32)) * HEAD_DIM ** (-0.5)
    peak = lax.optimization_barrier(jnp.max(scores, -1, keepdims=True))
    expo = jnp.exp(scores - peak)
    probs = (expo / lax.optimization_barrier(jnp.sum(expo, -1, keepdims=True))).astype(jnp.bfloat16)
    attended = jnp.einsum('bgrqk,bkge->bqgre', probs.astype(jnp.float32), value_part.astype(jnp.float32)).astype(jnp.bfloat16)
    attended = attended.reshape(passages, PASSAGE_LEN, width_q)
    mixed = jnp.dot(attended.reshape(passages * PASSAGE_LEN, width_q), w_out, preferred_element_type=jnp.float32)
    residual = values + mixed.reshape(passages, PASSAGE_LEN, D)
    pooled = lax.optimization_barrier(jnp.mean(residual, 1))
    inverse = lax.rsqrt(lax.optimization_barrier(jnp.mean(pooled * pooled, -1, keepdims=True)) + epsilon)
    unit = pooled * inverse
    score = lax.optimization_barrier(jnp.sum(unit * final_gain * w_score, -1)) + prior_part
    return (score, normal_rows, query_part, key_part, value_part, probs, attended, unit, inverse)

def backward_block(saved, d_score, w_out, final_gain, w_score):
    score, normal_rows, query_part, key_part, value_part, probs, attended, unit, inverse = saved
    passages = attended.shape[0]
    d_unit = d_score[:, None] * w_score[None, :] * final_gain[None, :]
    d_pooled = inverse * (d_unit - unit * lax.optimization_barrier(jnp.mean(d_unit * unit, -1, keepdims=True)))
    d_rows = (d_pooled / PASSAGE_LEN).astype(jnp.bfloat16)
    attn_sum = lax.optimization_barrier(jnp.sum(attended, 1, dtype=jnp.float32)).astype(jnp.bfloat16)
    d_attended = jnp.dot(d_rows, w_out.T, preferred_element_type=jnp.float32).astype(jnp.bfloat16)
    d_heads = d_attended.reshape(passages, KV_HEADS, HEADS // KV_HEADS, HEAD_DIM).astype(jnp.float32)
    d_probs = jnp.einsum('bgre,bkge->bgrk', d_heads, value_part.astype(jnp.float32))
    probs_f = probs.astype(jnp.float32)
    inner = lax.optimization_barrier(jnp.sum(probs_f * d_probs[:, :, :, None, :], -1, keepdims=True))
    d_scores = (probs_f * (d_probs[:, :, :, None, :] - inner) * HEAD_DIM ** (-0.5)).astype(jnp.bfloat16)
    d_scores_f = d_scores.astype(jnp.float32)
    d_query = jnp.einsum('bgrqk,bkge->bqgre', d_scores_f, key_part.astype(jnp.float32)).astype(jnp.bfloat16)
    d_key = jnp.einsum('bgrqk,bqgre->bkge', d_scores_f, query_part.astype(jnp.float32)).astype(jnp.bfloat16)
    d_value = jnp.einsum('bgrqk,bgre->bkge', probs_f, d_heads).astype(jnp.bfloat16)
    rows = passages * PASSAGE_LEN
    d_projected = jnp.concatenate([d_query.reshape(rows, -1), d_key.reshape(rows, -1), d_value.reshape(rows, -1)], 1)
    term_qkv = jnp.dot(normal_rows.T, d_projected, preferred_element_type=jnp.float32)
    term_out = jnp.dot(attn_sum.T, d_rows, preferred_element_type=jnp.float32)
    return (term_qkv, term_out)

def reference(hidden, norm_gain, w_qkv, w_out, final_gain, w_score, prior, labels, lengths):
    devices = N_LIST * N_FSDP
    blocks = hidden.reshape(devices, PASSAGES_DEV, PASSAGE_LEN, D)
    prior_blocks = prior.reshape(devices, PASSAGES_DEV)

    def scores_only(operands):
        return forward_block(operands[0], operands[1], norm_gain, w_qkv, w_out, final_gain, w_score)[0]
    score = lax.map(scores_only, (blocks, prior_blocks)).reshape(PASSAGES)
    position = jnp.arange(PASSAGES, dtype=jnp.int32)
    ends = jnp.cumsum(lengths).astype(jnp.int32)
    owner = lax.optimization_barrier(jnp.sum((position[:, None] >= ends[None, :]).astype(jnp.int32), 1))
    member = (owner[:, None] == jnp.arange(QUERIES, dtype=jnp.int32)[None, :]).astype(jnp.float32)
    peak = lax.optimization_barrier(jnp.max(jnp.where(member > 0, score[:, None], -1e+30), 0))
    own_peak = lax.optimization_barrier(jnp.sum(member * peak[None, :], 1))
    total = lax.optimization_barrier(jnp.sum(member * jnp.exp(score - own_peak)[:, None], 0))
    label_weight = jnp.exp(labels.astype(jnp.float32))
    label_total = lax.optimization_barrier(jnp.sum(member * label_weight[:, None], 0))
    log_norm = peak + jnp.log(total)
    log_prob = score - lax.optimization_barrier(jnp.sum(member * log_norm[None, :], 1))
    target = label_weight / lax.optimization_barrier(jnp.sum(member * label_total[None, :], 1))
    loss = -loss_scale * jnp.sum(target * log_prob)
    d_score = loss_scale * (jnp.exp(log_prob) - target)
    d_blocks = d_score.reshape(devices, PASSAGES_DEV)

    def accumulate(carry, operands):
        block, prior_part, d_part = operands
        saved = forward_block(block, prior_part, norm_gain, w_qkv, w_out, final_gain, w_score)
        term_qkv, term_out = backward_block(saved, d_part, w_out, final_gain, w_score)
        term_qkv = lax.optimization_barrier(term_qkv.astype(jnp.bfloat16)).astype(jnp.float32)
        return ((carry[0] + term_qkv, carry[1] + term_out), None)
    start = (jnp.zeros(w_qkv.shape, jnp.float32), jnp.zeros(w_out.shape, jnp.float32))
    grads, _ = lax.scan(accumulate, start, (blocks, prior_blocks, d_blocks))
    return (loss, grads[0], grads[1])
```

```python
import functools

import jax
import jax.numpy as jnp
from jax import lax
from jax.experimental import pallas as pl
from jax.experimental.pallas import tpu as pltpu
from jax.sharding import PartitionSpec as P

HEADS = 16
KV_HEADS = 4
HEAD_DIM = 64
PASSAGE_LEN = 64
LONGEST = 48
RATIO = HEADS // KV_HEADS
GROUP = RATIO * HEAD_DIM

epsilon = 1e-05
loss_scale = 64.0
scale = HEAD_DIM ** (-0.5)
VMEM = 48 * 1024 * 1024
BF16 = jnp.bfloat16
F32 = jnp.float32


def params(grid=1):
    return pltpu.CompilerParams(
        vmem_limit_bytes=VMEM, dimension_semantics=("arbitrary",) * grid
    )


def mm(a, b, dims=((1,), (0,))):
    return lax.dot_general(a, b, (dims, ((), ())), preferred_element_type=F32)


def norm_kernel(hidden_ref, gain_ref, normal_ref, sum_ref):
    values = hidden_ref[...].astype(F32)
    mean_square = jnp.mean(values * values, -1, keepdims=True)
    out = values * lax.rsqrt(mean_square + epsilon) * gain_ref[...][None]
    normal_ref[...] = out.astype(BF16)
    sum_ref[0] = jnp.sum(values, 1)


def norm(hidden, gain):
    passages, length, width = hidden.shape
    step = 4 if passages % 4 == 0 else 1
    steps = passages // step
    normal, sums = pl.pallas_call(
        norm_kernel,
        grid=(steps,),
        in_specs=[
            pl.BlockSpec((step, length, width), lambda i: (i, 0, 0)),
            pl.BlockSpec((1, width), lambda i: (0, 0)),
        ],
        out_specs=[
            pl.BlockSpec((step, length, width), lambda i: (i, 0, 0)),
            pl.BlockSpec((1, step, width), lambda i: (i, 0, 0)),
        ],
        out_shape=[
            jax.ShapeDtypeStruct((passages, length, width), BF16),
            jax.ShapeDtypeStruct((steps, step, width), F32),
        ],
        compiler_params=params(),
        cost_estimate=pl.CostEstimate(
            flops=6 * hidden.size, bytes_accessed=4 * hidden.size, transcendentals=0
        ),
        name="norm_rows",
    )(hidden, gain[None])
    return normal.reshape(passages * length, width), sums.reshape(passages, width)


def block_mask(rows, cols):
    row = lax.broadcasted_iota(jnp.int32, (rows, cols), 0) // HEAD_DIM
    col = lax.broadcasted_iota(jnp.int32, (rows, cols), 1) // HEAD_DIM
    return row == col


def doubled(pair, low):
    wide = pair.astype(F32)
    turned = pltpu.roll(wide, HEAD_DIM, 1)
    return jnp.where(low, wide, turned).astype(BF16), jnp.where(low, turned, wide).astype(BF16)


def spread(double, mask):
    row = jnp.concatenate([double] * (RATIO // 2), 1)
    return jnp.where(mask, jnp.concatenate([row] * RATIO, 0), jnp.zeros((), BF16))


def low_lanes():
    return lax.broadcasted_iota(jnp.int32, (HEAD_DIM, 2 * HEAD_DIM), 1) < HEAD_DIM


def segment_max(scores, low):
    tiles = []
    for start in range(0, scores.shape[1], 2 * HEAD_DIM):
        tile = scores[:, start : start + 2 * HEAD_DIM]
        first = jnp.max(jnp.where(low, tile, -jnp.inf), 1, keepdims=True)
        second = jnp.max(jnp.where(low, -jnp.inf, tile), 1, keepdims=True)
        tiles.append(jnp.where(low, first, second))
    return jnp.concatenate(tiles, 1)


def forward_kernel(pieces, groups, where_ref, rows_ref, *refs):
    weights = refs[: 2 * pieces]
    projected_ref, probs_ref, sum_ref = refs[2 * pieces :]
    chip = where_ref[0]
    depth = weights[0].shape[0]
    first, second = None, None
    for s in range(pieces):
        start = pl.multiple_of((chip ^ s) * depth, depth)
        block = rows_ref[:, pl.ds(start, depth)]
        a, b = mm(block, weights[2 * s][...]), mm(block, weights[2 * s + 1][...])
        first = a if first is None else first + a
        second = b if second is None else second + b
    projected = jnp.concatenate([first, second], 1).astype(BF16)
    projected_ref[...] = projected
    low = low_lanes()
    mask = block_mask(GROUP, GROUP)
    ones = jnp.where(mask, 1.0, 0.0).astype(BF16)
    width_q = groups * GROUP
    width_k = groups * HEAD_DIM
    for i in range(rows_ref.shape[0] // PASSAGE_LEN):
        rows = slice(i * PASSAGE_LEN, (i + 1) * PASSAGE_LEN)
        keys = doubled(projected[rows, width_q : width_q + width_k], low)
        values = doubled(projected[rows, width_q + width_k :], low)
        for g in range(groups):
            cols = slice(g * GROUP, (g + 1) * GROUP)
            scores = mm(projected[rows, cols], spread(keys[g], mask), ((1,), (1,))) * scale
            expo = jnp.exp(scores - segment_max(scores, low))
            total = mm(expo.astype(BF16), ones)
            probs = (expo / total).astype(BF16)
            probs_ref[rows, cols] = probs
            attended = mm(probs, spread(values[g], mask)).astype(BF16).astype(F32)
            sum_ref[0, i : i + 1, cols] = jnp.sum(attended, 0, keepdims=True)


def forward(where, rows, weights, groups):
    total, width = rows.shape
    pieces = len(weights)
    flat = [part for s in range(pieces) for part in weights[s]]
    out_width = flat[0].shape[1] + flat[1].shape[1]
    step = 4 * PASSAGE_LEN if total % (4 * PASSAGE_LEN) == 0 else PASSAGE_LEN
    steps, per = total // step, step // PASSAGE_LEN
    heads = groups * GROUP
    projected, probs, sums = pl.pallas_call(
        functools.partial(forward_kernel, pieces, groups),
        grid_spec=pltpu.PrefetchScalarGridSpec(
            num_scalar_prefetch=1,
            grid=(steps,),
            in_specs=[pl.BlockSpec((step, width), lambda i, w: (i, 0))]
            + [pl.BlockSpec(part.shape, lambda i, w: (0, 0)) for part in flat],
            out_specs=[
                pl.BlockSpec((step, out_width), lambda i, w: (i, 0)),
                pl.BlockSpec((step, heads), lambda i, w: (i, 0)),
                pl.BlockSpec((1, per, heads), lambda i, w: (i, 0, 0)),
            ],
        ),
        out_shape=[
            jax.ShapeDtypeStruct((total, out_width), BF16),
            jax.ShapeDtypeStruct((total, heads), BF16),
            jax.ShapeDtypeStruct((steps, per, heads), F32),
        ],
        compiler_params=params(),
        cost_estimate=pl.CostEstimate(
            flops=2 * total * width * out_width,
            bytes_accessed=2 * (rows.size + width * out_width + total * (out_width + heads)),
            transcendentals=total * heads,
        ),
        name="project_attend",
    )(where, rows, *flat)
    return projected, probs, sums.reshape(steps * per, heads)


def folded(first, second, low):
    half = HEAD_DIM
    kept = jnp.where(low, first[:half], first[half:]) + jnp.where(low, second[:half], second[half:])
    return kept + pltpu.roll(kept, half, 1)


def backward_kernel(groups, probs_ref, projected_ref, d_ref, out_ref):
    low = low_lanes()
    mask = block_mask(GROUP, GROUP)
    ones = jnp.where(mask, 1.0, 0.0).astype(BF16)
    width_q = groups * GROUP
    width_k = groups * HEAD_DIM
    half = GROUP // 2
    for i in range(probs_ref.shape[0] // PASSAGE_LEN):
        rows = slice(i * PASSAGE_LEN, (i + 1) * PASSAGE_LEN)
        keys = doubled(projected_ref[rows, width_q : width_q + width_k], low)
        values = doubled(projected_ref[rows, width_q + width_k :], low)
        d_keys, d_values = [], []
        for g in range(groups):
            cols = slice(g * GROUP, (g + 1) * GROUP)
            probs = probs_ref[rows, cols]
            queries = projected_ref[rows, cols]
            d_rows = jnp.broadcast_to(d_ref[0, i : i + 1, cols], (PASSAGE_LEN, GROUP)).astype(BF16)
            d_probs = mm(d_rows[:16], spread(values[g], mask), ((1,), (1,)))[:1]
            probs_f = probs.astype(F32)
            product = probs_f * d_probs
            upper = product.astype(BF16)
            lower = (product - upper.astype(F32)).astype(BF16)
            inner = mm(upper, ones) + mm(lower, ones)
            d_scores = (probs_f * (d_probs - inner) * scale).astype(BF16)
            out_ref[rows, cols] = mm(d_scores, spread(keys[g], mask)).astype(BF16)
            down = ((0,), (0,))
            d_keys.append(
                folded(
                    mm(d_scores[:, :half], queries[:, :half], down),
                    mm(d_scores[:, half:], queries[:, half:], down),
                    low,
                )
            )
            d_values.append(
                folded(
                    mm(probs[:, :half], d_rows[:, :half], down),
                    mm(probs[:, half:], d_rows[:, half:], down),
                    low,
                )
            )
        out_ref[rows, width_q : width_q + width_k] = jnp.where(low, *d_keys).astype(BF16)
        out_ref[rows, width_q + width_k :] = jnp.where(low, *d_values).astype(BF16)


def backward(probs, projected, d_attended, groups):
    total, heads = probs.shape
    out_width = projected.shape[1]
    step = 4 * PASSAGE_LEN if total % (4 * PASSAGE_LEN) == 0 else PASSAGE_LEN
    steps, per = total // step, step // PASSAGE_LEN
    return pl.pallas_call(
        functools.partial(backward_kernel, groups),
        grid=(steps,),
        in_specs=[
            pl.BlockSpec((step, heads), lambda i: (i, 0)),
            pl.BlockSpec((step, out_width), lambda i: (i, 0)),
            pl.BlockSpec((1, per, heads), lambda i: (i, 0, 0)),
        ],
        out_specs=pl.BlockSpec((step, out_width), lambda i: (i, 0)),
        out_shape=jax.ShapeDtypeStruct((total, out_width), BF16),
        compiler_params=params(),
        cost_estimate=pl.CostEstimate(
            flops=16 * total * heads * GROUP,
            bytes_accessed=2 * total * (heads + 2 * out_width),
            transcendentals=0,
        ),
        name="attend_back",
    )(probs, projected, d_attended.astype(F32).reshape(steps, per, heads))


def score_kernel(where_ref, mine_ref, other_ref, sum_ref, w_ref, final_ref, ws_ref, prior_ref,
                 unit_ref, inverse_ref, score_ref, attn_ref):
    core = where_ref[1]
    mine, other = mine_ref[...], other_ref[...]
    attn = jnp.concatenate(
        [jnp.where(core == 0, mine, other), jnp.where(core == 0, other, mine)], 1
    )
    count = attn.shape[0]
    upper = attn.astype(BF16)
    lower = (attn - upper.astype(F32)).astype(BF16)
    product = mm(jnp.concatenate([upper, lower], 0), w_ref[...])
    pooled = (sum_ref[...] + product[:count] + product[count:]) * (1.0 / PASSAGE_LEN)
    inverse = lax.rsqrt(jnp.mean(pooled * pooled, -1, keepdims=True) + epsilon)
    unit = pooled * inverse
    score = jnp.sum(unit * (final_ref[...] * ws_ref[...]), -1, keepdims=True)
    unit_ref[...] = unit
    inverse_ref[...] = jnp.broadcast_to(inverse, inverse_ref.shape)
    score_ref[...] = score + prior_ref[...]
    attn_ref[...] = upper


def score_pass(where, mine, other, sums, w_out, final_gain, w_score, prior):
    count, width = sums.shape
    lanes = prior.shape[1]
    inner = w_out.shape[0]
    vmem = pl.BlockSpec(memory_space=pltpu.VMEM)
    return pl.pallas_call(
        score_kernel,
        in_specs=[pl.BlockSpec(memory_space=pltpu.SMEM)] + [vmem] * 7,
        out_specs=[vmem] * 4,
        out_shape=[
            jax.ShapeDtypeStruct((count, width), F32),
            jax.ShapeDtypeStruct((count, lanes), F32),
            jax.ShapeDtypeStruct((count, lanes), F32),
            jax.ShapeDtypeStruct((count, inner), BF16),
        ],
        compiler_params=pltpu.CompilerParams(vmem_limit_bytes=VMEM),
        cost_estimate=pl.CostEstimate(
            flops=4 * count * width * inner, bytes_accessed=2 * w_out.size, transcendentals=0
        ),
        name="pool_score",
    )(where, mine, other, sums, w_out, final_gain[None], w_score[None], prior)


def list_kernel(blocks, passages, where_ref, place_ref, bounds_ref, unit_ref, inverse_ref, w_ref,
                final_ref, ws_ref, *refs):
    scores = [ref[...] for ref in refs[:blocks]]
    weights = [ref[...] for ref in refs[blocks : 2 * blocks]]
    d_rows_ref, d_att_ref, loss_ref = refs[2 * blocks :]
    core = where_ref[1]
    starts, ends = bounds_ref[0:1], bounds_ref[1:2]
    pair = 2 * passages
    lanes = starts.shape[1]
    row = lax.broadcasted_iota(jnp.int32, (pair, lanes), 0)
    offset = jnp.where(
        row < passages, core * passages + row, (1 - core) * passages + row - passages
    )
    members = []
    for j in range(blocks):
        place = place_ref[j] * pair + offset
        members.append((place >= starts) & (place < ends))
    column = [jnp.broadcast_to(score[:, :1], (pair, lanes)) for score in scores]
    heavy = [jnp.broadcast_to(weight[:, :1], (pair, lanes)) for weight in weights]
    peak = functools.reduce(
        jnp.maximum,
        [jnp.max(jnp.where(m, s, -1e30), 0, keepdims=True) for m, s in zip(members, column)],
    )
    total = sum(
        jnp.sum(jnp.where(m, jnp.exp(jnp.where(m, s - peak, 0.0)), 0.0), 0, keepdims=True)
        for m, s in zip(members, column)
    )
    label_total = sum(
        jnp.sum(jnp.where(m, w, 0.0), 0, keepdims=True) for m, w in zip(members, heavy)
    )
    log_norm = peak + jnp.log(total)
    own = members[0]
    log_prob = column[0][:, :1] - jnp.sum(jnp.where(own, log_norm, 0.0), 1, keepdims=True)
    target = heavy[0][:, :1] / jnp.sum(jnp.where(own, label_total, 0.0), 1, keepdims=True)
    loss = -loss_scale * jnp.sum((target * log_prob)[:passages], 0, keepdims=True)
    loss_ref[...] = jnp.broadcast_to(loss, loss_ref.shape)
    d_score = loss_scale * (jnp.exp(log_prob) - target)
    unit = unit_ref[...]
    d_unit = d_score * (ws_ref[...] * final_ref[...])
    mean = jnp.mean(d_unit * unit, -1, keepdims=True)
    d_pooled = inverse_ref[:, :1] * (d_unit - unit * mean)
    d_rows = (d_pooled * (1.0 / PASSAGE_LEN)).astype(BF16)
    d_rows_ref[...] = d_rows
    d_att = mm(d_rows, w_ref[...], ((1,), (1,))).astype(BF16).astype(F32)
    half = d_att.shape[1] // 2
    d_att_ref[...] = jnp.where(core == 0, d_att[:, :half], d_att[:, half:])


def list_pass(where, places, bounds, unit, inverse, w_out, final_gain, w_score, scores, weights,
              passages):
    count, width = unit.shape
    inner = w_out.shape[0]
    vmem = pl.BlockSpec(memory_space=pltpu.VMEM)
    smem = pl.BlockSpec(memory_space=pltpu.SMEM)
    return pl.pallas_call(
        functools.partial(list_kernel, len(scores), passages),
        in_specs=[smem] * 2 + [vmem] * (6 + 2 * len(scores)),
        out_specs=[vmem] * 3,
        out_shape=[
            jax.ShapeDtypeStruct((count, width), BF16),
            jax.ShapeDtypeStruct((count, inner // 2), F32),
            jax.ShapeDtypeStruct((8, 128), F32),
        ],
        compiler_params=pltpu.CompilerParams(vmem_limit_bytes=VMEM),
        cost_estimate=pl.CostEstimate(
            flops=2 * count * width * inner, bytes_accessed=2 * w_out.size, transcendentals=count
        ),
        name="list_grad",
    )(where, places, bounds, unit, inverse, w_out, final_gain[None], w_score[None], *scores,
      *weights)


def grad_kernel(where_ref, own_ref, sib_ref, d_own_ref, d_sib_ref, a_ref, b_ref):
    down = ((0,), (0,))
    out = mm(own_ref[...], d_own_ref[...], down) + mm(sib_ref[...], d_sib_ref[...], down)
    out = out.astype(BF16)
    a_ref[...] = out[:, : a_ref.shape[1]]
    b_ref[...] = out[:, a_ref.shape[1] :]


def grad_block(where, s, own, sib, d_own, d_sib, depth):
    rows = own.shape[0]
    width = d_own.shape[1]
    tile = min(depth, 256)
    tiles = depth // tile
    part = width // 2

    def lhs(i, w):
        return (0, (w[0] ^ s) * tiles + i)

    whole = lambda i, w: (0, 0)
    return pl.pallas_call(
        grad_kernel,
        grid_spec=pltpu.PrefetchScalarGridSpec(
            num_scalar_prefetch=1,
            grid=(tiles,),
            in_specs=[
                pl.BlockSpec((rows, tile), lhs),
                pl.BlockSpec((rows, tile), lhs),
                pl.BlockSpec((rows, width), whole),
                pl.BlockSpec((rows, width), whole),
            ],
            out_specs=[pl.BlockSpec((tile, part), lambda i, w: (i, 0))] * 2,
        ),
        out_shape=[jax.ShapeDtypeStruct((depth, part), BF16)] * 2,
        compiler_params=params(),
        cost_estimate=pl.CostEstimate(
            flops=4 * rows * depth * width,
            bytes_accessed=4 * rows * (depth + width) + 2 * depth * width,
            transcendentals=0,
        ),
        name="grad_rows",
    )(where, own, sib, d_own, d_sib)


def solution(mesh):
    n_list, n_fsdp = mesh.shape["list"], mesh.shape["fsdp"]
    bits = [1 << k for k in range(1, n_fsdp.bit_length() - 1)]
    pairs = n_list * n_fsdp // 2

    def across(value, distance):
        return lax.ppermute(value, "fsdp", [(i, i ^ distance) for i in range(n_fsdp)])

    def along(value, distance):
        return lax.ppermute(value, "list", [(i, i ^ distance) for i in range(n_list)])

    def partner(kind, pair):
        return (
            pair ^ 1,
            ((pair + 1) ^ 1) - 1,
            pair ^ 2,
            ((pair + 2) ^ 2) - 2,
        )[kind]

    def neighbour(value, kind):
        moves = []
        for pair in range(pairs):
            other = partner(kind, pair)
            if 0 <= other < pairs:
                moves += [(2 * pair + core, 2 * other + core) for core in (0, 1)]
        return lax.ppermute(value, ("list", "fsdp"), moves)

    def gathered(value, order):
        have = {0: value}
        for bit in order:
            have.update({s ^ (bit >> 1): across(part, bit) for s, part in list(have.items())})
        return have

    def scattered(parts, order):
        current = dict(parts)
        for bit in order:
            flag = bit >> 1
            come = {s ^ flag: across(current[s], bit) for s in sorted(current)[::-1] if s & flag}
            current = {
                s: (current[s].astype(F32) + come[s].astype(F32)).astype(BF16)
                for s in current
                if not s & flag
            }
        return current[0]

    def local(hidden, norm_gain, w_qkv, w_out, final_gain, w_score, prior, labels, lengths):
        passages, _, width = hidden.shape
        assert 4 * passages >= LONGEST - 1
        groups = KV_HEADS // 2
        width_q, width_k = groups * GROUP, groups * HEAD_DIM
        index = lax.axis_index("fsdp")
        core = index % 2
        chip = index // 2
        where = jnp.stack([chip, core]).astype(jnp.int32)
        first_core = core == 0

        def ordered(mine, other, axis):
            return jnp.where(
                first_core,
                jnp.concatenate([mine, other], axis),
                jnp.concatenate([other, mine], axis),
            )

        starts = (0, 2 * width_q, 2 * (width_q + width_k))
        sizes = (width_q, width_k, width_k)

        def half(h):
            return jnp.concatenate(
                [w_qkv[:, a + h * n : a + (h + 1) * n] for a, n in zip(starts, sizes)], 1
            )

        halves = half(0), half(1)
        keep = jnp.where(first_core, *halves)
        give = jnp.where(first_core, halves[1], halves[0])
        pair_rows = ordered(keep, across(give, 1), 0)
        middle = pair_rows.shape[1] // 2
        part_a = gathered(pair_rows[:, :middle], bits)
        part_b = gathered(pair_rows[:, middle:], bits[::-1])
        weights = [(part_a[s], part_b[s]) for s in range(n_fsdp // 2)]
        full_out = lax.all_gather(w_out, "fsdp", axis=0, tiled=True)

        normal, sums = norm(hidden, norm_gain)
        normal_sib, sums_sib = across(normal, 1), across(sums, 1)
        sums = jnp.concatenate([sums, sums_sib], 0)
        lanes = -(-lengths.shape[0] // 128) * 128
        label_weight = jnp.exp(labels.astype(F32))
        small = jnp.broadcast_to(
            jnp.concatenate([prior, label_weight])[:, None], (2 * passages, 128)
        )
        small_sib = across(small, 1)
        prior_pair = jnp.concatenate([small[:passages], small_sib[:passages]], 0)
        heavy = jnp.concatenate([small[passages:], small_sib[passages:]], 0)
        heavies = [heavy] + [neighbour(heavy, kind) for kind in range(4)]
        pair = lax.axis_index("list") * (n_fsdp // 2) + chip
        places = jnp.stack([pair] + [partner(kind, pair) for kind in range(4)]).astype(jnp.int32)
        ends = jnp.cumsum(lengths)
        bounds = jnp.pad(jnp.stack([ends - lengths, ends]), ((0, 0), (0, lanes - lengths.shape[0])))

        proj_sib, probs_sib, attn_sib = forward(where, normal_sib, weights, groups)
        attn_sib_other = across(attn_sib, 1)
        proj_own, probs_own, attn_own = forward(where, normal, weights, groups)
        attn_own_other = across(attn_own, 1)
        mine = jnp.concatenate([attn_own, attn_sib], 0)
        other = jnp.concatenate([attn_sib_other, attn_own_other], 0)
        unit, inverse, score, attn = score_pass(
            where, mine, other, sums, full_out, final_gain, w_score, prior_pair
        )
        scores = [score] + [neighbour(score, kind) for kind in range(4)]
        d_rows, d_attended, loss_part = list_pass(
            where, places, bounds, unit, inverse, full_out, final_gain, w_score, scores, heavies,
            passages,
        )

        d_own = backward(probs_own, proj_own, d_attended[:passages], groups)
        d_sib = backward(probs_sib, proj_sib, d_attended[passages:], groups)
        depth = pair_rows.shape[0]
        blocks = {
            s: grad_block(where, s, normal, normal_sib, d_own, d_sib, depth)
            for s in sorted(range(n_fsdp // 2), key=lambda s: -bin(s).count("1"))
        }
        sum_a = scattered({s: blocks[s][0] for s in blocks}, bits)
        sum_b = scattered({s: blocks[s][1] for s in blocks}, bits[::-1])
        chip_sum = jnp.concatenate([sum_a, sum_b], 1)
        upper, lower = chip_sum[: depth // 2], chip_sum[depth // 2 :]
        keep = jnp.where(first_core, upper, lower)
        come = across(jnp.where(first_core, lower, upper), 1)
        columns = []
        at = 0
        for n in sizes:
            columns.append(ordered(keep[:, at : at + n], come[:, at : at + n], 1))
            at += n
        rows_sum = jnp.concatenate(columns, 1)
        place = lax.axis_index("list")

        def list_scatter(value):
            n = value.shape[1] // n_list
            block = lambda which: lax.dynamic_slice_in_dim(value, which * n, n, 1)
            total = block(place).astype(F32)
            for distance in range(1, n_list):
                total = total + along(block(place ^ distance).astype(BF16), distance).astype(F32)
            return total

        grad_qkv = list_scatter(rows_sum)

        payload = jnp.concatenate([attn[:passages], d_rows[:passages]], 1)
        plane = lax.all_gather(payload, "fsdp", axis=0, tiled=True)
        inner = attn.shape[1]
        own_rows = inner // n_fsdp
        left = lax.dynamic_slice_in_dim(plane, index * own_rows, own_rows, 1)
        grad_out = list_scatter(
            lax.dot_general(
                left, plane[:, inner:], (((0,), (0,)), ((), ())), preferred_element_type=F32
            )
        )

        loss = loss_part
        for distance in [1] + bits:
            loss = loss + across(loss, distance)
        distance = 1
        while distance < n_list:
            loss = loss + along(loss, distance)
            distance *= 2
        return (loss[0, 0], grad_qkv, grad_out)

    placed = (
        P(("list", "fsdp"), None, None),
        P(),
        P("fsdp", None),
        P("fsdp", None),
        P(),
        P(),
        P(("list", "fsdp")),
        P(("list", "fsdp")),
        P(),
    )
    return jax.shard_map(
        local,
        mesh=mesh,
        in_specs=placed,
        out_specs=(P(), P("fsdp", "list"), P("fsdp", "list")),
        check_vma=False,
    )
```

```python
import functools

import jax
import jax.numpy as jnp
from jax import lax
from jax.experimental import pallas as pl
from jax.experimental.pallas import tpu as pltpu
from jax.sharding import PartitionSpec as P

HEADS = 16
KV_HEADS = 4
HEAD_DIM = 64
PASSAGE_LEN = 64
LONGEST = 48
RATIO = HEADS // KV_HEADS
GROUP = RATIO * HEAD_DIM

epsilon = 1e-05
loss_scale = 64.0
scale = HEAD_DIM ** (-0.5)
VMEM = 48 * 1024 * 1024
BF16 = jnp.bfloat16
F32 = jnp.float32


def params(grid=1):
    return pltpu.CompilerParams(
        vmem_limit_bytes=VMEM, dimension_semantics=("arbitrary",) * grid
    )


def mm(a, b, dims=((1,), (0,))):
    return lax.dot_general(a, b, (dims, ((), ())), preferred_element_type=F32)


def norm_kernel(hidden_ref, gain_ref, normal_ref, sum_ref):
    values = hidden_ref[...].astype(F32)
    mean_square = jnp.mean(values * values, -1, keepdims=True)
    out = values * lax.rsqrt(mean_square + epsilon) * gain_ref[...][None]
    normal_ref[...] = out.astype(BF16)
    sum_ref[0] = jnp.sum(values, 1)


def norm(hidden, gain):
    passages, length, width = hidden.shape
    step = 4 if passages % 4 == 0 else 1
    steps = passages // step
    normal, sums = pl.pallas_call(
        norm_kernel,
        grid=(steps,),
        in_specs=[
            pl.BlockSpec((step, length, width), lambda i: (i, 0, 0)),
            pl.BlockSpec((1, width), lambda i: (0, 0)),
        ],
        out_specs=[
            pl.BlockSpec((step, length, width), lambda i: (i, 0, 0)),
            pl.BlockSpec((1, step, width), lambda i: (i, 0, 0)),
        ],
        out_shape=[
            jax.ShapeDtypeStruct((passages, length, width), BF16),
            jax.ShapeDtypeStruct((steps, step, width), F32),
        ],
        compiler_params=params(),
        cost_estimate=pl.CostEstimate(
            flops=6 * hidden.size, bytes_accessed=4 * hidden.size, transcendentals=0
        ),
        name="norm_rows",
    )(hidden, gain[None])
    return normal.reshape(passages * length, width), sums.reshape(passages, width)


WIDE = 2 * HEAD_DIM
BATCH = 8


def low_lanes(rows):
    return lax.broadcasted_iota(jnp.int32, (rows, WIDE), 1) < HEAD_DIM


def ones_block(repeat):
    row = lax.broadcasted_iota(jnp.int32, (repeat * WIDE, WIDE), 0) // HEAD_DIM % 2
    col = lax.broadcasted_iota(jnp.int32, (repeat * WIDE, WIDE), 1) // HEAD_DIM
    return jnp.where(row == col, 1.0, 0.0).astype(BF16)


def diagonals(pair, factor):
    low = low_lanes(HEAD_DIM)
    wide = pair.astype(F32) * factor
    turned = pltpu.roll(wide, HEAD_DIM, 1)
    out = []
    for first, second in ((wide, turned), (turned, wide)):
        block = [jnp.where(low, first, 0.0), jnp.where(low, 0.0, second)]
        out.append(jnp.concatenate(block, 0).astype(BF16))
    return out


def segment_max(scores):
    low = low_lanes(scores.shape[0])
    first = jnp.max(jnp.where(low, scores, -jnp.inf), 1, keepdims=True)
    second = jnp.max(jnp.where(low, -jnp.inf, scores), 1, keepdims=True)
    return jnp.where(low, first, second)


def stacked(ref, rows, g):
    at = g * GROUP
    return jnp.concatenate([ref[rows, at : at + WIDE], ref[rows, at + WIDE : at + GROUP]], 0)


def project(refs, pieces, whole):
    blocks, refs = refs[:pieces], refs[pieces:]
    weights, refs = refs[: 2 * pieces], refs[2 * pieces :]
    join(weights, whole)
    rows = blocks[0][...]
    if pieces > 1:
        rows = jnp.concatenate([rows] + [block[...] for block in blocks[1:]], 1)
    return mm(rows, whole[...]), refs


def partial_kernel(pieces, before, where_ref, *refs):
    refs, whole = refs[:-1], refs[-1]
    product, refs = project(refs, pieces, whole)
    refs[-1][...] = product + refs[0][...] if before else product


def first_kernel(where_ref, rows_ref, a_ref, b_ref, out_ref, turned_ref):
    depth, part = a_ref.shape
    start = pl.multiple_of(where_ref[0] * depth, depth)
    block = rows_ref[:, pl.ds(start, depth)]
    out_ref[:, :part] = mm(block, a_ref[...])
    out_ref[:, part:] = mm(block, b_ref[...])
    turned_ref[...] = rows_ref[...].T


def forward_kernel(pieces, groups, where_ref, *refs):
    refs, whole = refs[:-1], refs[-1]
    projected, refs = project(refs, pieces, whole)
    before_ref, projected_ref, probs_ref, sum_ref = refs
    projected = projected + before_ref[...]
    projected_ref[...] = projected.astype(BF16)
    ones = ones_block(1)
    width_q = groups * GROUP
    width_k = groups * HEAD_DIM
    count = projected_ref.shape[0] // PASSAGE_LEN
    spans = [slice(i * PASSAGE_LEN, (i + 1) * PASSAGE_LEN) for i in range(count)]
    keys = [diagonals(projected_ref[r, width_q : width_q + width_k], scale) for r in spans]
    values = [diagonals(projected_ref[r, width_q + width_k :], 1.0) for r in spans]
    for g in range(groups):
        scores = jnp.concatenate(
            [mm(stacked(projected_ref, r, g), keys[i][g], ((1,), (1,))) for i, r in enumerate(spans)],
            0,
        )
        expo = jnp.exp(scores - segment_max(scores))
        total = mm(expo.astype(BF16), ones)
        probs = (expo / total).astype(BF16)
        probs_ref[0, g] = probs
        for i in range(count):
            attended = mm(probs[i * WIDE : (i + 1) * WIDE], values[i][g])
            attended = attended.astype(BF16).astype(F32)
            for j in range(2):
                at = g * GROUP + j * WIDE
                sum_ref[0, i : i + 1, at : at + WIDE] = jnp.sum(
                    attended[j * HEAD_DIM : (j + 1) * HEAD_DIM], 0, keepdims=True
                )


def join(weights, whole):
    @pl.when(pl.program_id(0) == 0)
    def _():
        depth, part = weights[0].shape
        for k in range(len(weights) // 2):
            rows = slice(k * depth, (k + 1) * depth)
            whole[rows, :part] = weights[2 * k][...]
            whole[rows, part:] = weights[2 * k + 1][...]


def row_step(total, batch):
    batch = batch if total % (batch * PASSAGE_LEN) == 0 else 1
    return batch, batch * PASSAGE_LEN


def block_of(step, depth, s):
    return pl.BlockSpec((step, depth), lambda i, w: (i, w[0] ^ s))


def first_project(where, rows, weights):
    total, width = rows.shape
    depth, part = weights[0].shape
    _, step = row_step(total, 4)
    whole = lambda i, w: (0, 0)
    return pl.pallas_call(
        first_kernel,
        grid_spec=pltpu.PrefetchScalarGridSpec(
            num_scalar_prefetch=1,
            grid=(total // step,),
            in_specs=[
                pl.BlockSpec((step, width), lambda i, w: (i, 0)),
                pl.BlockSpec((depth, part), whole),
                pl.BlockSpec((depth, part), whole),
            ],
            out_specs=[
                pl.BlockSpec((step, 2 * part), lambda i, w: (i, 0)),
                pl.BlockSpec((width, step), lambda i, w: (0, i)),
            ],
        ),
        out_shape=[
            jax.ShapeDtypeStruct((total, 2 * part), F32),
            jax.ShapeDtypeStruct((width, total), BF16),
        ],
        compiler_params=params(),
        cost_estimate=pl.CostEstimate(
            flops=4 * total * depth * part, bytes_accessed=4 * rows.size + 8 * total * part,
            transcendentals=0,
        ),
        name="project_first",
    )(where, rows, *weights)


def partial_project(where, rows, weights, before):
    total, width = rows.shape
    depth, part = next(iter(weights.values()))[0].shape
    _, step = row_step(total, BATCH)
    pieces = len(weights)
    flat = [x for s in weights for x in weights[s]]
    out = pl.BlockSpec((step, 2 * part), lambda i, w: (i, 0))
    return pl.pallas_call(
        functools.partial(partial_kernel, pieces, True),
        grid_spec=pltpu.PrefetchScalarGridSpec(
            num_scalar_prefetch=1,
            grid=(total // step,),
            in_specs=[block_of(step, depth, s) for s in weights]
            + [pl.BlockSpec(x.shape, lambda i, w: (0, 0)) for x in flat]
            + [out],
            out_specs=out,
            scratch_shapes=[pltpu.VMEM((pieces * depth, 2 * part), BF16)],
        ),
        out_shape=jax.ShapeDtypeStruct((total, 2 * part), F32),
        compiler_params=params(),
        cost_estimate=pl.CostEstimate(
            flops=4 * total * depth * part * pieces,
            bytes_accessed=2 * total * depth * pieces + 16 * total * part,
            transcendentals=0,
        ),
        name="project_more",
    )(where, *([rows] * pieces), *flat, before)


def forward(where, rows, weights, groups, before):
    total, width = rows.shape
    pieces = len(weights)
    flat = [x for s in weights for x in weights[s]]
    depth, part = flat[0].shape
    out_width = 2 * part
    batch, step = row_step(total, BATCH)
    steps = total // step
    heads = groups * GROUP
    return pl.pallas_call(
        functools.partial(forward_kernel, pieces, groups),
        grid_spec=pltpu.PrefetchScalarGridSpec(
            num_scalar_prefetch=1,
            grid=(steps,),
            in_specs=[block_of(step, depth, s) for s in weights]
            + [pl.BlockSpec(x.shape, lambda i, w: (0, 0)) for x in flat]
            + [pl.BlockSpec((step, out_width), lambda i, w: (i, 0))],
            out_specs=[
                pl.BlockSpec((step, out_width), lambda i, w: (i, 0)),
                pl.BlockSpec((1, groups, batch * WIDE, WIDE), lambda i, w: (i, 0, 0, 0)),
                pl.BlockSpec((1, batch, heads), lambda i, w: (i, 0, 0)),
            ],
            scratch_shapes=[pltpu.VMEM((pieces * depth, out_width), BF16)],
        ),
        out_shape=[
            jax.ShapeDtypeStruct((total, out_width), BF16),
            jax.ShapeDtypeStruct((steps, groups, batch * WIDE, WIDE), BF16),
            jax.ShapeDtypeStruct((steps, batch, heads), F32),
        ],
        compiler_params=params(),
        cost_estimate=pl.CostEstimate(
            flops=2 * total * depth * pieces * out_width + 8 * total * heads * GROUP,
            bytes_accessed=2 * total * (depth * pieces + 3 * out_width + heads),
            transcendentals=total * heads,
        ),
        name="project_attend",
    )(where, *([rows] * pieces), *flat, before)


def backward_kernel(groups, probs_ref, projected_ref, d_ref, out_ref):
    low = low_lanes(HEAD_DIM)
    ones = ones_block(2)
    width_q = groups * GROUP
    width_k = groups * HEAD_DIM
    count = projected_ref.shape[0] // PASSAGE_LEN
    spans = [slice(i * PASSAGE_LEN, (i + 1) * PASSAGE_LEN) for i in range(count)]
    keys = [diagonals(projected_ref[r, width_q : width_q + width_k], scale) for r in spans]
    values = [diagonals(projected_ref[r, width_q + width_k :], 1.0) for r in spans]
    down = ((0,), (0,))
    d_keys = [[] for _ in spans]
    d_values = [[] for _ in spans]

    def fold(product):
        kept = jnp.where(low, product[:HEAD_DIM], product[HEAD_DIM:])
        return kept + pltpu.roll(kept, HEAD_DIM, 1)

    for g in range(groups):
        probs = probs_ref[0, g]
        d_rows = []
        for i in range(count):
            row = [
                d_ref[0, i : i + 1, g * GROUP + j * WIDE : g * GROUP + (j + 1) * WIDE]
                for j in range(2)
            ]
            d_rows.append(
                jnp.concatenate(
                    [jnp.broadcast_to(x, (HEAD_DIM, WIDE)) for x in row], 0
                ).astype(BF16)
            )
        d_probs = jnp.concatenate(
            [mm(d_rows[i], values[i][g], ((1,), (1,))) for i in range(count)], 0
        )
        probs_f = probs.astype(F32)
        product = probs_f * d_probs
        upper = product.astype(BF16)
        lower = (product - upper.astype(F32)).astype(BF16)
        inner = mm(jnp.concatenate([upper, lower], 1), ones)
        d_scores = (probs_f * (d_probs - inner)).astype(BF16)
        for i, r in enumerate(spans):
            block = slice(i * WIDE, (i + 1) * WIDE)
            d_query = mm(d_scores[block], keys[i][g]).astype(BF16)
            at = g * GROUP
            out_ref[r, at : at + WIDE] = d_query[:HEAD_DIM]
            out_ref[r, at + WIDE : at + GROUP] = d_query[HEAD_DIM:]
            d_keys[i].append(fold(mm(d_scores[block], stacked(projected_ref, r, g), down)) * scale)
            d_values[i].append(fold(mm(probs[block], d_rows[i], down)))
    for i, r in enumerate(spans):
        out_ref[r, width_q : width_q + width_k] = jnp.where(low, *d_keys[i]).astype(BF16)
        out_ref[r, width_q + width_k :] = jnp.where(low, *d_values[i]).astype(BF16)


def backward(probs, projected, d_attended, groups):
    total, out_width = projected.shape
    steps = probs.shape[0]
    step = total // steps
    batch = step // PASSAGE_LEN
    heads = groups * GROUP
    return pl.pallas_call(
        functools.partial(backward_kernel, groups),
        grid=(steps,),
        in_specs=[
            pl.BlockSpec((1,) + probs.shape[1:], lambda i: (i, 0, 0, 0)),
            pl.BlockSpec((step, out_width), lambda i: (i, 0)),
            pl.BlockSpec((1, batch, heads), lambda i: (i, 0, 0)),
        ],
        out_specs=pl.BlockSpec((step, out_width), lambda i: (i, 0)),
        out_shape=jax.ShapeDtypeStruct((total, out_width), BF16),
        compiler_params=params(),
        cost_estimate=pl.CostEstimate(
            flops=16 * total * heads * GROUP,
            bytes_accessed=2 * total * (heads + 2 * out_width),
            transcendentals=0,
        ),
        name="attend_back",
    )(probs, projected, d_attended.reshape(steps, batch, heads))


def score_kernel(chips, where_ref, mine_ref, other_ref, sum_ref, final_ref, ws_ref, prior_ref,
                 *refs):
    pieces, refs = refs[: 4 * chips], refs[4 * chips :]
    unit_ref, inverse_ref, score_ref, attn_ref, product_ref = refs
    chip, core = where_ref[0], where_ref[1]
    mine, other = mine_ref[...], other_ref[...]
    attn = jnp.concatenate(
        [jnp.where(core == 0, mine, other), jnp.where(core == 0, other, mine)], 1
    )
    count = attn.shape[0]
    upper = attn.astype(BF16)
    attn_ref[...] = upper
    both = jnp.concatenate([upper.astype(F32), attn - upper.astype(F32)], 0)
    product_ref[...] = both
    depth, part = pieces[0].shape
    out = [None] * 4
    for s in range(chips):
        start = pl.multiple_of((chip ^ s) * depth, depth)
        block = product_ref[:, pl.ds(start, depth)].astype(BF16)
        for k in range(4):
            x = mm(block, pieces[4 * s + k][...])
            out[k] = x if out[k] is None else out[k] + x
    out = [x[:count] + x[count:] for x in out]
    own, far = jnp.concatenate(out[:2], 1), jnp.concatenate(out[2:], 1)
    product = jnp.concatenate(
        [jnp.where(core == 0, own, far), jnp.where(core == 0, far, own)], 1
    )
    pooled = (sum_ref[...] + product) * (1.0 / PASSAGE_LEN)
    inverse = lax.rsqrt(jnp.mean(pooled * pooled, -1, keepdims=True) + epsilon)
    unit = pooled * inverse
    score = jnp.sum(unit * (final_ref[...] * ws_ref[...]), -1, keepdims=True)
    unit_ref[...] = unit
    inverse_ref[...] = jnp.broadcast_to(inverse, inverse_ref.shape)
    score_ref[...] = score + prior_ref[...]


def score_pass(where, mine, other, sums, final_gain, w_score, prior, pieces):
    count, width = sums.shape
    lanes = prior.shape[1]
    inner = 2 * mine.shape[1]
    vmem = pl.BlockSpec(memory_space=pltpu.VMEM)
    return pl.pallas_call(
        functools.partial(score_kernel, len(pieces) // 4),
        in_specs=[pl.BlockSpec(memory_space=pltpu.SMEM)] + [vmem] * (6 + len(pieces)),
        out_specs=[vmem] * 4,
        out_shape=[
            jax.ShapeDtypeStruct((count, width), F32),
            jax.ShapeDtypeStruct((count, lanes), F32),
            jax.ShapeDtypeStruct((count, lanes), F32),
            jax.ShapeDtypeStruct((count, inner), BF16),
        ],
        scratch_shapes=[pltpu.VMEM((2 * count, inner), F32)],
        compiler_params=pltpu.CompilerParams(vmem_limit_bytes=VMEM),
        cost_estimate=pl.CostEstimate(
            flops=4 * count * width * inner, bytes_accessed=2 * width * inner, transcendentals=0
        ),
        name="pool_score",
    )(where, mine, other, sums, final_gain[None], w_score[None], prior, *pieces)


def list_kernel(blocks, chips, passages, where_ref, place_ref, bounds_ref, unit_ref, inverse_ref,
                final_ref, ws_ref, *refs):
    scores = [ref[...] for ref in refs[:blocks]]
    weights = [ref[...] for ref in refs[blocks : 2 * blocks]]
    pieces, refs = refs[2 * blocks : 2 * blocks + 4 * chips], refs[2 * blocks + 4 * chips :]
    d_rows_ref, d_att_ref, loss_ref, back_ref = refs
    chip, core = where_ref[0], where_ref[1]
    starts, ends = bounds_ref[0:1], bounds_ref[1:2]
    pair = 2 * passages
    lanes = starts.shape[1]
    row = lax.broadcasted_iota(jnp.int32, (pair, lanes), 0)
    offset = jnp.where(
        row < passages, core * passages + row, (1 - core) * passages + row - passages
    )
    members = []
    for j in range(blocks):
        place = place_ref[j] * pair + offset
        members.append((place >= starts) & (place < ends))
    column = [jnp.broadcast_to(score[:, :1], (pair, lanes)) for score in scores]
    heavy = [jnp.broadcast_to(weight[:, :1], (pair, lanes)) for weight in weights]
    peak = functools.reduce(
        jnp.maximum,
        [jnp.max(jnp.where(m, s, -1e30), 0, keepdims=True) for m, s in zip(members, column)],
    )
    total = sum(
        jnp.sum(jnp.where(m, jnp.exp(jnp.where(m, s - peak, 0.0)), 0.0), 0, keepdims=True)
        for m, s in zip(members, column)
    )
    label_total = sum(
        jnp.sum(jnp.where(m, w, 0.0), 0, keepdims=True) for m, w in zip(members, heavy)
    )
    log_norm = peak + jnp.log(total)
    own = members[0]
    log_prob = column[0][:, :1] - jnp.sum(jnp.where(own, log_norm, 0.0), 1, keepdims=True)
    target = heavy[0][:, :1] / jnp.sum(jnp.where(own, label_total, 0.0), 1, keepdims=True)
    loss = -loss_scale * jnp.sum((target * log_prob)[:passages], 0, keepdims=True)
    loss_ref[...] = jnp.broadcast_to(loss, loss_ref.shape)
    d_score = loss_scale * (jnp.exp(log_prob) - target)
    unit = unit_ref[...]
    d_unit = d_score * (ws_ref[...] * final_ref[...])
    mean = jnp.mean(d_unit * unit, -1, keepdims=True)
    d_pooled = inverse_ref[:, :1] * (d_unit - unit * mean)
    d_rows = (d_pooled * (1.0 / PASSAGE_LEN)).astype(BF16)
    d_rows_ref[...] = d_rows
    depth, part = pieces[0].shape
    half = d_rows.shape[1] // 2
    own = jnp.where(core == 0, d_pooled[:, :half], d_pooled[:, half:])
    far = jnp.where(core == 0, d_pooled[:, half:], d_pooled[:, :half])
    cut = [own[:, :part], own[:, part:], far[:, :part], far[:, part:]]
    cut = [(x * (1.0 / PASSAGE_LEN)).astype(BF16) for x in cut]
    for s in range(chips):
        back = sum(mm(cut[k], pieces[4 * s + k][...], ((1,), (1,))) for k in range(4))
        start = pl.multiple_of((chip ^ s) * depth, depth)
        back_ref[:, pl.ds(start, depth)] = back.astype(BF16).astype(F32)
    back = back_ref[...]
    half = back.shape[1] // 2
    d_att_ref[...] = jnp.where(core == 0, back[:, :half], back[:, half:])


def list_pass(where, places, bounds, unit, inverse, final_gain, w_score, scores, weights, pieces,
              passages):
    count, width = unit.shape
    chips = len(pieces) // 4
    inner = chips * pieces[0].shape[0]
    vmem = pl.BlockSpec(memory_space=pltpu.VMEM)
    smem = pl.BlockSpec(memory_space=pltpu.SMEM)
    return pl.pallas_call(
        functools.partial(list_kernel, len(scores), chips, passages),
        in_specs=[smem] * 2 + [vmem] * (5 + 2 * len(scores) + len(pieces)),
        out_specs=[vmem] * 3,
        out_shape=[
            jax.ShapeDtypeStruct((count, width), BF16),
            jax.ShapeDtypeStruct((count, inner // 2), F32),
            jax.ShapeDtypeStruct((8, 128), F32),
        ],
        scratch_shapes=[pltpu.VMEM((count, inner), F32)],
        compiler_params=pltpu.CompilerParams(vmem_limit_bytes=VMEM),
        cost_estimate=pl.CostEstimate(
            flops=2 * count * width * inner, bytes_accessed=2 * width * inner, transcendentals=count
        ),
        name="list_grad",
    )(where, places, bounds, unit, inverse, final_gain[None], w_score[None], *scores, *weights,
      *pieces)


def grad_kernel(where_ref, own_ref, sib_ref, d_own_ref, d_sib_ref, a_ref, b_ref):
    out = mm(own_ref[...], d_own_ref[...]) + mm(sib_ref[...], d_sib_ref[...])
    out = out.astype(BF16)
    a_ref[...] = out[:, : a_ref.shape[1]]
    b_ref[...] = out[:, a_ref.shape[1] :]


def grad_block(where, s, own, sib, d_own, d_sib, depth):
    rows = own.shape[1]
    width = d_own.shape[1]
    tile = min(depth, 256)
    tiles = depth // tile
    part = width // 2

    def lhs(i, w):
        return ((w[0] ^ s) * tiles + i, 0)

    whole = lambda i, w: (0, 0)
    return pl.pallas_call(
        grad_kernel,
        grid_spec=pltpu.PrefetchScalarGridSpec(
            num_scalar_prefetch=1,
            grid=(tiles,),
            in_specs=[
                pl.BlockSpec((tile, rows), lhs),
                pl.BlockSpec((tile, rows), lhs),
                pl.BlockSpec((rows, width), whole),
                pl.BlockSpec((rows, width), whole),
            ],
            out_specs=[pl.BlockSpec((tile, part), lambda i, w: (i, 0))] * 2,
        ),
        out_shape=[jax.ShapeDtypeStruct((depth, part), BF16)] * 2,
        compiler_params=params(),
        cost_estimate=pl.CostEstimate(
            flops=4 * rows * depth * width,
            bytes_accessed=4 * rows * (depth + width) + 2 * depth * width,
            transcendentals=0,
        ),
        name="grad_rows",
    )(where, own, sib, d_own, d_sib)


def solution(mesh):
    n_list, n_fsdp = mesh.shape["list"], mesh.shape["fsdp"]
    bits = [1 << k for k in range(1, n_fsdp.bit_length() - 1)]
    pairs = n_list * n_fsdp // 2

    def across(value, distance):
        return lax.ppermute(value, "fsdp", [(i, i ^ distance) for i in range(n_fsdp)])

    def along(value, distance):
        return lax.ppermute(value, "list", [(i, i ^ distance) for i in range(n_list)])

    def partner(kind, pair):
        return (
            pair ^ 1,
            ((pair + 1) ^ 1) - 1,
            pair ^ 2,
            ((pair + 2) ^ 2) - 2,
        )[kind]

    def neighbour(value, kind):
        moves = []
        for pair in range(pairs):
            other = partner(kind, pair)
            if 0 <= other < pairs:
                moves += [(2 * pair + core, 2 * other + core) for core in (0, 1)]
        return lax.ppermute(value, ("list", "fsdp"), moves)

    def gathered(value, order):
        have = {0: value}
        for bit in order:
            have.update({s ^ (bit >> 1): across(part, bit) for s, part in list(have.items())})
        return have

    def scattered(parts, order):
        current = dict(parts)
        for bit in order:
            flag = bit >> 1
            come = {s ^ flag: across(current[s], bit) for s in sorted(current)[::-1] if s & flag}
            current = {
                s: (current[s].astype(F32) + come[s].astype(F32)).astype(BF16)
                for s in current
                if not s & flag
            }
        return current[0]

    def local(hidden, norm_gain, w_qkv, w_out, final_gain, w_score, prior, labels, lengths):
        passages, _, width = hidden.shape
        assert 4 * passages >= LONGEST - 1
        groups = KV_HEADS // 2
        width_q, width_k = groups * GROUP, groups * HEAD_DIM
        index = lax.axis_index("fsdp")
        core = index % 2
        chip = index // 2
        where = jnp.stack([chip, core]).astype(jnp.int32)
        first_core = core == 0

        def ordered(mine, other, axis):
            return jnp.where(
                first_core,
                jnp.concatenate([mine, other], axis),
                jnp.concatenate([other, mine], axis),
            )

        starts = (0, 2 * width_q, 2 * (width_q + width_k))
        sizes = (width_q, width_k, width_k)

        def half(h):
            return jnp.concatenate(
                [w_qkv[:, a + h * n : a + (h + 1) * n] for a, n in zip(starts, sizes)], 1
            )

        halves = half(0), half(1)
        keep = jnp.where(first_core, *halves)
        give = jnp.where(first_core, halves[1], halves[0])
        come = across(give, 1)
        pair_rows = ordered(keep, come, 0)
        middle = pair_rows.shape[1] // 2
        part_a = gathered(pair_rows[:, :middle], bits)
        part_b = gathered(pair_rows[:, middle:], bits[::-1])
        chips = n_fsdp // 2
        last = max(bin(s).count("1") for s in range(chips))
        weights = [{}, {}, {}]
        for s in range(chips):
            ones = bin(s).count("1")
            weights[2 if ones == last else 1 if ones else 0][s] = (part_a[s], part_b[s])

        hidden, w_out, part_a[0] = lax.optimization_barrier((hidden, w_out, part_a[0]))
        cols = w_out.shape[1] // 2
        out_halves = w_out[:, :cols], w_out[:, cols:]
        out_keep = jnp.where(first_core, *out_halves)
        out_pair = ordered(out_keep, across(jnp.where(first_core, *out_halves[::-1]), 1), 0)
        out_a = gathered(out_pair[:, : cols // 2], bits)
        out_b = gathered(out_pair[:, cols // 2 :], bits[::-1])
        pieces = []
        for s in range(chips):
            pieces += [out_a[s], out_b[s], across(out_a[s], 1), across(out_b[s], 1)]

        normal, sums = norm(hidden, norm_gain)
        normal_sib, sums_sib = across(normal, 1), across(sums, 1)
        sums = jnp.concatenate([sums, sums_sib], 0)
        lanes = -(-lengths.shape[0] // 128) * 128
        label_weight = jnp.exp(labels.astype(F32))
        small = jnp.broadcast_to(
            jnp.concatenate([prior, label_weight])[:, None], (2 * passages, 128)
        )
        small_sib = across(small, 1)
        prior_pair = jnp.concatenate([small[:passages], small_sib[:passages]], 0)
        heavy = jnp.concatenate([small[passages:], small_sib[passages:]], 0)
        heavies = [heavy] + [neighbour(heavy, kind) for kind in range(4)]
        pair = lax.axis_index("list") * (n_fsdp // 2) + chip
        places = jnp.stack([pair] + [partner(kind, pair) for kind in range(4)]).astype(jnp.int32)
        ends = jnp.cumsum(lengths)
        bounds = jnp.pad(jnp.stack([ends - lengths, ends]), ((0, 0), (0, lanes - lengths.shape[0])))

        def begin(rows):
            before, turned = first_project(where, rows, weights[0][0])
            if weights[1]:
                before = partial_project(where, rows, weights[1], before)
            return before, turned

        before_own, turned_own = begin(normal)
        before_sib, turned_sib = begin(normal_sib)
        proj_sib, probs_sib, attn_sib = forward(where, normal_sib, weights[2], groups, before_sib)
        attn_sib = attn_sib.reshape(passages, -1)
        attn_sib_other = across(attn_sib, 1)
        proj_own, probs_own, attn_own = forward(where, normal, weights[2], groups, before_own)
        attn_own = attn_own.reshape(passages, -1)
        attn_own_other = across(attn_own, 1)
        mine = jnp.concatenate([attn_own, attn_sib], 0)
        other = jnp.concatenate([attn_sib_other, attn_own_other], 0)
        unit, inverse, score, attn = score_pass(
            where, mine, other, sums, final_gain, w_score, prior_pair, pieces
        )
        scores = [score] + [neighbour(score, kind) for kind in range(4)]
        d_rows, d_attended, loss_part = list_pass(
            where, places, bounds, unit, inverse, final_gain, w_score, scores, heavies, pieces,
            passages,
        )

        d_own = backward(probs_own, proj_own, d_attended[:passages], groups)
        d_sib = backward(probs_sib, proj_sib, d_attended[passages:], groups)
        depth = pair_rows.shape[0]
        blocks = {
            s: grad_block(where, s, turned_own, turned_sib, d_own, d_sib, depth)
            for s in sorted(range(n_fsdp // 2), key=lambda s: -bin(s).count("1"))
        }
        sum_a = scattered({s: blocks[s][0] for s in blocks}, bits)
        sum_b = scattered({s: blocks[s][1] for s in blocks}, bits[::-1])
        chip_sum = jnp.concatenate([sum_a, sum_b], 1)
        upper, lower = chip_sum[: depth // 2], chip_sum[depth // 2 :]
        keep = jnp.where(first_core, upper, lower)
        come = across(jnp.where(first_core, lower, upper), 1)
        columns = []
        at = 0
        for n in sizes:
            columns.append(ordered(keep[:, at : at + n], come[:, at : at + n], 1))
            at += n
        rows_sum = jnp.concatenate(columns, 1)
        place = lax.axis_index("list")

        def list_scatter(value):
            n = value.shape[1] // n_list
            block = lambda which: lax.dynamic_slice_in_dim(value, which * n, n, 1)
            total = block(place).astype(F32)
            for distance in range(1, n_list):
                total = total + along(block(place ^ distance).astype(BF16), distance).astype(F32)
            return total

        grad_qkv = list_scatter(rows_sum)

        inner = attn.shape[1]
        attn_halves = attn[:, : inner // 2], attn[:, inner // 2 :]
        row_halves = d_rows[:, :cols], d_rows[:, cols:]
        payload = jnp.concatenate(
            [jnp.where(first_core, *attn_halves), jnp.where(first_core, *row_halves)], 1
        )
        plane = gathered(payload, bits)
        plane = jnp.concatenate([plane[s] for s in range(chips)], 0)
        far = across(plane, 1)
        own_rows = inner // n_fsdp
        far = far.reshape(chips, 2, passages, -1)[:, ::-1].reshape(plane.shape)
        left = ordered(plane[:, : inner // 2], far[:, : inner // 2], 1)
        right = ordered(plane[:, inner // 2 :], far[:, inner // 2 :], 1)
        left = lax.dynamic_slice_in_dim(left, index * own_rows, own_rows, 1)
        grad_out = list_scatter(
            lax.dot_general(left, right, (((0,), (0,)), ((), ())), preferred_element_type=F32)
        )

        loss = loss_part
        for distance in [1] + bits:
            loss = loss + across(loss, distance)
        distance = 1
        while distance < n_list:
            loss = loss + along(loss, distance)
            distance *= 2
        return (loss[0, 0], grad_qkv, grad_out)

    placed = (
        P(("list", "fsdp"), None, None),
        P(),
        P("fsdp", None),
        P("fsdp", None),
        P(),
        P(),
        P(("list", "fsdp")),
        P(("list", "fsdp")),
        P(),
    )
    return jax.shard_map(
        local,
        mesh=mesh,
        in_specs=placed,
        out_specs=(P(), P("fsdp", "list"), P("fsdp", "list")),
        check_vma=False,
    )
```

```python
import functools

import jax
import jax.numpy as jnp
from jax import lax
from jax.experimental import pallas as pl
from jax.experimental.pallas import tpu as pltpu
from jax.sharding import PartitionSpec as P

HEADS = 16
KV_HEADS = 4
HEAD_DIM = 64
PASSAGE_LEN = 64
LONGEST = 48
RATIO = HEADS // KV_HEADS
GROUP = RATIO * HEAD_DIM

epsilon = 1e-05
loss_scale = 64.0
scale = HEAD_DIM ** (-0.5)
VMEM = 48 * 1024 * 1024
COST = pl.CostEstimate(flops=1024, bytes_accessed=1024, transcendentals=0)
BF16 = jnp.bfloat16
F32 = jnp.float32


def params(grid=1):
    return pltpu.CompilerParams(
        vmem_limit_bytes=VMEM, dimension_semantics=("arbitrary",) * grid
    )


def mm(a, b, dims=((1,), (0,))):
    return lax.dot_general(a, b, (dims, ((), ())), preferred_element_type=F32)


def norm_kernel(where_ref, hidden_ref, gain_ref, a_ref, b_ref, normal_ref, sum_ref, out_ref):
    values = hidden_ref[...].astype(F32)
    mean_square = jnp.mean(values * values, -1, keepdims=True)
    out = values * lax.rsqrt(mean_square + epsilon) * gain_ref[...][None]
    normal_ref[...] = out.reshape(normal_ref.shape).astype(BF16)
    sum_ref[0] = jnp.sum(values, 1)
    depth, part = a_ref.shape
    start = pl.multiple_of(where_ref[0] * depth, depth)
    block = normal_ref[:, pl.ds(start, depth)]
    out_ref[:, :part] = mm(block, a_ref[...])
    out_ref[:, part:] = mm(block, b_ref[...])


def norm(where, hidden, gain, weights):
    passages, length, width = hidden.shape
    depth, part = weights[0].shape
    step = 4 if passages % 4 == 0 else 1
    steps = passages // step
    whole = lambda i, w: (0, 0)
    normal, sums, product = pl.pallas_call(
        norm_kernel,
        grid_spec=pltpu.PrefetchScalarGridSpec(
            num_scalar_prefetch=1,
            grid=(steps,),
            in_specs=[
                pl.BlockSpec((step, length, width), lambda i, w: (i, 0, 0)),
                pl.BlockSpec((1, width), whole),
                pl.BlockSpec((depth, part), whole),
                pl.BlockSpec((depth, part), whole),
            ],
            out_specs=[
                pl.BlockSpec((step * length, width), lambda i, w: (i, 0)),
                pl.BlockSpec((1, step, width), lambda i, w: (i, 0, 0)),
                pl.BlockSpec((step * length, 2 * part), lambda i, w: (i, 0)),
            ],
        ),
        out_shape=[
            jax.ShapeDtypeStruct((passages * length, width), BF16),
            jax.ShapeDtypeStruct((steps, step, width), F32),
            jax.ShapeDtypeStruct((passages * length, 2 * part), F32),
        ],
        compiler_params=params(),
        cost_estimate=COST,
        name="norm_project",
    )(where, hidden, gain[None], *weights)
    return normal, sums.reshape(passages, width), product


WIDE = 2 * HEAD_DIM
BATCH = 8


def low_lanes(rows):
    return lax.broadcasted_iota(jnp.int32, (rows, WIDE), 1) < HEAD_DIM


def ones_block(repeat):
    row = lax.broadcasted_iota(jnp.int32, (repeat * WIDE, WIDE), 0) // HEAD_DIM % 2
    col = lax.broadcasted_iota(jnp.int32, (repeat * WIDE, WIDE), 1) // HEAD_DIM
    return jnp.where(row == col, 1.0, 0.0).astype(BF16)


def diagonals(pair, factor):
    low = low_lanes(HEAD_DIM)
    wide = pair.astype(F32) * factor
    turned = pltpu.roll(wide, HEAD_DIM, 1)
    out = []
    for first, second in ((wide, turned), (turned, wide)):
        block = [jnp.where(low, first, 0.0), jnp.where(low, 0.0, second)]
        out.append(jnp.concatenate(block, 0).astype(BF16))
    return out


def segment_max(scores):
    low = low_lanes(scores.shape[0])
    first = jnp.max(jnp.where(low, scores, -jnp.inf), 1, keepdims=True)
    second = jnp.max(jnp.where(low, -jnp.inf, scores), 1, keepdims=True)
    return jnp.where(low, first, second)


def stacked(ref, rows, g):
    at = g * GROUP
    return jnp.concatenate([ref[rows, at : at + WIDE], ref[rows, at + WIDE : at + GROUP]], 0)


def project(refs, pieces, whole):
    blocks, refs = refs[:pieces], refs[pieces:]
    weights, refs = refs[: 2 * pieces], refs[2 * pieces :]
    join(weights, whole)
    rows = blocks[0][...]
    if pieces > 1:
        rows = jnp.concatenate([rows] + [block[...] for block in blocks[1:]], 1)
    return mm(rows, whole[...]), refs


def partial_kernel(pieces, before, where_ref, *refs):
    refs, whole = refs[:-1], refs[-1]
    product, refs = project(refs, pieces, whole)
    refs[-1][...] = product + refs[0][...] if before else product


def forward_kernel(pieces, groups, where_ref, *refs):
    refs, whole = refs[:-1], refs[-1]
    projected, refs = project(refs, pieces, whole)
    before_ref, projected_ref, probs_ref, sum_ref = refs
    projected = projected + before_ref[...]
    projected_ref[...] = projected.astype(BF16)
    ones = ones_block(1)
    width_q = groups * GROUP
    width_k = groups * HEAD_DIM
    count = projected_ref.shape[0] // PASSAGE_LEN
    spans = [slice(i * PASSAGE_LEN, (i + 1) * PASSAGE_LEN) for i in range(count)]
    keys = [diagonals(projected_ref[r, width_q : width_q + width_k], scale) for r in spans]
    values = [diagonals(projected_ref[r, width_q + width_k :], 1.0) for r in spans]
    for g in range(groups):
        scores = jnp.concatenate(
            [mm(stacked(projected_ref, r, g), keys[i][g], ((1,), (1,))) for i, r in enumerate(spans)],
            0,
        )
        expo = jnp.exp(scores - segment_max(scores))
        total = mm(expo.astype(BF16), ones)
        probs = (expo / total).astype(BF16)
        probs_ref[0, g] = probs
        for i in range(count):
            attended = mm(probs[i * WIDE : (i + 1) * WIDE], values[i][g])
            attended = attended.astype(BF16).astype(F32)
            for j in range(2):
                at = g * GROUP + j * WIDE
                sum_ref[0, i : i + 1, at : at + WIDE] = jnp.sum(
                    attended[j * HEAD_DIM : (j + 1) * HEAD_DIM], 0, keepdims=True
                )


def join(weights, whole):
    @pl.when(pl.program_id(0) == 0)
    def _():
        depth, part = weights[0].shape
        for k in range(len(weights) // 2):
            rows = slice(k * depth, (k + 1) * depth)
            whole[rows, :part] = weights[2 * k][...]
            whole[rows, part:] = weights[2 * k + 1][...]


def row_step(total, batch):
    batch = batch if total % (batch * PASSAGE_LEN) == 0 else 1
    return batch, batch * PASSAGE_LEN


def block_of(step, depth, s):
    return pl.BlockSpec((step, depth), lambda i, w: (i, w[0] ^ s))


def partial_project(where, rows, weights, before):
    total, width = rows.shape
    depth, part = next(iter(weights.values()))[0].shape
    _, step = row_step(total, BATCH)
    pieces = len(weights)
    flat = [x for s in weights for x in weights[s]]
    out = pl.BlockSpec((step, 2 * part), lambda i, w: (i, 0))
    return pl.pallas_call(
        functools.partial(partial_kernel, pieces, True),
        grid_spec=pltpu.PrefetchScalarGridSpec(
            num_scalar_prefetch=1,
            grid=(total // step,),
            in_specs=[block_of(step, depth, s) for s in weights]
            + [pl.BlockSpec(x.shape, lambda i, w: (0, 0)) for x in flat]
            + [out],
            out_specs=out,
            scratch_shapes=[pltpu.VMEM((pieces * depth, 2 * part), BF16)],
        ),
        out_shape=jax.ShapeDtypeStruct((total, 2 * part), F32),
        compiler_params=params(),
        cost_estimate=COST,
        name="project_more",
    )(where, *([rows] * pieces), *flat, before)


def forward(where, rows, weights, groups, before):
    total, width = rows.shape
    pieces = len(weights)
    flat = [x for s in weights for x in weights[s]]
    depth, part = flat[0].shape
    out_width = 2 * part
    batch, step = row_step(total, BATCH)
    steps = total // step
    heads = groups * GROUP
    return pl.pallas_call(
        functools.partial(forward_kernel, pieces, groups),
        grid_spec=pltpu.PrefetchScalarGridSpec(
            num_scalar_prefetch=1,
            grid=(steps,),
            in_specs=[block_of(step, depth, s) for s in weights]
            + [pl.BlockSpec(x.shape, lambda i, w: (0, 0)) for x in flat]
            + [pl.BlockSpec((step, out_width), lambda i, w: (i, 0))],
            out_specs=[
                pl.BlockSpec((step, out_width), lambda i, w: (i, 0)),
                pl.BlockSpec((1, groups, batch * WIDE, WIDE), lambda i, w: (i, 0, 0, 0)),
                pl.BlockSpec((1, batch, heads), lambda i, w: (i, 0, 0)),
            ],
            scratch_shapes=[pltpu.VMEM((pieces * depth, out_width), BF16)],
        ),
        out_shape=[
            jax.ShapeDtypeStruct((total, out_width), BF16),
            jax.ShapeDtypeStruct((steps, groups, batch * WIDE, WIDE), BF16),
            jax.ShapeDtypeStruct((steps, batch, heads), F32),
        ],
        compiler_params=params(),
        cost_estimate=COST,
        name="project_attend",
    )(where, *([rows] * pieces), *flat, before)


def backward_kernel(groups, probs_ref, projected_ref, d_ref, out_ref):
    low = low_lanes(HEAD_DIM)
    ones = ones_block(2)
    width_q = groups * GROUP
    width_k = groups * HEAD_DIM
    count = projected_ref.shape[0] // PASSAGE_LEN
    spans = [slice(i * PASSAGE_LEN, (i + 1) * PASSAGE_LEN) for i in range(count)]
    keys = [diagonals(projected_ref[r, width_q : width_q + width_k], scale) for r in spans]
    values = [diagonals(projected_ref[r, width_q + width_k :], 1.0) for r in spans]
    down = ((0,), (0,))
    d_keys = [[] for _ in spans]
    d_values = [[] for _ in spans]

    def fold(product):
        kept = jnp.where(low, product[:HEAD_DIM], product[HEAD_DIM:])
        return kept + pltpu.roll(kept, HEAD_DIM, 1)

    for g in range(groups):
        probs = probs_ref[0, g]
        d_rows = []
        for i in range(count):
            row = [
                d_ref[0, i : i + 1, g * GROUP + j * WIDE : g * GROUP + (j + 1) * WIDE]
                for j in range(2)
            ]
            d_rows.append(
                jnp.concatenate(
                    [jnp.broadcast_to(x, (HEAD_DIM, WIDE)) for x in row], 0
                ).astype(BF16)
            )
        d_probs = jnp.concatenate(
            [mm(d_rows[i], values[i][g], ((1,), (1,))) for i in range(count)], 0
        )
        probs_f = probs.astype(F32)
        product = probs_f * d_probs
        upper = product.astype(BF16)
        lower = (product - upper.astype(F32)).astype(BF16)
        inner = mm(jnp.concatenate([upper, lower], 1), ones)
        d_scores = (probs_f * (d_probs - inner)).astype(BF16)
        for i, r in enumerate(spans):
            block = slice(i * WIDE, (i + 1) * WIDE)
            d_query = mm(d_scores[block], keys[i][g]).astype(BF16)
            at = g * GROUP
            out_ref[r, at : at + WIDE] = d_query[:HEAD_DIM]
            out_ref[r, at + WIDE : at + GROUP] = d_query[HEAD_DIM:]
            d_keys[i].append(fold(mm(d_scores[block], stacked(projected_ref, r, g), down)) * scale)
            d_values[i].append(fold(mm(probs[block], d_rows[i], down)))
    for i, r in enumerate(spans):
        out_ref[r, width_q : width_q + width_k] = jnp.where(low, *d_keys[i]).astype(BF16)
        out_ref[r, width_q + width_k :] = jnp.where(low, *d_values[i]).astype(BF16)


def backward(probs, projected, d_attended, groups):
    total, out_width = projected.shape
    steps = probs.shape[0]
    step = total // steps
    batch = step // PASSAGE_LEN
    heads = groups * GROUP
    return pl.pallas_call(
        functools.partial(backward_kernel, groups),
        grid=(steps,),
        in_specs=[
            pl.BlockSpec((1,) + probs.shape[1:], lambda i: (i, 0, 0, 0)),
            pl.BlockSpec((step, out_width), lambda i: (i, 0)),
            pl.BlockSpec((1, batch, heads), lambda i: (i, 0, 0)),
        ],
        out_specs=pl.BlockSpec((step, out_width), lambda i: (i, 0)),
        out_shape=jax.ShapeDtypeStruct((total, out_width), BF16),
        compiler_params=params(),
        cost_estimate=COST,
        name="attend_back",
    )(probs, projected, d_attended.reshape(steps, batch, heads))


def score_kernel(chips, where_ref, mine_ref, other_ref, sum_ref, final_ref, ws_ref, prior_ref,
                 *refs):
    pieces, refs = refs[: 4 * chips], refs[4 * chips :]
    unit_ref, inverse_ref, score_ref, attn_ref, product_ref = refs
    chip, core = where_ref[0], where_ref[1]
    mine, other = mine_ref[...], other_ref[...]
    attn = jnp.concatenate(
        [jnp.where(core == 0, mine, other), jnp.where(core == 0, other, mine)], 1
    )
    count = attn.shape[0]
    upper = attn.astype(BF16)
    attn_ref[...] = upper
    both = jnp.concatenate([upper.astype(F32), attn - upper.astype(F32)], 0)
    product_ref[...] = both
    depth, part = pieces[0].shape
    out = [None] * 4
    for s in range(chips):
        start = pl.multiple_of((chip ^ s) * depth, depth)
        block = product_ref[:, pl.ds(start, depth)].astype(BF16)
        for k in range(4):
            x = mm(block, pieces[4 * s + k][...])
            out[k] = x if out[k] is None else out[k] + x
    out = [x[:count] + x[count:] for x in out]
    own, far = jnp.concatenate(out[:2], 1), jnp.concatenate(out[2:], 1)
    product = jnp.concatenate(
        [jnp.where(core == 0, own, far), jnp.where(core == 0, far, own)], 1
    )
    pooled = (sum_ref[...] + product) * (1.0 / PASSAGE_LEN)
    inverse = lax.rsqrt(jnp.mean(pooled * pooled, -1, keepdims=True) + epsilon)
    unit = pooled * inverse
    score = jnp.sum(unit * (final_ref[...] * ws_ref[...]), -1, keepdims=True)
    unit_ref[...] = unit
    inverse_ref[...] = jnp.broadcast_to(inverse, inverse_ref.shape)
    score_ref[...] = score + prior_ref[...]


def score_pass(where, mine, other, sums, final_gain, w_score, prior, pieces):
    count, width = sums.shape
    lanes = prior.shape[1]
    inner = 2 * mine.shape[1]
    vmem = pl.BlockSpec(memory_space=pltpu.VMEM)
    return pl.pallas_call(
        functools.partial(score_kernel, len(pieces) // 4),
        in_specs=[pl.BlockSpec(memory_space=pltpu.SMEM)] + [vmem] * (6 + len(pieces)),
        out_specs=[vmem] * 4,
        out_shape=[
            jax.ShapeDtypeStruct((count, width), F32),
            jax.ShapeDtypeStruct((count, lanes), F32),
            jax.ShapeDtypeStruct((count, lanes), F32),
            jax.ShapeDtypeStruct((count, inner), BF16),
        ],
        scratch_shapes=[pltpu.VMEM((2 * count, inner), F32)],
        compiler_params=pltpu.CompilerParams(vmem_limit_bytes=VMEM),
        cost_estimate=COST,
        name="pool_score",
    )(where, mine, other, sums, final_gain[None], w_score[None], prior, *pieces)


def list_kernel(blocks, chips, passages, where_ref, place_ref, bounds_ref, unit_ref, inverse_ref,
                final_ref, ws_ref, *refs):
    scores = [ref[...] for ref in refs[:blocks]]
    weights = [ref[...] for ref in refs[blocks : 2 * blocks]]
    pieces, refs = refs[2 * blocks : 2 * blocks + 4 * chips], refs[2 * blocks + 4 * chips :]
    d_rows_ref, d_att_ref, loss_ref, back_ref = refs
    chip, core = where_ref[0], where_ref[1]
    starts, ends = bounds_ref[0:1], bounds_ref[1:2]
    pair = 2 * passages
    lanes = starts.shape[1]
    row = lax.broadcasted_iota(jnp.int32, (pair, lanes), 0)
    offset = jnp.where(
        row < passages, core * passages + row, (1 - core) * passages + row - passages
    )
    members = []
    for j in range(blocks):
        place = place_ref[j] * pair + offset
        members.append((place >= starts) & (place < ends))
    column = [jnp.broadcast_to(score[:, :1], (pair, lanes)) for score in scores]
    heavy = [jnp.broadcast_to(weight[:, :1], (pair, lanes)) for weight in weights]
    peak = functools.reduce(
        jnp.maximum,
        [jnp.max(jnp.where(m, s, -1e30), 0, keepdims=True) for m, s in zip(members, column)],
    )
    total = sum(
        jnp.sum(jnp.where(m, jnp.exp(jnp.where(m, s - peak, 0.0)), 0.0), 0, keepdims=True)
        for m, s in zip(members, column)
    )
    label_total = sum(
        jnp.sum(jnp.where(m, w, 0.0), 0, keepdims=True) for m, w in zip(members, heavy)
    )
    log_norm = peak + jnp.log(total)
    own = members[0]
    log_prob = column[0][:, :1] - jnp.sum(jnp.where(own, log_norm, 0.0), 1, keepdims=True)
    target = heavy[0][:, :1] / jnp.sum(jnp.where(own, label_total, 0.0), 1, keepdims=True)
    loss = -loss_scale * jnp.sum((target * log_prob)[:passages], 0, keepdims=True)
    loss_ref[...] = jnp.broadcast_to(loss, loss_ref.shape)
    d_score = loss_scale * (jnp.exp(log_prob) - target)
    unit = unit_ref[...]
    d_unit = d_score * (ws_ref[...] * final_ref[...])
    mean = jnp.mean(d_unit * unit, -1, keepdims=True)
    d_pooled = inverse_ref[:, :1] * (d_unit - unit * mean)
    d_rows = (d_pooled * (1.0 / PASSAGE_LEN)).astype(BF16)
    d_rows_ref[...] = d_rows
    depth, part = pieces[0].shape
    half = d_rows.shape[1] // 2
    own = jnp.where(core == 0, d_pooled[:, :half], d_pooled[:, half:])
    far = jnp.where(core == 0, d_pooled[:, half:], d_pooled[:, :half])
    cut = [own[:, :part], own[:, part:], far[:, :part], far[:, part:]]
    cut = [(x * (1.0 / PASSAGE_LEN)).astype(BF16) for x in cut]
    for s in range(chips):
        back = sum(mm(cut[k], pieces[4 * s + k][...], ((1,), (1,))) for k in range(4))
        start = pl.multiple_of((chip ^ s) * depth, depth)
        back_ref[:, pl.ds(start, depth)] = back.astype(BF16).astype(F32)
    back = back_ref[...]
    half = back.shape[1] // 2
    d_att_ref[...] = jnp.where(core == 0, back[:, :half], back[:, half:])


def list_pass(where, places, bounds, unit, inverse, final_gain, w_score, scores, weights, pieces,
              passages):
    count, width = unit.shape
    chips = len(pieces) // 4
    inner = chips * pieces[0].shape[0]
    vmem = pl.BlockSpec(memory_space=pltpu.VMEM)
    smem = pl.BlockSpec(memory_space=pltpu.SMEM)
    return pl.pallas_call(
        functools.partial(list_kernel, len(scores), chips, passages),
        in_specs=[smem] * 2 + [vmem] * (5 + 2 * len(scores) + len(pieces)),
        out_specs=[vmem] * 3,
        out_shape=[
            jax.ShapeDtypeStruct((count, width), BF16),
            jax.ShapeDtypeStruct((count, inner // 2), F32),
            jax.ShapeDtypeStruct((8, 128), F32),
        ],
        scratch_shapes=[pltpu.VMEM((count, inner), F32)],
        compiler_params=pltpu.CompilerParams(vmem_limit_bytes=VMEM),
        cost_estimate=COST,
        name="list_grad",
    )(where, places, bounds, unit, inverse, final_gain[None], w_score[None], *scores, *weights,
      *pieces)


def grad_kernel(where_ref, own_ref, sib_ref, d_own_ref, d_sib_ref, a_ref, b_ref):
    down = ((0,), (0,))
    out = mm(own_ref[...], d_own_ref[...], down) + mm(sib_ref[...], d_sib_ref[...], down)
    out = out.astype(BF16)
    a_ref[...] = out[:, : a_ref.shape[1]]
    b_ref[...] = out[:, a_ref.shape[1] :]


def grad_block(where, s, own, sib, d_own, d_sib, depth):
    rows = own.shape[0]
    width = d_own.shape[1]
    tile = min(depth, 256)
    tiles = depth // tile
    part = width // 2

    def lhs(i, w):
        return (0, (w[0] ^ s) * tiles + i)

    whole = lambda i, w: (0, 0)
    return pl.pallas_call(
        grad_kernel,
        grid_spec=pltpu.PrefetchScalarGridSpec(
            num_scalar_prefetch=1,
            grid=(tiles,),
            in_specs=[
                pl.BlockSpec((rows, tile), lhs),
                pl.BlockSpec((rows, tile), lhs),
                pl.BlockSpec((rows, width), whole),
                pl.BlockSpec((rows, width), whole),
            ],
            out_specs=[pl.BlockSpec((tile, part), lambda i, w: (i, 0))] * 2,
        ),
        out_shape=[jax.ShapeDtypeStruct((depth, part), BF16)] * 2,
        compiler_params=params(),
        cost_estimate=COST,
        name="grad_rows",
    )(where, own, sib, d_own, d_sib)


def solution(mesh):
    n_list, n_fsdp = mesh.shape["list"], mesh.shape["fsdp"]
    bits = [1 << k for k in range(1, n_fsdp.bit_length() - 1)]
    pairs = n_list * n_fsdp // 2

    def across(value, distance):
        return lax.ppermute(value, "fsdp", [(i, i ^ distance) for i in range(n_fsdp)])

    def along(value, distance):
        return lax.ppermute(value, "list", [(i, i ^ distance) for i in range(n_list)])

    def partner(kind, pair):
        return (
            pair ^ 1,
            ((pair + 1) ^ 1) - 1,
            pair ^ 2,
            ((pair + 2) ^ 2) - 2,
        )[kind]

    def neighbour(value, kind):
        moves = []
        for pair in range(pairs):
            other = partner(kind, pair)
            if 0 <= other < pairs:
                moves += [(2 * pair + core, 2 * other + core) for core in (0, 1)]
        return lax.ppermute(value, ("list", "fsdp"), moves)

    def gathered(value, order):
        have = {0: value}
        for bit in order:
            have.update({s ^ (bit >> 1): across(part, bit) for s, part in list(have.items())})
        return have

    def scattered(parts, order):
        current = dict(parts)
        for bit in order:
            flag = bit >> 1
            come = {s ^ flag: across(current[s], bit) for s in sorted(current)[::-1] if s & flag}
            current = {
                s: (current[s].astype(F32) + come[s].astype(F32)).astype(BF16)
                for s in current
                if not s & flag
            }
        return current[0]

    def local(hidden, norm_gain, w_qkv, w_out, final_gain, w_score, prior, labels, lengths):
        passages, _, width = hidden.shape
        assert 4 * passages >= LONGEST - 1
        groups = KV_HEADS // 2
        width_q, width_k = groups * GROUP, groups * HEAD_DIM
        index = lax.axis_index("fsdp")
        core = index % 2
        chip = index // 2
        where = jnp.stack([chip, core]).astype(jnp.int32)
        first_core = core == 0

        def ordered(mine, other, axis):
            return jnp.where(
                first_core,
                jnp.concatenate([mine, other], axis),
                jnp.concatenate([other, mine], axis),
            )

        starts = (0, 2 * width_q, 2 * (width_q + width_k))
        sizes = (width_q, width_k, width_k)

        def half(value, h):
            return jnp.concatenate(
                [value[:, a + h * n : a + (h + 1) * n] for a, n in zip(starts, sizes)], 1
            )

        come = across(w_qkv, 1)
        both = ordered(w_qkv, come, 0)
        pair_rows = jnp.where(first_core, half(both, 0), half(both, 1))
        middle = pair_rows.shape[1] // 2
        part_a = gathered(pair_rows[:, :middle], bits)
        part_b = gathered(pair_rows[:, middle:], bits[::-1])
        chips = n_fsdp // 2
        last = max(bin(s).count("1") for s in range(chips))
        weights = [{}, {}, {}]
        for s in range(chips):
            ones = bin(s).count("1")
            weights[2 if ones == last else 1 if ones else 0][s] = (part_a[s], part_b[s])

        hidden, w_out, come = lax.optimization_barrier((hidden, w_out, come))
        hidden_sib = across(hidden, 1)
        cols = w_out.shape[1] // 2
        both = ordered(w_out, across(w_out, 1), 0)
        out_pair = jnp.where(first_core, both[:, :cols], both[:, cols:])
        out_pair, weights[1] = lax.optimization_barrier((out_pair, weights[1]))
        out_a = gathered(out_pair[:, : cols // 2], bits)
        out_b = gathered(out_pair[:, cols // 2 :], bits[::-1])
        pieces = []
        for s in range(chips):
            pieces += [out_a[s], out_b[s], across(out_a[s], 1), across(out_b[s], 1)]

        normal, sums, before_own = norm(where, hidden, norm_gain, weights[0][0])
        normal_sib, sums_sib, before_sib = norm(where, hidden_sib, norm_gain, weights[0][0])
        sums = jnp.concatenate([sums, sums_sib], 0)
        lanes = -(-lengths.shape[0] // 128) * 128
        label_weight = jnp.exp(labels.astype(F32))
        small = jnp.broadcast_to(
            jnp.concatenate([prior, label_weight])[:, None], (2 * passages, 128)
        )
        small_sib = across(small, 1)
        prior_pair = jnp.concatenate([small[:passages], small_sib[:passages]], 0)
        heavy = jnp.concatenate([small[passages:], small_sib[passages:]], 0)
        heavies = [heavy] + [neighbour(heavy, kind) for kind in range(4)]
        pair = lax.axis_index("list") * (n_fsdp // 2) + chip
        places = jnp.stack([pair] + [partner(kind, pair) for kind in range(4)]).astype(jnp.int32)
        ends = jnp.cumsum(lengths)
        bounds = jnp.pad(jnp.stack([ends - lengths, ends]), ((0, 0), (0, lanes - lengths.shape[0])))

        if weights[1]:
            before_own = partial_project(where, normal, weights[1], before_own)
            before_sib = partial_project(where, normal_sib, weights[1], before_sib)
        weights[2], before_own, before_sib, heavies, prior_pair, bounds = lax.optimization_barrier(
            (weights[2], before_own, before_sib, heavies, prior_pair, bounds)
        )
        proj_sib, probs_sib, attn_sib = forward(where, normal_sib, weights[2], groups, before_sib)
        attn_sib = attn_sib.reshape(passages, -1)
        attn_sib_other = across(attn_sib, 1)
        proj_own, probs_own, attn_own = forward(where, normal, weights[2], groups, before_own)
        attn_own = attn_own.reshape(passages, -1)
        attn_own_other = across(attn_own, 1)
        mine = jnp.concatenate([attn_own, attn_sib], 0)
        other = jnp.concatenate([attn_sib_other, attn_own_other], 0)
        unit, inverse, score, attn = score_pass(
            where, mine, other, sums, final_gain, w_score, prior_pair, pieces
        )
        scores = [score] + [neighbour(score, kind) for kind in range(4)]
        d_rows, d_attended, loss_part = list_pass(
            where, places, bounds, unit, inverse, final_gain, w_score, scores, heavies, pieces,
            passages,
        )

        d_own = backward(probs_own, proj_own, d_attended[:passages], groups)
        d_sib = backward(probs_sib, proj_sib, d_attended[passages:], groups)
        depth = pair_rows.shape[0]
        blocks = {
            s: grad_block(where, s, normal, normal_sib, d_own, d_sib, depth)
            for s in sorted(range(n_fsdp // 2), key=lambda s: -bin(s).count("1"))
        }
        sum_a = scattered({s: blocks[s][0] for s in blocks}, bits)
        sum_b = scattered({s: blocks[s][1] for s in blocks}, bits[::-1])
        chip_sum = jnp.concatenate([sum_a, sum_b], 1)
        upper, lower = chip_sum[: depth // 2], chip_sum[depth // 2 :]
        keep = jnp.where(first_core, upper, lower)
        come = across(jnp.where(first_core, lower, upper), 1)
        columns = []
        at = 0
        for n in sizes:
            columns.append(ordered(keep[:, at : at + n], come[:, at : at + n], 1))
            at += n
        rows_sum = jnp.concatenate(columns, 1)
        place = lax.axis_index("list")

        def list_scatter(value):
            n = value.shape[1] // n_list
            block = lambda which: lax.dynamic_slice_in_dim(value, which * n, n, 1)
            total = block(place).astype(F32)
            for distance in range(1, n_list):
                total = total + along(block(place ^ distance).astype(BF16), distance).astype(F32)
            return total

        grad_qkv = list_scatter(rows_sum)

        inner = attn.shape[1]
        attn_halves = attn[:, : inner // 2], attn[:, inner // 2 :]
        row_halves = d_rows[:, :cols], d_rows[:, cols:]
        loss = loss_part[:1]
        parts = []
        for _ in range(3):
            upper = lax.reduce_precision(loss, 8, 7)
            parts.append(upper.astype(BF16))
            loss = loss - upper
        extra = jnp.broadcast_to(jnp.concatenate(parts, 1), (2 * passages, 3 * 128))
        payload = jnp.concatenate(
            [
                jnp.where(first_core, *attn_halves),
                jnp.where(first_core, *row_halves),
                extra,
            ],
            1,
        )
        plane = gathered(payload, bits)
        plane = jnp.concatenate([plane[s] for s in range(chips)], 0)
        far = across(plane, 1)
        own_rows = inner // n_fsdp
        far = far.reshape(chips, 2, passages, -1)[:, ::-1].reshape(plane.shape)
        left = ordered(plane[:, : inner // 2], far[:, : inner // 2], 1)
        span = slice(inner // 2, inner // 2 + cols)
        right = ordered(plane[:, span], far[:, span], 1)
        left = lax.dynamic_slice_in_dim(left, index * own_rows, own_rows, 1)
        grad_out = list_scatter(
            lax.dot_general(left, right, (((0,), (0,)), ((), ())), preferred_element_type=F32)
        )

        def loss_of(value):
            rows = value[:, inner // 2 + cols :].reshape(chips, 2 * passages, 3, 128)
            return sum(rows[:, 0, k, 0].astype(F32) for k in range(3))

        losses = loss_of(plane) + loss_of(far)
        while losses.shape[0] > 1:
            losses = losses[0::2] + losses[1::2]
        loss = jnp.broadcast_to(losses[:, None], (8, 128))
        distance = 1
        while distance < n_list:
            loss = loss + along(loss, distance)
            distance *= 2
        return (loss[0, 0], grad_qkv, grad_out)

    placed = (
        P(("list", "fsdp"), None, None),
        P(),
        P("fsdp", None),
        P("fsdp", None),
        P(),
        P(),
        P(("list", "fsdp")),
        P(("list", "fsdp")),
        P(),
    )
    return jax.shard_map(
        local,
        mesh=mesh,
        in_specs=placed,
        out_specs=(P(), P("fsdp", "list"), P("fsdp", "list")),
        check_vma=False,
    )
```

```python
import functools

import jax
import jax.numpy as jnp
from jax import lax
from jax.experimental import pallas as pl
from jax.experimental.pallas import tpu as pltpu
from jax.sharding import PartitionSpec as P

HEADS = 16
KV_HEADS = 4
HEAD_DIM = 64
PASSAGE_LEN = 64
LONGEST = 48
RATIO = HEADS // KV_HEADS
GROUP = RATIO * HEAD_DIM

epsilon = 1e-05
loss_scale = 64.0
scale = HEAD_DIM ** (-0.5)
VMEM = 20 * 1024 * 1024
SMALL = 20 * 1024 * 1024


def cost(micros):
    return pl.CostEstimate(flops=int(micros * 1e8), bytes_accessed=int(micros * 3.5e6), transcendentals=0)

BF16 = jnp.bfloat16
F32 = jnp.float32


def params(grid=1):
    return pltpu.CompilerParams(
        vmem_limit_bytes=VMEM, dimension_semantics=("arbitrary",) * grid
    )


def held(space, *values):
    return [pltpu.with_memory_space_constraint(x, space) for x in values]


def mm(a, b, dims=((1,), (0,))):
    return lax.dot_general(a, b, (dims, ((), ())), preferred_element_type=F32)


def norm_kernel(where_ref, hidden_ref, gain_ref, a_ref, b_ref, normal_ref, sum_ref, out_ref):
    values = hidden_ref[...].astype(F32)
    mean_square = jnp.mean(values * values, -1, keepdims=True)
    out = values * lax.rsqrt(mean_square + epsilon) * gain_ref[...][None]
    normal_ref[...] = out.reshape(normal_ref.shape).astype(BF16)
    sum_ref[0] = jnp.sum(values, 1)
    depth, part = a_ref.shape
    start = pl.multiple_of(where_ref[0] * depth, depth)
    block = normal_ref[:, pl.ds(start, depth)]
    out_ref[:, :part] = mm(block, a_ref[...])
    out_ref[:, part:] = mm(block, b_ref[...])


def norm(where, hidden, gain, weights):
    passages, length, width = hidden.shape
    depth, part = weights[0].shape
    step = 4 if passages % 4 == 0 else 1
    steps = passages // step
    whole = lambda i, w: (0, 0)
    normal, sums, product = pl.pallas_call(
        norm_kernel,
        grid_spec=pltpu.PrefetchScalarGridSpec(
            num_scalar_prefetch=1,
            grid=(steps,),
            in_specs=[
                pl.BlockSpec((step, length, width), lambda i, w: (i, 0, 0)),
                pl.BlockSpec((1, width), whole),
                pl.BlockSpec((depth, part), whole),
                pl.BlockSpec((depth, part), whole),
            ],
            out_specs=[
                pl.BlockSpec((step * length, width), lambda i, w: (i, 0)),
                pl.BlockSpec((1, step, width), lambda i, w: (i, 0, 0)),
                pl.BlockSpec((step * length, 2 * part), lambda i, w: (i, 0)),
            ],
        ),
        out_shape=[
            pltpu.VMEM((passages * length, width), BF16),
            jax.ShapeDtypeStruct((steps, step, width), F32),
            pltpu.VMEM((passages * length, 2 * part), F32),
        ],
        compiler_params=params(),
        cost_estimate=cost(7),
        name="norm_project",
    )(where, *held(pltpu.HBM, hidden), gain[None], *weights)
    return normal, sums, product


WIDE = 2 * HEAD_DIM
BATCH = 8


def low_lanes(rows):
    return lax.broadcasted_iota(jnp.int32, (rows, WIDE), 1) < HEAD_DIM


def ones_block(repeat):
    row = lax.broadcasted_iota(jnp.int32, (repeat * WIDE, WIDE), 0) // HEAD_DIM % 2
    col = lax.broadcasted_iota(jnp.int32, (repeat * WIDE, WIDE), 1) // HEAD_DIM
    return jnp.where(row == col, 1.0, 0.0).astype(BF16)


def diagonals(pair, factor):
    low = low_lanes(HEAD_DIM)
    wide = pair.astype(F32) * factor
    turned = pltpu.roll(wide, HEAD_DIM, 1)
    out = []
    for first, second in ((wide, turned), (turned, wide)):
        block = [jnp.where(low, first, 0.0), jnp.where(low, 0.0, second)]
        out.append(jnp.concatenate(block, 0).astype(BF16))
    return out


def segment_max(scores):
    low = low_lanes(scores.shape[0])
    first = jnp.max(jnp.where(low, scores, -jnp.inf), 1, keepdims=True)
    second = jnp.max(jnp.where(low, -jnp.inf, scores), 1, keepdims=True)
    return jnp.where(low, first, second)


def stacked(ref, rows, g):
    at = g * GROUP
    return jnp.concatenate([ref[rows, at : at + WIDE], ref[rows, at + WIDE : at + GROUP]], 0)


def project(refs, pieces, whole):
    blocks, refs = refs[:pieces], refs[pieces:]
    weights, refs = refs[: 2 * pieces], refs[2 * pieces :]
    join(weights, whole)
    rows = blocks[0][...]
    if pieces > 1:
        rows = jnp.concatenate([rows] + [block[...] for block in blocks[1:]], 1)
    return mm(rows, whole[...]), refs


def partial_kernel(pieces, before, where_ref, *refs):
    refs, whole = refs[:-1], refs[-1]
    product, refs = project(refs, pieces, whole)
    refs[-1][...] = product + refs[0][...] if before else product


def forward_kernel(pieces, groups, where_ref, *refs):
    refs, whole = refs[:-1], refs[-1]
    projected, refs = project(refs, pieces, whole)
    before_ref, projected_ref, probs_ref, sum_ref = refs
    projected = projected + before_ref[...]
    projected_ref[...] = projected.astype(BF16)
    ones = ones_block(1)
    width_q = groups * GROUP
    width_k = groups * HEAD_DIM
    count = projected_ref.shape[0] // PASSAGE_LEN
    spans = [slice(i * PASSAGE_LEN, (i + 1) * PASSAGE_LEN) for i in range(count)]
    keys = [diagonals(projected_ref[r, width_q : width_q + width_k], scale) for r in spans]
    values = [diagonals(projected_ref[r, width_q + width_k :], 1.0) for r in spans]
    for g in range(groups):
        scores = jnp.concatenate(
            [mm(stacked(projected_ref, r, g), keys[i][g], ((1,), (1,))) for i, r in enumerate(spans)],
            0,
        )
        expo = jnp.exp(scores - segment_max(scores))
        total = mm(expo.astype(BF16), ones)
        probs = (expo / total).astype(BF16)
        probs_ref[0, g] = probs
        for i in range(count):
            attended = mm(probs[i * WIDE : (i + 1) * WIDE], values[i][g])
            attended = attended.astype(BF16).astype(F32)
            for j in range(2):
                at = g * GROUP + j * WIDE
                sum_ref[0, i : i + 1, at : at + WIDE] = jnp.sum(
                    attended[j * HEAD_DIM : (j + 1) * HEAD_DIM], 0, keepdims=True
                )


def join(weights, whole):
    @pl.when(pl.program_id(0) == 0)
    def _():
        depth, part = weights[0].shape
        for k in range(len(weights) // 2):
            rows = slice(k * depth, (k + 1) * depth)
            whole[rows, :part] = weights[2 * k][...]
            whole[rows, part:] = weights[2 * k + 1][...]


def row_step(total, batch):
    batch = batch if total % (batch * PASSAGE_LEN) == 0 else 1
    return batch, batch * PASSAGE_LEN


def block_of(step, depth, s):
    return pl.BlockSpec((step, depth), lambda i, w: (i, w[0] ^ s))


def partial_project(where, rows, weights, before):
    total, width = rows.shape
    depth, part = next(iter(weights.values()))[0].shape
    _, step = row_step(total, BATCH)
    pieces = len(weights)
    flat = [x for s in weights for x in weights[s]]
    out = pl.BlockSpec((step, 2 * part), lambda i, w: (i, 0))
    return pl.pallas_call(
        functools.partial(partial_kernel, pieces, True),
        grid_spec=pltpu.PrefetchScalarGridSpec(
            num_scalar_prefetch=1,
            grid=(total // step,),
            in_specs=[block_of(step, depth, s) for s in weights]
            + [pl.BlockSpec(x.shape, lambda i, w: (0, 0)) for x in flat]
            + [out],
            out_specs=out,
            scratch_shapes=[pltpu.VMEM((pieces * depth, 2 * part), BF16)],
        ),
        out_shape=pltpu.VMEM((total, 2 * part), F32),
        compiler_params=params(),
        cost_estimate=cost(4.5),
        name="project_more",
    )(where, *held(pltpu.VMEM, *([rows] * pieces)), *flat, *held(pltpu.VMEM, before))


def forward(where, rows, weights, groups, before):
    total, width = rows.shape
    pieces = len(weights)
    flat = [x for s in weights for x in weights[s]]
    depth, part = flat[0].shape
    out_width = 2 * part
    batch, step = row_step(total, BATCH)
    steps = total // step
    heads = groups * GROUP
    return pl.pallas_call(
        functools.partial(forward_kernel, pieces, groups),
        grid_spec=pltpu.PrefetchScalarGridSpec(
            num_scalar_prefetch=1,
            grid=(steps,),
            in_specs=[block_of(step, depth, s) for s in weights]
            + [pl.BlockSpec(x.shape, lambda i, w: (0, 0)) for x in flat]
            + [pl.BlockSpec((step, out_width), lambda i, w: (i, 0))],
            out_specs=[
                pl.BlockSpec((step, out_width), lambda i, w: (i, 0)),
                pl.BlockSpec((1, groups, batch * WIDE, WIDE), lambda i, w: (i, 0, 0, 0)),
                pl.BlockSpec((1, batch, heads), lambda i, w: (i, 0, 0)),
            ],
            scratch_shapes=[pltpu.VMEM((pieces * depth, out_width), BF16)],
        ),
        out_shape=[
            jax.ShapeDtypeStruct((total, out_width), BF16),
            jax.ShapeDtypeStruct((steps, groups, batch * WIDE, WIDE), BF16),
            jax.ShapeDtypeStruct((steps, batch, heads), F32),
        ],
        compiler_params=params(),
        cost_estimate=cost(6.5),
        name="project_attend",
    )(where, *held(pltpu.VMEM, *([rows] * pieces)), *flat, *held(pltpu.VMEM, before))


def backward_kernel(groups, probs_ref, projected_ref, d_ref, out_ref):
    low = low_lanes(HEAD_DIM)
    ones = ones_block(2)
    width_q = groups * GROUP
    width_k = groups * HEAD_DIM
    count = projected_ref.shape[0] // PASSAGE_LEN
    spans = [slice(i * PASSAGE_LEN, (i + 1) * PASSAGE_LEN) for i in range(count)]
    keys = [diagonals(projected_ref[r, width_q : width_q + width_k], scale) for r in spans]
    values = [diagonals(projected_ref[r, width_q + width_k :], 1.0) for r in spans]
    down = ((0,), (0,))
    d_keys = [[] for _ in spans]
    d_values = [[] for _ in spans]

    def fold(product):
        kept = jnp.where(low, product[:HEAD_DIM], product[HEAD_DIM:])
        return kept + pltpu.roll(kept, HEAD_DIM, 1)

    for g in range(groups):
        probs = probs_ref[0, g]
        d_rows = []
        for i in range(count):
            row = [
                d_ref[0, i : i + 1, g * GROUP + j * WIDE : g * GROUP + (j + 1) * WIDE]
                for j in range(2)
            ]
            d_rows.append(
                jnp.concatenate(
                    [jnp.broadcast_to(x, (HEAD_DIM, WIDE)) for x in row], 0
                ).astype(BF16)
            )
        d_probs = jnp.concatenate(
            [mm(d_rows[i], values[i][g], ((1,), (1,))) for i in range(count)], 0
        )
        probs_f = probs.astype(F32)
        product = probs_f * d_probs
        upper = product.astype(BF16)
        lower = (product - upper.astype(F32)).astype(BF16)
        inner = mm(jnp.concatenate([upper, lower], 1), ones)
        d_scores = (probs_f * (d_probs - inner)).astype(BF16)
        for i, r in enumerate(spans):
            block = slice(i * WIDE, (i + 1) * WIDE)
            d_query = mm(d_scores[block], keys[i][g]).astype(BF16)
            at = g * GROUP
            out_ref[r, at : at + WIDE] = d_query[:HEAD_DIM]
            out_ref[r, at + WIDE : at + GROUP] = d_query[HEAD_DIM:]
            d_keys[i].append(fold(mm(d_scores[block], stacked(projected_ref, r, g), down)) * scale)
            d_values[i].append(fold(mm(probs[block], d_rows[i], down)))
    for i, r in enumerate(spans):
        out_ref[r, width_q : width_q + width_k] = jnp.where(low, *d_keys[i]).astype(BF16)
        out_ref[r, width_q + width_k :] = jnp.where(low, *d_values[i]).astype(BF16)


def backward(probs, projected, d_attended, groups):
    total, out_width = projected.shape
    steps = probs.shape[0]
    step = total // steps
    batch = step // PASSAGE_LEN
    heads = groups * GROUP
    return pl.pallas_call(
        functools.partial(backward_kernel, groups),
        grid=(steps,),
        in_specs=[
            pl.BlockSpec((1,) + probs.shape[1:], lambda i: (i, 0, 0, 0)),
            pl.BlockSpec((step, out_width), lambda i: (i, 0)),
            pl.BlockSpec((1, batch, heads), lambda i: (i, 0, 0)),
        ],
        out_specs=pl.BlockSpec((step, out_width), lambda i: (i, 0)),
        out_shape=pltpu.VMEM((total, out_width), BF16),
        compiler_params=params(),
        cost_estimate=cost(3.4),
        name="attend_back",
    )(probs, projected, d_attended.reshape(steps, batch, heads))


def score_kernel(chips, where_ref, own_ref, sib_ref, own_far_ref, sib_far_ref, sum_ref, sib_sum_ref,
                 final_ref, ws_ref, prior_ref, prior_sib_ref, *refs):
    pieces, refs = refs[: 4 * chips], refs[4 * chips :]
    unit_ref, inverse_ref, score_ref, attn_ref, product_ref = refs
    chip, core = where_ref[0], where_ref[1]
    mine = jnp.concatenate([own_ref[...], sib_ref[...]], 0)
    other = jnp.concatenate([own_far_ref[...], sib_far_ref[...]], 0)
    sums = [ref[k] for ref in (sum_ref, sib_sum_ref) for k in range(ref.shape[0])]
    attn = jnp.concatenate(
        [jnp.where(core == 0, mine, other), jnp.where(core == 0, other, mine)], 1
    )
    count = attn.shape[0]
    upper = attn.astype(BF16)
    attn_ref[...] = upper
    both = jnp.concatenate([upper.astype(F32), attn - upper.astype(F32)], 0)
    product_ref[...] = both
    depth, part = pieces[0].shape
    out = [None] * 4
    for s in range(chips):
        start = pl.multiple_of((chip ^ s) * depth, depth)
        block = product_ref[:, pl.ds(start, depth)].astype(BF16)
        for k in range(4):
            x = mm(block, pieces[4 * s + k][...])
            out[k] = x if out[k] is None else out[k] + x
    out = [x[:count] + x[count:] for x in out]
    own, far = jnp.concatenate(out[:2], 1), jnp.concatenate(out[2:], 1)
    product = jnp.concatenate(
        [jnp.where(core == 0, own, far), jnp.where(core == 0, far, own)], 1
    )
    pooled = (jnp.concatenate(sums, 0) + product) * (1.0 / PASSAGE_LEN)
    inverse = lax.rsqrt(jnp.mean(pooled * pooled, -1, keepdims=True) + epsilon)
    unit = pooled * inverse
    score = jnp.sum(unit * (final_ref[...] * ws_ref[...]), -1, keepdims=True)
    unit_ref[...] = unit
    inverse_ref[...] = jnp.broadcast_to(inverse, inverse_ref.shape)
    lane = lax.broadcasted_iota(jnp.int32, score_ref.shape, 1)
    half = score_ref.shape[1] // 2
    prior = jnp.concatenate([prior_ref[...], prior_sib_ref[...]], 0)
    score_ref[...] = jnp.where(lane < half, score, 0.0) + prior


def score_pass(where, attn, sums, final_gain, w_score, priors, pieces):
    count, width = 2 * attn[0].shape[0], sums[0].shape[2]
    lanes = priors[0].shape[1]
    inner = 2 * attn[0].shape[1]
    vmem = pl.BlockSpec(memory_space=pltpu.VMEM)
    return pl.pallas_call(
        functools.partial(score_kernel, len(pieces) // 4),
        in_specs=[pl.BlockSpec(memory_space=pltpu.SMEM)] + [vmem] * (10 + len(pieces)),
        out_specs=[vmem] * 4,
        out_shape=[
            jax.ShapeDtypeStruct((count, width), F32),
            jax.ShapeDtypeStruct((count, lanes), F32),
            jax.ShapeDtypeStruct((count, lanes), F32),
            jax.ShapeDtypeStruct((count, inner), BF16),
        ],
        scratch_shapes=[pltpu.VMEM((2 * count, inner), F32)],
        compiler_params=pltpu.CompilerParams(vmem_limit_bytes=SMALL),
        cost_estimate=cost(2),
        name="pool_score",
    )(where, *attn, *sums, final_gain[None], w_score[None], *priors, *pieces)


def list_kernel(blocks, chips, passages, where_ref, place_ref, bounds_ref, unit_ref, inverse_ref,
                attn_ref, final_ref, ws_ref, *refs):
    scores = [ref[...] for ref in refs[:blocks]]
    pieces, refs = refs[blocks : blocks + 4 * chips], refs[blocks + 4 * chips :]
    d_att_ref, payload_ref, back_ref = refs
    chip, core = where_ref[0], where_ref[1]
    pair = 2 * passages
    lanes = bounds_ref.shape[1]
    lane = lax.broadcasted_iota(jnp.int32, bounds_ref.shape, 1)
    ends, reach = bounds_ref[...], 1
    while reach < lanes:
        ends = ends + jnp.where(lane >= reach, pltpu.roll(ends, reach, 1), 0)
        reach *= 2
    starts, ends = (ends - bounds_ref[...])[:1], ends[:1]
    row = lax.broadcasted_iota(jnp.int32, (pair, lanes), 0)
    near = jnp.where(row < passages, core * passages + row, (1 - core) * passages + row - passages)
    far = jnp.where(row < passages, (1 - core) * passages + row, core * passages + row - passages)
    members = []
    for j in range(blocks):
        place = place_ref[j] * pair + (near if j <= blocks // 2 else far)
        members.append((place >= starts) & (place < ends))
    high = scores[0].shape[1] // 2
    column = [jnp.broadcast_to(score[:, :1], (pair, lanes)) for score in scores]
    heavy = [jnp.broadcast_to(score[:, high : high + 1], (pair, lanes)) for score in scores]
    peak = functools.reduce(
        jnp.maximum,
        [jnp.max(jnp.where(m, s, -1e30), 0, keepdims=True) for m, s in zip(members, column)],
    )
    total = sum(
        jnp.sum(jnp.where(m, jnp.exp(jnp.where(m, s - peak, 0.0)), 0.0), 0, keepdims=True)
        for m, s in zip(members, column)
    )
    label_total = sum(
        jnp.sum(jnp.where(m, w, 0.0), 0, keepdims=True) for m, w in zip(members, heavy)
    )
    log_norm = peak + jnp.log(total)
    own = members[0]
    log_prob = column[0][:, :1] - jnp.sum(jnp.where(own, log_norm, 0.0), 1, keepdims=True)
    target = heavy[0][:, :1] / jnp.sum(jnp.where(own, label_total, 0.0), 1, keepdims=True)
    loss = -loss_scale * jnp.sum((target * log_prob)[:passages], 0, keepdims=True)
    d_score = loss_scale * (jnp.exp(log_prob) - target)
    unit = unit_ref[...]
    d_unit = d_score * (ws_ref[...] * final_ref[...])
    mean = jnp.mean(d_unit * unit, -1, keepdims=True)
    d_pooled = inverse_ref[:, :1] * (d_unit - unit * mean)
    depth, part = pieces[0].shape
    half = d_pooled.shape[1] // 2
    own = jnp.where(core == 0, d_pooled[:, :half], d_pooled[:, half:])
    far = jnp.where(core == 0, d_pooled[:, half:], d_pooled[:, :half])
    cut = [own[:, :part], own[:, part:], far[:, :part], far[:, part:]]
    cut = [(x * (1.0 / PASSAGE_LEN)).astype(BF16) for x in cut]
    for s in range(chips):
        back = sum(mm(cut[k], pieces[4 * s + k][...], ((1,), (1,))) for k in range(4))
        start = pl.multiple_of((chip ^ s) * depth, depth)
        back_ref[:, pl.ds(start, depth)] = back.astype(BF16).astype(F32)
    back = back_ref[...]
    half = back.shape[1] // 2
    d_att_ref[...] = jnp.where(core == 0, back[:, :half], back[:, half:])
    attn = attn_ref[...].astype(F32)
    columns = [jnp.where(core == 0, attn[:, :half], attn[:, half:])]
    columns += [x.astype(F32) for x in cut[:2]]
    rest = jnp.broadcast_to(loss, (pair, 128))
    for _ in range(3):
        columns.append(rest.astype(BF16).astype(F32))
        rest = rest - columns[-1]
    columns = jnp.concatenate(columns, 1)
    turned = jnp.concatenate([columns[passages:], columns[:passages]], 0)
    payload_ref[...] = jnp.where(core == 0, columns, turned).astype(BF16)


def list_pass(where, places, bounds, unit, inverse, attn, final_gain, w_score, scores, pieces,
              passages):
    count, width = unit.shape
    chips = len(pieces) // 4
    inner = chips * pieces[0].shape[0]
    vmem = pl.BlockSpec(memory_space=pltpu.VMEM)
    smem = pl.BlockSpec(memory_space=pltpu.SMEM)
    return pl.pallas_call(
        functools.partial(list_kernel, len(scores), chips, passages),
        in_specs=[smem] * 2 + [vmem] * (6 + len(scores) + len(pieces)),
        out_specs=[vmem] * 2,
        out_shape=[
            jax.ShapeDtypeStruct((count, inner // 2), F32),
            jax.ShapeDtypeStruct((count, (inner + width) // 2 + 3 * 128), BF16),
        ],
        scratch_shapes=[pltpu.VMEM((count, inner), F32)],
        compiler_params=pltpu.CompilerParams(vmem_limit_bytes=SMALL),
        cost_estimate=cost(2.5),
        name="list_grad",
    )(where, places, bounds, unit, inverse, attn, final_gain[None], w_score[None], *scores,
      *pieces)


EXTRA = 16


def out_kernel(chips, where_ref, left_ref, *refs):
    near, far, out_ref = refs[:chips], refs[chips], refs[chips + 1]
    core = where_ref[1]
    cols = out_ref.shape[1] // 2
    own_rows = out_ref.shape[0] - EXTRA
    lead = far.shape[1] - 3 * 128 - cols
    mine = jnp.concatenate([ref[...] for ref in near], 0)
    other = far[...]
    down = ((0,), (0,))
    products = [mm(left_ref[...], x[:, lead : lead + cols], down) for x in (mine, other)]
    out_ref[:own_rows, :cols] = jnp.where(core == 0, *products).astype(BF16)
    out_ref[:own_rows, cols:] = jnp.where(core == 0, *products[::-1]).astype(BF16)

    count = mine.shape[0] // chips
    losses = []
    for s in range(chips):
        total = 0.0
        for x in (mine, other):
            row = x[s * count : s * count + EXTRA, lead + cols :].astype(F32)
            total = total + (row[:, :128] + row[:, 128:256] + row[:, 256:])
        losses.append(total)
    while len(losses) > 1:
        losses = [a + b for a, b in zip(losses[0::2], losses[1::2])]
    rest = losses[0]
    parts = []
    for _ in range(3):
        parts.append(rest.astype(BF16).astype(F32))
        rest = rest - parts[-1]
    row = jnp.concatenate(parts + [jnp.zeros_like(rest)], 1).astype(BF16)
    out_ref[own_rows:] = jnp.concatenate([row] * (2 * cols // row.shape[1]), 1)


def out_pass(where, left, near, far, cols):
    vmem = pl.BlockSpec(memory_space=pltpu.VMEM)
    return pl.pallas_call(
        functools.partial(out_kernel, len(near)),
        in_specs=[pl.BlockSpec(memory_space=pltpu.SMEM)] + [vmem] * (2 + len(near)),
        out_specs=vmem,
        out_shape=jax.ShapeDtypeStruct((left.shape[1] + EXTRA, 2 * cols), BF16),
        compiler_params=pltpu.CompilerParams(vmem_limit_bytes=SMALL),
        cost_estimate=cost(1),
        name="out_rows",
    )(where, left, *near, far)


def grad_kernel(where_ref, own_ref, sib_ref, d_own_ref, d_sib_ref, a_ref, b_ref):
    down = ((0,), (0,))
    out = mm(own_ref[...], d_own_ref[...], down) + mm(sib_ref[...], d_sib_ref[...], down)
    out = out.astype(BF16)
    a_ref[...] = out[:, : a_ref.shape[1]]
    b_ref[...] = out[:, a_ref.shape[1] :]


def grad_block(where, s, own, sib, d_own, d_sib, depth):
    rows = own.shape[0]
    width = d_own.shape[1]
    tile = min(depth, 256)
    tiles = depth // tile
    part = width // 2

    def lhs(i, w):
        return (0, (w[0] ^ s) * tiles + i)

    whole = lambda i, w: (0, 0)
    return pl.pallas_call(
        grad_kernel,
        grid_spec=pltpu.PrefetchScalarGridSpec(
            num_scalar_prefetch=1,
            grid=(tiles,),
            in_specs=[
                pl.BlockSpec((rows, tile), lhs),
                pl.BlockSpec((rows, tile), lhs),
                pl.BlockSpec((rows, width), whole),
                pl.BlockSpec((rows, width), whole),
            ],
            out_specs=[pl.BlockSpec((tile, part), lambda i, w: (i, 0))] * 2,
        ),
        out_shape=[jax.ShapeDtypeStruct((depth, part), BF16)] * 2,
        compiler_params=params(),
        cost_estimate=cost(3.8),
        name="grad_rows",
    )(where, *held(pltpu.VMEM, own, sib), *held(pltpu.VMEM, d_own, d_sib))


def pick_kernel(starts, sizes, where_ref, mine_ref, come_ref, a_ref, b_ref):
    core = where_ref[1]
    mine, come = mine_ref[...].astype(F32), come_ref[...].astype(F32)
    rows = mine.shape[0]
    halves = []
    for h in range(2):
        spans = [slice(a + h * n, a + (h + 1) * n) for a, n in zip(starts, sizes)]
        halves.append([jnp.concatenate([x[:, t] for t in spans], 1) for x in (mine, come)])
    first = jnp.where(core == 0, halves[0][0], halves[1][1]).astype(BF16)
    second = jnp.where(core == 0, halves[0][1], halves[1][0]).astype(BF16)
    part = a_ref.shape[1]
    a_ref[:rows], b_ref[:rows] = first[:, :part], first[:, part:]
    a_ref[rows:], b_ref[rows:] = second[:, :part], second[:, part:]


def pick(where, mine, come, starts, sizes):
    rows = mine.shape[0]
    vmem = pl.BlockSpec(memory_space=pltpu.VMEM)
    return pl.pallas_call(
        functools.partial(pick_kernel, starts, sizes),
        in_specs=[pl.BlockSpec(memory_space=pltpu.SMEM), vmem, vmem],
        out_specs=[vmem] * 2,
        out_shape=[jax.ShapeDtypeStruct((2 * rows, sum(sizes) // 2), BF16)] * 2,
        compiler_params=pltpu.CompilerParams(vmem_limit_bytes=SMALL),
        cost_estimate=cost(1),
        name="pick_columns",
    )(where, mine, come)


def solution(mesh):
    n_list, n_fsdp = mesh.shape["list"], mesh.shape["fsdp"]
    bits = [1 << k for k in range(1, n_fsdp.bit_length() - 1)]
    pairs = n_list * n_fsdp // 2

    def across(value, distance):
        return lax.ppermute(value, "fsdp", [(i, i ^ distance) for i in range(n_fsdp)])

    def along(value, distance):
        return lax.ppermute(value, "list", [(i, i ^ distance) for i in range(n_list)])

    def partner(kind, pair):
        return (
            pair ^ 1,
            ((pair + 1) ^ 1) - 1,
            pair ^ 2,
            ((pair + 2) ^ 2) - 2,
        )[kind]

    def neighbour(value, kind):
        moves = []
        for pair in range(pairs):
            for core in (0, 1):
                other = partner(kind + core, pair)
                if 0 <= other < pairs:
                    moves.append((2 * pair + core, 2 * other + core))
        return lax.ppermute(value, ("list", "fsdp"), moves)

    def after(value, *others):
        return lax.optimization_barrier((value, others))[0]

    def gathered(value, order, gates=()):
        have = {0: value}
        for k, bit in enumerate(order):
            near, far = gates[k - 1] if 0 < k <= len(gates) else (None, None)
            ready = {
                s: after(part, far if s else near) if k and gates else part
                for s, part in have.items()
            }
            have.update({s ^ (bit >> 1): across(part, bit) for s, part in ready.items()})
        return have

    def joined(parts, come, bit):
        return {
            s: (parts[s].astype(F32) + come[s].astype(F32)).astype(BF16)
            for s in parts
            if not s & (bit >> 1)
        }

    def sent(parts, bit):
        flag = bit >> 1
        return {s ^ flag: across(parts[s], bit) for s in sorted(parts)[::-1] if s & flag}

    def local(hidden, norm_gain, w_qkv, w_out, final_gain, w_score, prior, labels, lengths):
        passages, _, width = hidden.shape
        assert 4 * passages >= LONGEST - 1
        groups = KV_HEADS // 2
        width_q, width_k = groups * GROUP, groups * HEAD_DIM
        index = lax.axis_index("fsdp")
        core = index % 2
        chip = index // 2
        where = jnp.stack([chip, core]).astype(jnp.int32)
        first_core = core == 0

        def ordered(mine, other, axis):
            return jnp.where(
                first_core,
                jnp.concatenate([mine, other], axis),
                jnp.concatenate([other, mine], axis),
            )

        starts = (0, 2 * width_q, 2 * (width_q + width_k))
        sizes = (width_q, width_k, width_k)
        come = across(w_qkv, 1)
        pair_a, pair_b = pick(where, w_qkv, come, starts, sizes)
        w_out = after(w_out, come)
        out_come = across(w_out, 1)
        hidden_sib = across(after(hidden, come), 1)

        normal, sums, before_own = norm(where, hidden, norm_gain, (pair_a, pair_b))
        normal_sib, sums_sib, before_sib = norm(
            where, after(hidden_sib, before_own), norm_gain, (pair_a, pair_b)
        )
        gates = ((before_own, before_sib),) * (len(bits) - 1)
        part_a = gathered(pair_a, bits, gates)
        part_b = gathered(pair_b, bits[::-1], gates)
        chips = n_fsdp // 2
        last = max(bin(s).count("1") for s in range(chips))
        weights = [{}, {}, {}]
        for s in range(chips):
            ones = bin(s).count("1")
            weights[2 if ones == last else 1 if ones else 0][s] = (part_a[s], part_b[s])

        cols = w_out.shape[1] // 2
        both = ordered(w_out, out_come, 0)
        out_pair = jnp.where(first_core, both[:, :cols], both[:, cols:])
        prior, labels, lengths, out_pair = after((prior, labels, lengths, out_pair), before_sib)
        if weights[1]:
            normal_first = after(normal, before_sib)
            before_own = partial_project(where, normal_first, weights[1], before_own)
            before_sib = partial_project(
                where, after(normal_sib, before_own), weights[1], before_sib
            )
            out_pair = after(out_pair, before_sib)
        before_own, before_sib, weights[2] = after((before_own, before_sib, weights[2]), before_sib)
        proj_sib, probs_sib, attn_sib = forward(where, normal_sib, weights[2], groups, before_sib)
        attn_sib = attn_sib.reshape(passages, -1)
        attn_sib_other = across(attn_sib, 1)
        gates = ((attn_sib, attn_sib),) * (len(bits) - 1)
        out_a = gathered(out_pair[:, : cols // 2], bits, gates)
        out_b = gathered(out_pair[:, cols // 2 :], bits[::-1], gates)
        lanes = -(-lengths.shape[0] // 128) * 128
        label_weight = jnp.exp(labels.astype(F32))
        small = jnp.concatenate(
            [jnp.broadcast_to(x[:, None], (passages, 64)) for x in (prior, label_weight)], 1
        )
        small_sib = across(small, 1)
        pair = lax.axis_index("list") * (n_fsdp // 2) + chip
        places = [pair] + [
            jnp.where(first_core == near, partner(2 * kind, pair), partner(2 * kind + 1, pair))
            for near in (True, False)
            for kind in range(2)
        ]
        places = jnp.stack(places).astype(jnp.int32)
        bounds = jnp.broadcast_to(
            jnp.pad(lengths, (0, lanes - lengths.shape[0]))[None], (8, lanes)
        )

        normal_last = after(normal, probs_sib, places, bounds, small_sib)
        proj_own, probs_own, attn_own = forward(where, normal_last, weights[2], groups, before_own)
        attn_own = attn_own.reshape(passages, -1)
        attn_own_other = across(attn_own, 1)
        pieces = []
        for s in range(chips):
            gate = probs_sib if bin(s).count("1") == last else before_sib
            pieces += [out_a[s], out_b[s]]
            pieces += [across(after(x, gate), 1) for x in (out_a[s], out_b[s])]
        unit, inverse, score, attn = score_pass(
            where,
            (attn_own, attn_sib, attn_sib_other, attn_own_other),
            (sums, sums_sib),
            final_gain,
            w_score,
            (small, small_sib),
            pieces,
        )
        near = [neighbour(score, kind) for kind in (0, 2)]
        scores = [score] + near + [across(x, 1) for x in near]
        d_attended, payload = list_pass(
            where, places, bounds, unit, inverse, attn, final_gain, w_score, scores, pieces,
            passages,
        )

        d_own = backward(probs_own, proj_own, d_attended[:passages], groups)
        d_sib = backward(
            after(probs_sib, d_own), proj_sib, d_attended[passages:], groups
        )
        depth = pair_a.shape[0]
        parts_a, parts_b, come_a, come_b = {}, {}, {}, {}
        flag_a, flag_b = bits[0] >> 1, bits[-1] >> 1
        before = d_sib
        for s in sorted(range(chips), key=lambda s: (-bin(s).count("1"), s)):
            gate = (before, come_a, come_b) if s == 0 else before
            parts_a[s], parts_b[s] = grad_block(
                where, s, normal, normal_sib, d_own, after(d_sib, gate), depth
            )
            if s & flag_a and s & flag_b:
                come_a[s ^ flag_a] = across(parts_a[s], bits[0])
                come_b[s ^ flag_b] = across(parts_b[s], bits[-1])
            before = parts_a[s]
        first_a, first_b = dict(come_a), dict(come_b)
        for s in range(chips):
            if s & flag_a and s ^ flag_a not in first_a:
                first_a[s ^ flag_a] = across(parts_a[s], bits[0])
            if s & flag_b and s ^ flag_b not in first_b:
                first_b[s ^ flag_b] = across(parts_b[s], bits[-1])
        left_a, left_b = joined(parts_a, first_a, bits[0]), joined(parts_b, first_b, bits[-1])
        gate = (left_a, left_b)
        for bit_a, bit_b in zip(bits[1:], bits[::-1][1:]):
            left_a = joined(left_a, sent(left_a, bit_a), bit_a)
            left_b = joined(left_b, sent(left_b, bit_b), bit_b)
        sum_a, sum_b = left_a[0], left_b[0]
        gates = ((parts_a[0], parts_a[0]),) * (len(bits) - 1)
        plane = gathered(after(payload, d_own), bits, gates)
        plane = after([plane[s] for s in range(chips)], gate)
        chip_sum = jnp.concatenate([sum_a, sum_b], 1)
        upper, lower = chip_sum[: depth // 2], chip_sum[depth // 2 :]
        keep = jnp.where(first_core, upper, lower)
        come = across(jnp.where(first_core, lower, upper), 1)
        columns = []
        at = 0
        for n in sizes:
            columns.append(ordered(keep[:, at : at + n], come[:, at : at + n], 1))
            at += n
        rows_sum = jnp.concatenate(columns, 1)
        place = lax.axis_index("list")

        def list_scatter(value):
            n = value.shape[1] // n_list
            block = lambda which: lax.dynamic_slice_in_dim(value, which * n, n, 1)
            total = block(place).astype(F32)
            for distance in range(1, n_list):
                total = total + along(block(place ^ distance).astype(BF16), distance).astype(F32)
            return total

        grad_qkv = list_scatter(rows_sum)

        far = across(jnp.concatenate(plane, 0), 1)
        inner = 2 * width_q
        left = ordered(
            jnp.concatenate([x[:, :width_q] for x in plane], 0), far[:, :width_q], 1
        )
        own_rows = inner // n_fsdp
        left = lax.dynamic_slice_in_dim(left, index * own_rows, own_rows, 1)
        rows = out_pass(where, left, plane, far, cols)
        blocks = rows.shape[1] // n_list
        block = lambda which: lax.dynamic_slice_in_dim(rows, which * blocks, blocks, 1)
        come = [block(place)]
        come += [along(block(place ^ distance), distance) for distance in range(1, n_list)]
        grad_out = sum(x[:own_rows].astype(F32) for x in come)
        losses = []
        for x in come:
            x = x[own_rows].astype(F32)
            losses.append(x[0] + x[128] + x[256])
        while len(losses) > 1:
            losses = [a + b for a, b in zip(losses[0::2], losses[1::2])]
        return (losses[0], grad_qkv, grad_out)

    placed = (
        P(("list", "fsdp"), None, None),
        P(),
        P("fsdp", None),
        P("fsdp", None),
        P(),
        P(),
        P(("list", "fsdp")),
        P(("list", "fsdp")),
        P(),
    )
    return jax.shard_map(
        local,
        mesh=mesh,
        in_specs=placed,
        out_specs=(P(), P("fsdp", "list"), P("fsdp", "list")),
        check_vma=False,
    )
```

```python
import functools

import jax
import jax.numpy as jnp
from jax import lax
from jax.experimental import pallas as pl
from jax.experimental.pallas import tpu as pltpu
from jax.sharding import PartitionSpec as P

HEADS = 16
KV_HEADS = 4
HEAD_DIM = 64
PASSAGE_LEN = 64
LONGEST = 48
RATIO = HEADS // KV_HEADS
GROUP = RATIO * HEAD_DIM

epsilon = 1e-05
loss_scale = 64.0
scale = HEAD_DIM ** (-0.5)
VMEM = 16 * 1024 * 1024
SMALL = 10 * 1024 * 1024


def cost(micros):
    return pl.CostEstimate(flops=int(micros * 5e8), bytes_accessed=int(micros * 3.5e6), transcendentals=0)

BF16 = jnp.bfloat16
F32 = jnp.float32


def params(grid=1):
    return pltpu.CompilerParams(
        vmem_limit_bytes=VMEM, dimension_semantics=("arbitrary",) * grid
    )


def held(space, *values):
    return [pltpu.with_memory_space_constraint(x, space) for x in values]


def mm(a, b, dims=((1,), (0,))):
    return lax.dot_general(a, b, (dims, ((), ())), preferred_element_type=F32)


def norm_kernel(where_ref, hidden_ref, gain_ref, a_ref, b_ref, normal_ref, sum_ref, out_ref):
    values = hidden_ref[...].astype(F32)
    mean_square = jnp.mean(values * values, -1, keepdims=True)
    out = values * lax.rsqrt(mean_square + epsilon) * gain_ref[...][None]
    normal_ref[...] = out.reshape(normal_ref.shape).astype(BF16)
    sum_ref[0] = jnp.sum(values, 1)
    depth, part = a_ref.shape
    start = pl.multiple_of(where_ref[0] * depth, depth)
    block = normal_ref[:, pl.ds(start, depth)]
    out_ref[:, :part] = mm(block, a_ref[...])
    out_ref[:, part:] = mm(block, b_ref[...])


def norm(where, hidden, gain, weights):
    passages, length, width = hidden.shape
    depth, part = weights[0].shape
    step = 4 if passages % 4 == 0 else 1
    steps = passages // step
    whole = lambda i, w: (0, 0)
    normal, sums, product = pl.pallas_call(
        norm_kernel,
        grid_spec=pltpu.PrefetchScalarGridSpec(
            num_scalar_prefetch=1,
            grid=(steps,),
            in_specs=[
                pl.BlockSpec((step, length, width), lambda i, w: (i, 0, 0)),
                pl.BlockSpec((1, width), whole),
                pl.BlockSpec((depth, part), whole),
                pl.BlockSpec((depth, part), whole),
            ],
            out_specs=[
                pl.BlockSpec((step * length, width), lambda i, w: (i, 0)),
                pl.BlockSpec((1, step, width), lambda i, w: (i, 0, 0)),
                pl.BlockSpec((step * length, 2 * part), lambda i, w: (i, 0)),
            ],
        ),
        out_shape=[
            pltpu.VMEM((passages * length, width), BF16),
            jax.ShapeDtypeStruct((steps, step, width), F32),
            pltpu.VMEM((passages * length, 2 * part), F32),
        ],
        compiler_params=params(),
        cost_estimate=cost(7),
        name="norm_project",
    )(where, *held(pltpu.HBM, hidden), gain[None], *weights)
    return normal, sums, product


WIDE = 2 * HEAD_DIM
BATCH = 8


def low_lanes(rows):
    return lax.broadcasted_iota(jnp.int32, (rows, WIDE), 1) < HEAD_DIM


def ones_block(repeat):
    row = lax.broadcasted_iota(jnp.int32, (repeat * WIDE, WIDE), 0) // HEAD_DIM % 2
    col = lax.broadcasted_iota(jnp.int32, (repeat * WIDE, WIDE), 1) // HEAD_DIM
    return jnp.where(row == col, 1.0, 0.0).astype(BF16)


def diagonals(pair, factor):
    low = low_lanes(HEAD_DIM)
    wide = pair.astype(F32) * factor
    turned = pltpu.roll(wide, HEAD_DIM, 1)
    out = []
    for first, second in ((wide, turned), (turned, wide)):
        block = [jnp.where(low, first, 0.0), jnp.where(low, 0.0, second)]
        out.append(jnp.concatenate(block, 0).astype(BF16))
    return out


def segment_max(scores):
    low = low_lanes(scores.shape[0])
    first = jnp.max(jnp.where(low, scores, -jnp.inf), 1, keepdims=True)
    second = jnp.max(jnp.where(low, -jnp.inf, scores), 1, keepdims=True)
    return jnp.where(low, first, second)


def stacked(ref, rows, g):
    at = g * GROUP
    return jnp.concatenate([ref[rows, at : at + WIDE], ref[rows, at + WIDE : at + GROUP]], 0)


def product_of(chip, rows_ref, rows, shifts, weights):
    depth = weights[0].shape[0]
    out = []
    for part in range(2):
        total = None
        for k, s in enumerate(shifts):
            start = pl.multiple_of((chip ^ s) * depth, depth)
            x = mm(rows_ref[rows, pl.ds(start, depth)], weights[2 * k + part][...])
            total = x if total is None else total + x
        out.append(total)
    return out


def partial_kernel(shifts, step, where_ref, rows_ref, before_ref, *refs):
    weights, out_ref = refs[:-1], refs[-1]
    part = weights[0].shape[1]
    for i in range(rows_ref.shape[0] // step):
        rows = slice(i * step, (i + 1) * step)
        a, b = product_of(where_ref[0], rows_ref, rows, shifts, weights)
        out_ref[rows, :part] = a + before_ref[rows, :part]
        out_ref[rows, part:] = b + before_ref[rows, part:]


def forward_kernel(shifts, groups, batch, where_ref, rows_ref, before_ref, *refs):
    weights, refs = refs[: 2 * len(shifts)], refs[2 * len(shifts) :]
    projected_ref, probs_ref, sum_ref = refs
    part = weights[0].shape[1]
    ones = ones_block(1)
    width_q = groups * GROUP
    width_k = groups * HEAD_DIM
    step = batch * PASSAGE_LEN
    for n in range(rows_ref.shape[0] // step):
        rows = slice(n * step, (n + 1) * step)
        a, b = product_of(where_ref[0], rows_ref, rows, shifts, weights)
        projected_ref[rows, :part] = (a + before_ref[rows, :part]).astype(BF16)
        projected_ref[rows, part:] = (b + before_ref[rows, part:]).astype(BF16)
        spans = [
            slice(n * step + i * PASSAGE_LEN, n * step + (i + 1) * PASSAGE_LEN)
            for i in range(batch)
        ]
        keys = [diagonals(projected_ref[r, width_q : width_q + width_k], scale) for r in spans]
        values = [diagonals(projected_ref[r, width_q + width_k :], 1.0) for r in spans]
        for g in range(groups):
            scores = [
                mm(stacked(projected_ref, r, g), keys[i][g], ((1,), (1,)))
                for i, r in enumerate(spans)
            ]
            scores = jnp.concatenate(scores, 0)
            expo = jnp.exp(scores - segment_max(scores))
            total = mm(expo.astype(BF16), ones)
            probs = (expo / total).astype(BF16)
            probs_ref[n, g] = probs
            for i in range(batch):
                attended = mm(probs[i * WIDE : (i + 1) * WIDE], values[i][g])
                attended = attended.astype(BF16).astype(F32)
                for j in range(2):
                    at = g * GROUP + j * WIDE
                    sum_ref[n, i : i + 1, at : at + WIDE] = jnp.sum(
                        attended[j * HEAD_DIM : (j + 1) * HEAD_DIM], 0, keepdims=True
                    )


def row_step(total, batch):
    batch = batch if total % (batch * PASSAGE_LEN) == 0 else 1
    return batch, batch * PASSAGE_LEN


def local_call(kernel, name, micros, where, operands, out_shape):
    vmem = pl.BlockSpec(memory_space=pltpu.VMEM)
    return pl.pallas_call(
        kernel,
        in_specs=[pl.BlockSpec(memory_space=pltpu.SMEM)] + [vmem] * len(operands),
        out_specs=jax.tree.map(lambda _: vmem, out_shape),
        out_shape=out_shape,
        compiler_params=pltpu.CompilerParams(vmem_limit_bytes=VMEM),
        cost_estimate=cost(micros),
        name=name,
    )(where, *operands)


def partial_project(where, rows, weights, before):
    _, step = row_step(rows.shape[0], BATCH)
    return local_call(
        functools.partial(partial_kernel, tuple(weights), step),
        "project_more",
        4.5,
        where,
        [rows, before] + [x for s in weights for x in weights[s]],
        jax.ShapeDtypeStruct(before.shape, F32),
    )


def forward(where, rows, weights, groups, before):
    total = rows.shape[0]
    batch, step = row_step(total, BATCH)
    steps = total // step
    heads = groups * GROUP
    return local_call(
        functools.partial(forward_kernel, tuple(weights), groups, batch),
        "project_attend",
        6.5,
        where,
        [rows, before] + [x for s in weights for x in weights[s]],
        [
            jax.ShapeDtypeStruct(before.shape, BF16),
            jax.ShapeDtypeStruct((steps, groups, batch * WIDE, WIDE), BF16),
            jax.ShapeDtypeStruct((steps, batch, heads), F32),
        ],
    )


def backward_kernel(groups, where_ref, probs_ref, projected_ref, d_ref, out_ref):
    for n in range(probs_ref.shape[0]):
        backward_step(groups, n, probs_ref, projected_ref, d_ref, out_ref)


def backward_step(groups, n, probs_ref, projected_ref, d_ref, out_ref):
    low = low_lanes(HEAD_DIM)
    ones = ones_block(2)
    width_q = groups * GROUP
    width_k = groups * HEAD_DIM
    count = d_ref.shape[1]
    at = n * count
    spans = [slice((at + i) * PASSAGE_LEN, (at + i + 1) * PASSAGE_LEN) for i in range(count)]
    keys = [diagonals(projected_ref[r, width_q : width_q + width_k], scale) for r in spans]
    values = [diagonals(projected_ref[r, width_q + width_k :], 1.0) for r in spans]
    down = ((0,), (0,))
    d_keys = [[] for _ in spans]
    d_values = [[] for _ in spans]

    def fold(product):
        kept = jnp.where(low, product[:HEAD_DIM], product[HEAD_DIM:])
        return kept + pltpu.roll(kept, HEAD_DIM, 1)

    for g in range(groups):
        probs = probs_ref[n, g]
        d_rows = []
        for i in range(count):
            row = [
                d_ref[n, i : i + 1, g * GROUP + j * WIDE : g * GROUP + (j + 1) * WIDE]
                for j in range(2)
            ]
            d_rows.append(
                jnp.concatenate(
                    [jnp.broadcast_to(x, (HEAD_DIM, WIDE)) for x in row], 0
                ).astype(BF16)
            )
        d_probs = jnp.concatenate(
            [mm(d_rows[i], values[i][g], ((1,), (1,))) for i in range(count)], 0
        )
        probs_f = probs.astype(F32)
        product = probs_f * d_probs
        upper = product.astype(BF16)
        lower = (product - upper.astype(F32)).astype(BF16)
        inner = mm(jnp.concatenate([upper, lower], 1), ones)
        d_scores = (probs_f * (d_probs - inner)).astype(BF16)
        for i, r in enumerate(spans):
            block = slice(i * WIDE, (i + 1) * WIDE)
            d_query = mm(d_scores[block], keys[i][g]).astype(BF16)
            at = g * GROUP
            out_ref[r, at : at + WIDE] = d_query[:HEAD_DIM]
            out_ref[r, at + WIDE : at + GROUP] = d_query[HEAD_DIM:]
            d_keys[i].append(fold(mm(d_scores[block], stacked(projected_ref, r, g), down)) * scale)
            d_values[i].append(fold(mm(probs[block], d_rows[i], down)))
    for i, r in enumerate(spans):
        out_ref[r, width_q : width_q + width_k] = jnp.where(low, *d_keys[i]).astype(BF16)
        out_ref[r, width_q + width_k :] = jnp.where(low, *d_values[i]).astype(BF16)


def backward(where, probs, projected, d_attended, groups):
    steps = probs.shape[0]
    batch = probs.shape[2] // WIDE
    return local_call(
        functools.partial(backward_kernel, groups),
        "attend_back",
        3.4,
        where,
        [probs, projected, d_attended.reshape(steps, batch, groups * GROUP)],
        jax.ShapeDtypeStruct(projected.shape, BF16),
    )


def score_kernel(chips, where_ref, own_ref, sib_ref, own_far_ref, sib_far_ref, sum_ref, sib_sum_ref,
                 final_ref, ws_ref, prior_ref, prior_sib_ref, *refs):
    pieces, refs = refs[: 4 * chips], refs[4 * chips :]
    unit_ref, inverse_ref, score_ref, attn_ref, product_ref = refs
    chip, core = where_ref[0], where_ref[1]
    mine = jnp.concatenate([own_ref[...], sib_ref[...]], 0)
    other = jnp.concatenate([own_far_ref[...], sib_far_ref[...]], 0)
    sums = [ref[k] for ref in (sum_ref, sib_sum_ref) for k in range(ref.shape[0])]
    attn = jnp.concatenate(
        [jnp.where(core == 0, mine, other), jnp.where(core == 0, other, mine)], 1
    )
    count = attn.shape[0]
    upper = attn.astype(BF16)
    attn_ref[...] = upper
    both = jnp.concatenate([upper.astype(F32), attn - upper.astype(F32)], 0)
    product_ref[...] = both
    depth, part = pieces[0].shape
    out = [None] * 4
    for s in range(chips):
        start = pl.multiple_of((chip ^ s) * depth, depth)
        block = product_ref[:, pl.ds(start, depth)].astype(BF16)
        for k in range(4):
            x = mm(block, pieces[4 * s + k][...])
            out[k] = x if out[k] is None else out[k] + x
    out = [x[:count] + x[count:] for x in out]
    own, far = jnp.concatenate(out[:2], 1), jnp.concatenate(out[2:], 1)
    product = jnp.concatenate(
        [jnp.where(core == 0, own, far), jnp.where(core == 0, far, own)], 1
    )
    pooled = (jnp.concatenate(sums, 0) + product) * (1.0 / PASSAGE_LEN)
    inverse = lax.rsqrt(jnp.mean(pooled * pooled, -1, keepdims=True) + epsilon)
    unit = pooled * inverse
    score = jnp.sum(unit * (final_ref[...] * ws_ref[...]), -1, keepdims=True)
    unit_ref[...] = unit
    inverse_ref[...] = jnp.broadcast_to(inverse, inverse_ref.shape)
    lane = lax.broadcasted_iota(jnp.int32, score_ref.shape, 1)
    half = score_ref.shape[1] // 2
    prior = jnp.concatenate([prior_ref[...], prior_sib_ref[...]], 0)
    score_ref[...] = jnp.where(lane < half, score, 0.0) + prior


def score_pass(where, attn, sums, final_gain, w_score, priors, pieces):
    count, width = 2 * attn[0].shape[0], sums[0].shape[2]
    lanes = priors[0].shape[1]
    inner = 2 * attn[0].shape[1]
    vmem = pl.BlockSpec(memory_space=pltpu.VMEM)
    return pl.pallas_call(
        functools.partial(score_kernel, len(pieces) // 4),
        in_specs=[pl.BlockSpec(memory_space=pltpu.SMEM)] + [vmem] * (10 + len(pieces)),
        out_specs=[vmem] * 4,
        out_shape=[
            jax.ShapeDtypeStruct((count, width), F32),
            jax.ShapeDtypeStruct((count, lanes), F32),
            jax.ShapeDtypeStruct((count, lanes), F32),
            jax.ShapeDtypeStruct((count, inner), BF16),
        ],
        scratch_shapes=[pltpu.VMEM((2 * count, inner), F32)],
        compiler_params=pltpu.CompilerParams(vmem_limit_bytes=SMALL),
        cost_estimate=cost(2),
        name="pool_score",
    )(where, *attn, *sums, final_gain[None], w_score[None], *priors, *pieces)


def list_kernel(blocks, chips, passages, where_ref, place_ref, bounds_ref, unit_ref, inverse_ref,
                final_ref, ws_ref, *refs):
    scores = [ref[...] for ref in refs[:blocks]]
    pieces, refs = refs[blocks : blocks + 4 * chips], refs[blocks + 4 * chips :]
    d_att_ref, d_rows_ref, loss_ref, back_ref = refs
    chip, core = where_ref[0], where_ref[1]
    pair = 2 * passages
    lanes = bounds_ref.shape[1]
    lane = lax.broadcasted_iota(jnp.int32, bounds_ref.shape, 1)
    ends, reach = bounds_ref[...], 1
    while reach < lanes:
        ends = ends + jnp.where(lane >= reach, pltpu.roll(ends, reach, 1), 0)
        reach *= 2
    starts, ends = (ends - bounds_ref[...])[:1], ends[:1]
    row = lax.broadcasted_iota(jnp.int32, (pair, lanes), 0)
    near = jnp.where(row < passages, core * passages + row, (1 - core) * passages + row - passages)
    far = jnp.where(row < passages, (1 - core) * passages + row, core * passages + row - passages)
    members = []
    for j in range(blocks):
        place = place_ref[j] * pair + (near if j <= blocks // 2 else far)
        members.append((place >= starts) & (place < ends))
    high = scores[0].shape[1] // 2
    column = [jnp.broadcast_to(score[:, :1], (pair, lanes)) for score in scores]
    heavy = [jnp.broadcast_to(score[:, high : high + 1], (pair, lanes)) for score in scores]
    peak = functools.reduce(
        jnp.maximum,
        [jnp.max(jnp.where(m, s, -1e30), 0, keepdims=True) for m, s in zip(members, column)],
    )
    total = sum(
        jnp.sum(jnp.where(m, jnp.exp(jnp.where(m, s - peak, 0.0)), 0.0), 0, keepdims=True)
        for m, s in zip(members, column)
    )
    label_total = sum(
        jnp.sum(jnp.where(m, w, 0.0), 0, keepdims=True) for m, w in zip(members, heavy)
    )
    log_norm = peak + jnp.log(total)
    own = members[0]
    log_prob = column[0][:, :1] - jnp.sum(jnp.where(own, log_norm, 0.0), 1, keepdims=True)
    target = heavy[0][:, :1] / jnp.sum(jnp.where(own, label_total, 0.0), 1, keepdims=True)
    loss = -loss_scale * jnp.sum((target * log_prob)[:passages], 0, keepdims=True)
    d_score = loss_scale * (jnp.exp(log_prob) - target)
    unit = unit_ref[...]
    d_unit = d_score * (ws_ref[...] * final_ref[...])
    mean = jnp.mean(d_unit * unit, -1, keepdims=True)
    d_pooled = inverse_ref[:, :1] * (d_unit - unit * mean)
    depth, part = pieces[0].shape
    half = d_pooled.shape[1] // 2
    own = jnp.where(core == 0, d_pooled[:, :half], d_pooled[:, half:])
    far = jnp.where(core == 0, d_pooled[:, half:], d_pooled[:, :half])
    cut = [own[:, :part], own[:, part:], far[:, :part], far[:, part:]]
    cut = [(x * (1.0 / PASSAGE_LEN)).astype(BF16) for x in cut]
    for s in range(chips):
        back = sum(mm(cut[k], pieces[4 * s + k][...], ((1,), (1,))) for k in range(4))
        start = pl.multiple_of((chip ^ s) * depth, depth)
        back_ref[:, pl.ds(start, depth)] = back.astype(BF16).astype(F32)
    back = back_ref[...]
    half = back.shape[1] // 2
    d_att_ref[...] = jnp.where(core == 0, back[:, :half], back[:, half:])
    loss_ref[...] = jnp.broadcast_to(loss, loss_ref.shape)
    d_rows_ref[:, :part] = cut[0]
    d_rows_ref[:, part:] = cut[1]


def list_pass(where, places, bounds, unit, inverse, final_gain, w_score, scores, pieces,
              passages):
    count, width = unit.shape
    chips = len(pieces) // 4
    inner = chips * pieces[0].shape[0]
    vmem = pl.BlockSpec(memory_space=pltpu.VMEM)
    smem = pl.BlockSpec(memory_space=pltpu.SMEM)
    return pl.pallas_call(
        functools.partial(list_kernel, len(scores), chips, passages),
        in_specs=[smem] * 2 + [vmem] * (5 + len(scores) + len(pieces)),
        out_specs=[vmem] * 3,
        out_shape=[
            jax.ShapeDtypeStruct((count, inner // 2), F32),
            jax.ShapeDtypeStruct((count, width // 2), BF16),
            jax.ShapeDtypeStruct((8, 128), F32),
        ],
        scratch_shapes=[pltpu.VMEM((count, inner), F32)],
        compiler_params=pltpu.CompilerParams(vmem_limit_bytes=SMALL),
        cost_estimate=cost(2.5),
        name="list_grad",
    )(where, places, bounds, unit, inverse, final_gain[None], w_score[None], *scores,
      *pieces)


def payload_kernel(passages, where_ref, attn_ref, d_rows_ref, loss_ref, out_ref):
    core = where_ref[1]
    attn = attn_ref[...].astype(F32)
    half = attn.shape[1] // 2
    columns = [jnp.where(core == 0, attn[:, :half], attn[:, half:]), d_rows_ref[...].astype(F32)]
    rest = jnp.broadcast_to(loss_ref[:1], (attn.shape[0], 128))
    for _ in range(3):
        columns.append(rest.astype(BF16).astype(F32))
        rest = rest - columns[-1]
    columns = jnp.concatenate(columns, 1)
    turned = jnp.concatenate([columns[passages:], columns[:passages]], 0)
    out_ref[...] = jnp.where(core == 0, columns, turned).astype(BF16)


def payload_pass(where, attn, d_rows, loss):
    count = attn.shape[0]
    vmem = pl.BlockSpec(memory_space=pltpu.VMEM)
    return pl.pallas_call(
        functools.partial(payload_kernel, count // 2),
        in_specs=[pl.BlockSpec(memory_space=pltpu.SMEM)] + [vmem] * 3,
        out_specs=vmem,
        out_shape=jax.ShapeDtypeStruct(
            (count, attn.shape[1] // 2 + d_rows.shape[1] + 3 * 128), BF16
        ),
        compiler_params=pltpu.CompilerParams(vmem_limit_bytes=SMALL),
        cost_estimate=cost(1),
        name="out_payload",
    )(where, attn, d_rows, loss)


EXTRA = 16


def out_kernel(chips, where_ref, left_ref, *refs):
    near, far, out_ref = refs[:chips], refs[chips], refs[chips + 1]
    core = where_ref[1]
    cols = out_ref.shape[1] // 2
    own_rows = out_ref.shape[0] - EXTRA
    lead = far.shape[1] - 3 * 128 - cols
    mine = jnp.concatenate([ref[...] for ref in near], 0)
    other = far[...]
    down = ((0,), (0,))
    products = [mm(left_ref[...], x[:, lead : lead + cols], down) for x in (mine, other)]
    out_ref[:own_rows, :cols] = jnp.where(core == 0, *products).astype(BF16)
    out_ref[:own_rows, cols:] = jnp.where(core == 0, *products[::-1]).astype(BF16)

    count = mine.shape[0] // chips
    losses = []
    for s in range(chips):
        total = 0.0
        for x in (mine, other):
            row = x[s * count : s * count + EXTRA, lead + cols :].astype(F32)
            total = total + (row[:, :128] + row[:, 128:256] + row[:, 256:])
        losses.append(total)
    while len(losses) > 1:
        losses = [a + b for a, b in zip(losses[0::2], losses[1::2])]
    rest = losses[0]
    parts = []
    for _ in range(3):
        parts.append(rest.astype(BF16).astype(F32))
        rest = rest - parts[-1]
    row = jnp.concatenate(parts + [jnp.zeros_like(rest)], 1).astype(BF16)
    out_ref[own_rows:] = jnp.concatenate([row] * (2 * cols // row.shape[1]), 1)


def out_pass(where, left, near, far, cols):
    vmem = pl.BlockSpec(memory_space=pltpu.VMEM)
    return pl.pallas_call(
        functools.partial(out_kernel, len(near)),
        in_specs=[pl.BlockSpec(memory_space=pltpu.SMEM)] + [vmem] * (2 + len(near)),
        out_specs=vmem,
        out_shape=jax.ShapeDtypeStruct((left.shape[1] + EXTRA, 2 * cols), BF16),
        compiler_params=pltpu.CompilerParams(vmem_limit_bytes=SMALL),
        cost_estimate=cost(1),
        name="out_rows",
    )(where, left, *near, far)


def grad_kernel(blocks, where_ref, own_ref, sib_ref, d_own_ref, d_sib_ref, *out):
    depth, part = out[0].shape
    tile = min(depth, 256)
    down = ((0,), (0,))
    for n, s in enumerate(blocks):
        for i in range(depth // tile):
            start = pl.multiple_of((where_ref[0] ^ s) * depth + i * tile, tile)
            cols = pl.ds(start, tile)
            total = mm(own_ref[:, cols], d_own_ref[...], down)
            total = (total + mm(sib_ref[:, cols], d_sib_ref[...], down)).astype(BF16)
            out[2 * n][i * tile : (i + 1) * tile] = total[:, :part]
            out[2 * n + 1][i * tile : (i + 1) * tile] = total[:, part:]


def grad_blocks(where, blocks, own, sib, d_own, d_sib, depth):
    part = d_own.shape[1] // 2
    return local_call(
        functools.partial(grad_kernel, tuple(blocks)),
        "grad_rows",
        2.5 * len(blocks),
        where,
        [own, sib, d_own, d_sib],
        [jax.ShapeDtypeStruct((depth, part), BF16)] * (2 * len(blocks)),
    )


def pick_kernel(starts, sizes, where_ref, mine_ref, come_ref, a_ref, b_ref):
    core = where_ref[1]
    mine, come = mine_ref[...].astype(F32), come_ref[...].astype(F32)
    rows = mine.shape[0]
    halves = []
    for h in range(2):
        spans = [slice(a + h * n, a + (h + 1) * n) for a, n in zip(starts, sizes)]
        halves.append([jnp.concatenate([x[:, t] for t in spans], 1) for x in (mine, come)])
    first = jnp.where(core == 0, halves[0][0], halves[1][1]).astype(BF16)
    second = jnp.where(core == 0, halves[0][1], halves[1][0]).astype(BF16)
    part = a_ref.shape[1]
    a_ref[:rows], b_ref[:rows] = first[:, :part], first[:, part:]
    a_ref[rows:], b_ref[rows:] = second[:, :part], second[:, part:]


def pick(where, mine, come, starts, sizes):
    rows = mine.shape[0]
    vmem = pl.BlockSpec(memory_space=pltpu.VMEM)
    return pl.pallas_call(
        functools.partial(pick_kernel, starts, sizes),
        in_specs=[pl.BlockSpec(memory_space=pltpu.SMEM), vmem, vmem],
        out_specs=[vmem] * 2,
        out_shape=[jax.ShapeDtypeStruct((2 * rows, sum(sizes) // 2), BF16)] * 2,
        compiler_params=pltpu.CompilerParams(vmem_limit_bytes=SMALL),
        cost_estimate=cost(1),
        name="pick_columns",
    )(where, mine, come)


def solution(mesh):
    n_list, n_fsdp = mesh.shape["list"], mesh.shape["fsdp"]
    bits = [1 << k for k in range(1, n_fsdp.bit_length() - 1)]
    pairs = n_list * n_fsdp // 2

    def across(value, distance):
        return lax.ppermute(value, "fsdp", [(i, i ^ distance) for i in range(n_fsdp)])

    def along(value, distance):
        return lax.ppermute(value, "list", [(i, i ^ distance) for i in range(n_list)])

    def partner(kind, pair):
        return (
            pair ^ 1,
            ((pair + 1) ^ 1) - 1,
            pair ^ 2,
            ((pair + 2) ^ 2) - 2,
        )[kind]

    def neighbour(value, kind):
        moves = []
        for pair in range(pairs):
            for core in (0, 1):
                other = partner(kind + core, pair)
                if 0 <= other < pairs:
                    moves.append((2 * pair + core, 2 * other + core))
        return lax.ppermute(value, ("list", "fsdp"), moves)

    def after(value, *others):
        return lax.optimization_barrier((value, others))[0]

    def gathered(value, order, near=(), far=()):
        have = {0: value}
        for bit in order:
            first = [part for s, part in have.items() if s]
            ready = dict(have)
            if first:
                ready = {s: after(part, far if s else near, first) for s, part in have.items()}
            have.update({s ^ (bit >> 1): across(part, bit) for s, part in ready.items()})
        return have

    def joined(parts, come, bit):
        return {
            s: (parts[s].astype(F32) + come[s].astype(F32)).astype(BF16)
            for s in parts
            if not s & (bit >> 1)
        }

    def sent(parts, bit):
        flag = bit >> 1
        return {s ^ flag: across(parts[s], bit) for s in sorted(parts)[::-1] if s & flag}

    def local(hidden, norm_gain, w_qkv, w_out, final_gain, w_score, prior, labels, lengths):
        passages, _, width = hidden.shape
        assert 4 * passages >= LONGEST - 1
        groups = KV_HEADS // 2
        width_q, width_k = groups * GROUP, groups * HEAD_DIM
        index = lax.axis_index("fsdp")
        core = index % 2
        chip = index // 2
        where = jnp.stack([chip, core]).astype(jnp.int32)
        first_core = core == 0

        def ordered(mine, other, axis):
            return jnp.where(
                first_core,
                jnp.concatenate([mine, other], axis),
                jnp.concatenate([other, mine], axis),
            )

        starts = (0, 2 * width_q, 2 * (width_q + width_k))
        sizes = (width_q, width_k, width_k)
        come = across(w_qkv, 1)
        pair_a, pair_b = pick(where, w_qkv, come, starts, sizes)
        w_out = after(w_out, come)
        out_come = across(w_out, 1)
        hidden_sib = across(after(hidden, come), 1)

        normal, sums, before_own = norm(where, hidden, norm_gain, (pair_a, pair_b))
        prior, labels, lengths, out_come = after((prior, labels, lengths, out_come), before_own)
        lanes = -(-lengths.shape[0] // 128) * 128
        label_weight = jnp.exp(labels.astype(F32))
        small = jnp.concatenate(
            [jnp.broadcast_to(x[:, None], (passages, 64)) for x in (prior, label_weight)], 1
        )
        small_sib = across(small, 1)
        pair = lax.axis_index("list") * (n_fsdp // 2) + chip
        places = [pair] + [
            jnp.where(first_core == near, partner(2 * kind, pair), partner(2 * kind + 1, pair))
            for near in (True, False)
            for kind in range(2)
        ]
        places = jnp.stack(places).astype(jnp.int32)
        bounds = jnp.broadcast_to(
            jnp.pad(lengths, (0, lanes - lengths.shape[0]))[None], (8, lanes)
        )

        cols = w_out.shape[1] // 2
        both = ordered(w_out, out_come, 0)
        out_pair = jnp.where(first_core, both[:, :cols], both[:, cols:])
        normal_sib, sums_sib, before_sib = norm(
            where,
            after(hidden_sib, before_own, places, bounds, small_sib, out_pair),
            norm_gain,
            (pair_a, pair_b),
        )
        part_a = gathered(pair_a, bits, far=before_own)
        part_b = gathered(pair_b, bits[::-1], far=before_own)
        chips = n_fsdp // 2
        last = max(bin(s).count("1") for s in range(chips))
        weights = [{}, {}, {}]
        for s in range(chips):
            ones = bin(s).count("1")
            weights[2 if ones == last else 1 if ones else 0][s] = (part_a[s], part_b[s])

        out_pair = after(out_pair, weights[1], before_sib)
        if weights[1]:
            normal_first = after(normal, before_sib)
            before_own = partial_project(where, normal_first, weights[1], before_own)
            before_sib = partial_project(
                where, after(normal_sib, before_own), weights[1], before_sib
            )
        before_own, before_sib, weights[2] = after(
            (before_own, before_sib, weights[2]), before_sib
        )
        proj_sib, probs_sib, attn_sib = forward(where, normal_sib, weights[2], groups, before_sib)
        attn_sib = attn_sib.reshape(passages, -1)
        attn_sib_other = across(attn_sib, 1)
        normal_last = after(normal, probs_sib)
        proj_own, probs_own, attn_own = forward(where, normal_last, weights[2], groups, before_own)
        attn_own = attn_own.reshape(passages, -1)
        attn_own_other = across(attn_own, 1)
        out_a = gathered(out_pair[:, : cols // 2], bits, before_sib, before_sib)
        out_b = gathered(out_pair[:, cols // 2 :], bits[::-1], before_sib, before_sib)
        pieces = []
        for s in range(chips):
            pieces += [out_a[s], out_b[s]]
            gate = probs_own if bin(s).count("1") == last else ()
            pieces += [across(after(x, gate), 1) for x in (out_a[s], out_b[s])]
        unit, inverse, score, attn = score_pass(
            where,
            (attn_own, attn_sib, attn_sib_other, attn_own_other),
            (sums, sums_sib),
            final_gain,
            w_score,
            (small, small_sib),
            pieces,
        )
        near = [neighbour(score, kind) for kind in (0, 2)]
        scores = [score] + near + [across(x, 1) for x in near]
        d_attended, d_rows, loss_part = list_pass(
            where, places, bounds, unit, inverse, final_gain, w_score, scores, pieces, passages
        )

        d_own = backward(where, probs_own, proj_own, d_attended[:passages], groups)
        payload = payload_pass(where, attn, d_rows, loss_part)
        d_sib = backward(
            where, after(probs_sib, d_own), proj_sib, d_attended[passages:], groups
        )
        depth = pair_a.shape[0]
        flag_a, flag_b = bits[0] >> 1, bits[-1] >> 1
        lead = [s for s in range(chips) if s & flag_a and s & flag_b]
        rest = [s for s in range(1, chips) if s not in lead]

        def grads(blocks, *gate):
            out = grad_blocks(where, blocks, normal, normal_sib, d_own, after(d_sib, gate), depth)
            return dict(zip(blocks, out[0::2])), dict(zip(blocks, out[1::2]))

        parts_a, parts_b = grads(lead)
        first_a = {s ^ flag_a: across(parts_a[s], bits[0]) for s in lead}
        first_b = {s ^ flag_b: across(parts_b[s], bits[-1]) for s in lead}
        plane = gathered(payload, bits)
        plane = [plane[s] for s in range(chips)]
        more_a, more_b = grads(rest, parts_a, plane)
        far = across(jnp.concatenate(plane, 0), 1)
        own_a, own_b = grads([0], more_a, first_a, first_b, far)
        parts_a.update(more_a)
        parts_b.update(more_b)
        parts_a.update(own_a)
        parts_b.update(own_b)
        for s in rest:
            if s & flag_a:
                first_a[s ^ flag_a] = across(parts_a[s], bits[0])
            if s & flag_b:
                first_b[s ^ flag_b] = across(parts_b[s], bits[-1])
        left_a, left_b = joined(parts_a, first_a, bits[0]), joined(parts_b, first_b, bits[-1])
        for bit_a, bit_b in zip(bits[1:], bits[::-1][1:]):
            left_a = joined(left_a, sent(left_a, bit_a), bit_a)
            left_b = joined(left_b, sent(left_b, bit_b), bit_b)
        sum_a, sum_b = left_a[0], left_b[0]
        place = lax.axis_index("list")
        inner = 2 * width_q
        left = ordered(
            jnp.concatenate([x[:, :width_q] for x in plane], 0), far[:, :width_q], 1
        )
        own_rows = inner // n_fsdp
        left = lax.dynamic_slice_in_dim(left, index * own_rows, own_rows, 1)
        rows = out_pass(where, left, plane, far, cols)
        blocks = rows.shape[1] // n_list
        block = lambda which: lax.dynamic_slice_in_dim(rows, which * blocks, blocks, 1)
        come_out = [block(place)]
        come_out += [along(block(place ^ distance), distance) for distance in range(1, n_list)]
        chip_sum = after(jnp.concatenate([sum_a, sum_b], 1), come_out)
        upper, lower = chip_sum[: depth // 2], chip_sum[depth // 2 :]
        keep = jnp.where(first_core, upper, lower)
        come = across(jnp.where(first_core, lower, upper), 1)
        columns = []
        at = 0
        for n in sizes:
            columns.append(ordered(keep[:, at : at + n], come[:, at : at + n], 1))
            at += n
        rows_sum = jnp.concatenate(columns, 1)
        place = lax.axis_index("list")

        def list_scatter(value):
            n = value.shape[1] // n_list
            block = lambda which: lax.dynamic_slice_in_dim(value, which * n, n, 1)
            total = block(place).astype(F32)
            for distance in range(1, n_list):
                total = total + along(block(place ^ distance).astype(BF16), distance).astype(F32)
            return total

        grad_qkv = list_scatter(rows_sum)

        grad_out = sum(x[:own_rows].astype(F32) for x in come_out)
        losses = []
        for x in come_out:
            x = x[own_rows].astype(F32)
            losses.append(x[0] + x[128] + x[256])
        while len(losses) > 1:
            losses = [a + b for a, b in zip(losses[0::2], losses[1::2])]
        return (losses[0], grad_qkv, grad_out)

    placed = (
        P(("list", "fsdp"), None, None),
        P(),
        P("fsdp", None),
        P("fsdp", None),
        P(),
        P(),
        P(("list", "fsdp")),
        P(("list", "fsdp")),
        P(),
    )
    return jax.shard_map(
        local,
        mesh=mesh,
        in_specs=placed,
        out_specs=(P(), P("fsdp", "list"), P("fsdp", "list")),
        check_vma=False,
    )
```

```python
import functools

import jax
import jax.numpy as jnp
from jax import lax
from jax.experimental import pallas as pl
from jax.experimental.pallas import tpu as pltpu
from jax.sharding import PartitionSpec as P

HEADS = 16
KV_HEADS = 4
HEAD_DIM = 64
PASSAGE_LEN = 64
LONGEST = 48
RATIO = HEADS // KV_HEADS
GROUP = RATIO * HEAD_DIM

epsilon = 1e-05
loss_scale = 64.0
scale = HEAD_DIM ** (-0.5)
VMEM = 10 * 1024 * 1024
SMALL = 6 * 1024 * 1024


def cost(micros):
    return pl.CostEstimate(flops=int(micros * 5e8), bytes_accessed=int(micros * 3.5e6), transcendentals=0)

BF16 = jnp.bfloat16
F32 = jnp.float32


def params(grid=1):
    return pltpu.CompilerParams(
        vmem_limit_bytes=VMEM, dimension_semantics=("arbitrary",) * grid
    )


def held(space, *values):
    return [pltpu.with_memory_space_constraint(x, space) for x in values]


def mm(a, b, dims=((1,), (0,))):
    return lax.dot_general(a, b, (dims, ((), ())), preferred_element_type=F32)


def norm_kernel(where_ref, hidden_ref, gain_ref, a_ref, b_ref, normal_ref, sum_ref, out_ref):
    values = hidden_ref[...].astype(F32)
    mean_square = jnp.mean(values * values, -1, keepdims=True)
    out = values * lax.rsqrt(mean_square + epsilon) * gain_ref[...][None]
    normal_ref[...] = out.reshape(normal_ref.shape).astype(BF16)
    sum_ref[0] = jnp.sum(values, 1)
    depth, part = a_ref.shape
    start = pl.multiple_of(where_ref[0] * depth, depth)
    block = normal_ref[:, pl.ds(start, depth)]
    out_ref[:, :part] = mm(block, a_ref[...])
    out_ref[:, part:] = mm(block, b_ref[...])


def norm(where, hidden, gain, weights):
    passages, length, width = hidden.shape
    depth, part = weights[0].shape
    step = 4 if passages % 4 == 0 else 1
    steps = passages // step
    whole = lambda i, w: (0, 0)
    normal, sums, product = pl.pallas_call(
        norm_kernel,
        grid_spec=pltpu.PrefetchScalarGridSpec(
            num_scalar_prefetch=1,
            grid=(steps,),
            in_specs=[
                pl.BlockSpec((step, length, width), lambda i, w: (i, 0, 0)),
                pl.BlockSpec((1, width), whole),
                pl.BlockSpec((depth, part), whole),
                pl.BlockSpec((depth, part), whole),
            ],
            out_specs=[
                pl.BlockSpec((step * length, width), lambda i, w: (i, 0)),
                pl.BlockSpec((1, step, width), lambda i, w: (i, 0, 0)),
                pl.BlockSpec((step * length, 2 * part), lambda i, w: (i, 0)),
            ],
        ),
        out_shape=[
            pltpu.VMEM((passages * length, width), BF16),
            jax.ShapeDtypeStruct((steps, step, width), F32),
            pltpu.VMEM((passages * length, 2 * part), F32),
        ],
        compiler_params=params(),
        cost_estimate=cost(7),
        name="norm_project",
    )(where, *held(pltpu.HBM, hidden), gain[None], *weights)
    return normal, sums, product


WIDE = 2 * HEAD_DIM
BATCH = 8


def low_lanes(rows):
    return lax.broadcasted_iota(jnp.int32, (rows, WIDE), 1) < HEAD_DIM


def ones_block(repeat):
    row = lax.broadcasted_iota(jnp.int32, (repeat * WIDE, WIDE), 0) // HEAD_DIM % 2
    col = lax.broadcasted_iota(jnp.int32, (repeat * WIDE, WIDE), 1) // HEAD_DIM
    return jnp.where(row == col, 1.0, 0.0).astype(BF16)


def diagonals(pair, factor):
    low = low_lanes(HEAD_DIM)
    wide = pair.astype(F32) * factor
    turned = pltpu.roll(wide, HEAD_DIM, 1)
    out = []
    for first, second in ((wide, turned), (turned, wide)):
        block = [jnp.where(low, first, 0.0), jnp.where(low, 0.0, second)]
        out.append(jnp.concatenate(block, 0).astype(BF16))
    return out


def segment_max(scores):
    low = low_lanes(scores.shape[0])
    first = jnp.max(jnp.where(low, scores, -jnp.inf), 1, keepdims=True)
    second = jnp.max(jnp.where(low, -jnp.inf, scores), 1, keepdims=True)
    return jnp.where(low, first, second)


def stacked(ref, rows, g):
    at = g * GROUP
    return jnp.concatenate([ref[rows, at : at + WIDE], ref[rows, at + WIDE : at + GROUP]], 0)


def product_of(chip, rows_ref, rows, shifts, weights):
    depth = weights[0].shape[0]
    out = []
    for part in range(2):
        total = None
        for k, s in enumerate(shifts):
            start = pl.multiple_of((chip ^ s) * depth, depth)
            x = mm(rows_ref[rows, pl.ds(start, depth)], weights[2 * k + part][...])
            total = x if total is None else total + x
        out.append(total)
    return out


def partial_kernel(shifts, step, where_ref, rows_ref, before_ref, *refs):
    weights, out_ref = refs[:-1], refs[-1]
    part = weights[0].shape[1]
    for i in range(rows_ref.shape[0] // step):
        rows = slice(i * step, (i + 1) * step)
        a, b = product_of(where_ref[0], rows_ref, rows, shifts, weights)
        out_ref[rows, :part] = a + before_ref[rows, :part]
        out_ref[rows, part:] = b + before_ref[rows, part:]


def forward_kernel(shifts, groups, batch, where_ref, rows_ref, before_ref, *refs):
    weights, refs = refs[: 2 * len(shifts)], refs[2 * len(shifts) :]
    projected_ref, probs_ref, sum_ref = refs
    part = weights[0].shape[1]
    ones = ones_block(1)
    width_q = groups * GROUP
    width_k = groups * HEAD_DIM
    step = batch * PASSAGE_LEN
    for n in range(rows_ref.shape[0] // step):
        rows = slice(n * step, (n + 1) * step)
        a, b = product_of(where_ref[0], rows_ref, rows, shifts, weights)
        projected_ref[rows, :part] = (a + before_ref[rows, :part]).astype(BF16)
        projected_ref[rows, part:] = (b + before_ref[rows, part:]).astype(BF16)
        spans = [
            slice(n * step + i * PASSAGE_LEN, n * step + (i + 1) * PASSAGE_LEN)
            for i in range(batch)
        ]
        keys = [diagonals(projected_ref[r, width_q : width_q + width_k], scale) for r in spans]
        values = [diagonals(projected_ref[r, width_q + width_k :], 1.0) for r in spans]
        for g in range(groups):
            scores = [
                mm(stacked(projected_ref, r, g), keys[i][g], ((1,), (1,)))
                for i, r in enumerate(spans)
            ]
            scores = jnp.concatenate(scores, 0)
            expo = jnp.exp(scores - segment_max(scores))
            total = mm(expo.astype(BF16), ones)
            probs = (expo / total).astype(BF16)
            probs_ref[n, g] = probs
            for i in range(batch):
                attended = mm(probs[i * WIDE : (i + 1) * WIDE], values[i][g])
                attended = attended.astype(BF16).astype(F32)
                for j in range(2):
                    at = g * GROUP + j * WIDE
                    sum_ref[n, i : i + 1, at : at + WIDE] = jnp.sum(
                        attended[j * HEAD_DIM : (j + 1) * HEAD_DIM], 0, keepdims=True
                    )


def row_step(total, batch):
    batch = batch if total % (batch * PASSAGE_LEN) == 0 else 1
    return batch, batch * PASSAGE_LEN


def local_call(kernel, name, micros, where, operands, out_shape):
    vmem = pl.BlockSpec(memory_space=pltpu.VMEM)
    return pl.pallas_call(
        kernel,
        in_specs=[pl.BlockSpec(memory_space=pltpu.SMEM)] + [vmem] * len(operands),
        out_specs=jax.tree.map(lambda _: vmem, out_shape),
        out_shape=out_shape,
        compiler_params=pltpu.CompilerParams(vmem_limit_bytes=VMEM),
        cost_estimate=cost(micros),
        name=name,
    )(where, *operands)


def partial_project(where, rows, weights, before):
    _, step = row_step(rows.shape[0], BATCH)
    return local_call(
        functools.partial(partial_kernel, tuple(weights), step),
        "project_more",
        4.5,
        where,
        [rows, before] + [x for s in weights for x in weights[s]],
        jax.ShapeDtypeStruct(before.shape, F32),
    )


def forward(where, rows, weights, groups, before):
    total = rows.shape[0]
    batch, step = row_step(total, BATCH)
    steps = total // step
    heads = groups * GROUP
    return local_call(
        functools.partial(forward_kernel, tuple(weights), groups, batch),
        "project_attend",
        6.5,
        where,
        [rows, before] + [x for s in weights for x in weights[s]],
        [
            jax.ShapeDtypeStruct(before.shape, BF16),
            jax.ShapeDtypeStruct((steps, groups, batch * WIDE, WIDE), BF16),
            jax.ShapeDtypeStruct((steps, batch, heads), F32),
        ],
    )


def backward_kernel(groups, where_ref, probs_ref, projected_ref, d_ref, out_ref):
    for n in range(probs_ref.shape[0]):
        backward_step(groups, n, probs_ref, projected_ref, d_ref, out_ref)


def backward_step(groups, n, probs_ref, projected_ref, d_ref, out_ref):
    low = low_lanes(HEAD_DIM)
    ones = ones_block(2)
    width_q = groups * GROUP
    width_k = groups * HEAD_DIM
    count = d_ref.shape[1]
    at = n * count
    spans = [slice((at + i) * PASSAGE_LEN, (at + i + 1) * PASSAGE_LEN) for i in range(count)]
    keys = [diagonals(projected_ref[r, width_q : width_q + width_k], scale) for r in spans]
    values = [diagonals(projected_ref[r, width_q + width_k :], 1.0) for r in spans]
    down = ((0,), (0,))
    d_keys = [[] for _ in spans]
    d_values = [[] for _ in spans]

    def fold(product):
        kept = jnp.where(low, product[:HEAD_DIM], product[HEAD_DIM:])
        return kept + pltpu.roll(kept, HEAD_DIM, 1)

    for g in range(groups):
        probs = probs_ref[n, g]
        d_rows = []
        for i in range(count):
            row = [
                d_ref[n, i : i + 1, g * GROUP + j * WIDE : g * GROUP + (j + 1) * WIDE]
                for j in range(2)
            ]
            d_rows.append(
                jnp.concatenate(
                    [jnp.broadcast_to(x, (HEAD_DIM, WIDE)) for x in row], 0
                ).astype(BF16)
            )
        d_probs = jnp.concatenate(
            [mm(d_rows[i], values[i][g], ((1,), (1,))) for i in range(count)], 0
        )
        probs_f = probs.astype(F32)
        product = probs_f * d_probs
        upper = product.astype(BF16)
        lower = (product - upper.astype(F32)).astype(BF16)
        inner = mm(jnp.concatenate([upper, lower], 1), ones)
        d_scores = (probs_f * (d_probs - inner)).astype(BF16)
        for i, r in enumerate(spans):
            block = slice(i * WIDE, (i + 1) * WIDE)
            d_query = mm(d_scores[block], keys[i][g]).astype(BF16)
            at = g * GROUP
            out_ref[r, at : at + WIDE] = d_query[:HEAD_DIM]
            out_ref[r, at + WIDE : at + GROUP] = d_query[HEAD_DIM:]
            d_keys[i].append(fold(mm(d_scores[block], stacked(projected_ref, r, g), down)) * scale)
            d_values[i].append(fold(mm(probs[block], d_rows[i], down)))
    for i, r in enumerate(spans):
        out_ref[r, width_q : width_q + width_k] = jnp.where(low, *d_keys[i]).astype(BF16)
        out_ref[r, width_q + width_k :] = jnp.where(low, *d_values[i]).astype(BF16)


def backward(where, probs, projected, d_attended, groups):
    steps = probs.shape[0]
    batch = probs.shape[2] // WIDE
    return local_call(
        functools.partial(backward_kernel, groups),
        "attend_back",
        3.4,
        where,
        [probs, projected, d_attended.reshape(steps, batch, groups * GROUP)],
        jax.ShapeDtypeStruct(projected.shape, BF16),
    )


def score_kernel(chips, where_ref, own_ref, sib_ref, own_far_ref, sib_far_ref, sum_ref, sib_sum_ref,
                 final_ref, ws_ref, prior_ref, prior_sib_ref, *refs):
    pieces, refs = refs[: 4 * chips], refs[4 * chips :]
    unit_ref, inverse_ref, score_ref, attn_ref, product_ref = refs
    chip, core = where_ref[0], where_ref[1]
    mine = jnp.concatenate([own_ref[...], sib_ref[...]], 0)
    other = jnp.concatenate([own_far_ref[...], sib_far_ref[...]], 0)
    sums = [ref[k] for ref in (sum_ref, sib_sum_ref) for k in range(ref.shape[0])]
    attn = jnp.concatenate(
        [jnp.where(core == 0, mine, other), jnp.where(core == 0, other, mine)], 1
    )
    count = attn.shape[0]
    upper = attn.astype(BF16)
    attn_ref[...] = upper
    both = jnp.concatenate([upper.astype(F32), attn - upper.astype(F32)], 0)
    product_ref[...] = both
    depth, part = pieces[0].shape
    out = [None] * 4
    for s in range(chips):
        start = pl.multiple_of((chip ^ s) * depth, depth)
        block = product_ref[:, pl.ds(start, depth)].astype(BF16)
        for k in range(4):
            x = mm(block, pieces[4 * s + k][...])
            out[k] = x if out[k] is None else out[k] + x
    out = [x[:count] + x[count:] for x in out]
    own, far = jnp.concatenate(out[:2], 1), jnp.concatenate(out[2:], 1)
    product = jnp.concatenate(
        [jnp.where(core == 0, own, far), jnp.where(core == 0, far, own)], 1
    )
    pooled = (jnp.concatenate(sums, 0) + product) * (1.0 / PASSAGE_LEN)
    inverse = lax.rsqrt(jnp.mean(pooled * pooled, -1, keepdims=True) + epsilon)
    unit = pooled * inverse
    score = jnp.sum(unit * (final_ref[...] * ws_ref[...]), -1, keepdims=True)
    unit_ref[...] = unit
    inverse_ref[...] = jnp.broadcast_to(inverse, inverse_ref.shape)
    lane = lax.broadcasted_iota(jnp.int32, score_ref.shape, 1)
    half = score_ref.shape[1] // 2
    prior = jnp.concatenate([prior_ref[...], prior_sib_ref[...]], 0)
    score_ref[...] = jnp.where(lane < half, score, 0.0) + prior


def score_pass(where, attn, sums, final_gain, w_score, priors, pieces):
    count, width = 2 * attn[0].shape[0], sums[0].shape[2]
    lanes = priors[0].shape[1]
    inner = 2 * attn[0].shape[1]
    vmem = pl.BlockSpec(memory_space=pltpu.VMEM)
    return pl.pallas_call(
        functools.partial(score_kernel, len(pieces) // 4),
        in_specs=[pl.BlockSpec(memory_space=pltpu.SMEM)] + [vmem] * (10 + len(pieces)),
        out_specs=[vmem] * 4,
        out_shape=[
            jax.ShapeDtypeStruct((count, width), F32),
            jax.ShapeDtypeStruct((count, lanes), F32),
            jax.ShapeDtypeStruct((count, lanes), F32),
            jax.ShapeDtypeStruct((count, inner), BF16),
        ],
        scratch_shapes=[pltpu.VMEM((2 * count, inner), F32)],
        compiler_params=pltpu.CompilerParams(vmem_limit_bytes=SMALL),
        cost_estimate=cost(2),
        name="pool_score",
    )(where, *attn, *sums, final_gain[None], w_score[None], *priors, *pieces)


def list_kernel(blocks, chips, passages, where_ref, place_ref, bounds_ref, unit_ref, inverse_ref,
                final_ref, ws_ref, *refs):
    scores = [ref[...] for ref in refs[:blocks]]
    pieces, refs = refs[blocks : blocks + 4 * chips], refs[blocks + 4 * chips :]
    d_att_ref, d_rows_ref, loss_ref, back_ref = refs
    chip, core = where_ref[0], where_ref[1]
    pair = 2 * passages
    lanes = bounds_ref.shape[1]
    lane = lax.broadcasted_iota(jnp.int32, bounds_ref.shape, 1)
    ends, reach = bounds_ref[...], 1
    while reach < lanes:
        ends = ends + jnp.where(lane >= reach, pltpu.roll(ends, reach, 1), 0)
        reach *= 2
    starts, ends = (ends - bounds_ref[...])[:1], ends[:1]
    row = lax.broadcasted_iota(jnp.int32, (pair, lanes), 0)
    near = jnp.where(row < passages, core * passages + row, (1 - core) * passages + row - passages)
    far = jnp.where(row < passages, (1 - core) * passages + row, core * passages + row - passages)
    members = []
    for j in range(blocks):
        place = place_ref[j] * pair + (near if j <= blocks // 2 else far)
        members.append((place >= starts) & (place < ends))
    high = scores[0].shape[1] // 2
    column = [jnp.broadcast_to(score[:, :1], (pair, lanes)) for score in scores]
    heavy = [jnp.broadcast_to(score[:, high : high + 1], (pair, lanes)) for score in scores]
    peak = functools.reduce(
        jnp.maximum,
        [jnp.max(jnp.where(m, s, -1e30), 0, keepdims=True) for m, s in zip(members, column)],
    )
    total = sum(
        jnp.sum(jnp.where(m, jnp.exp(jnp.where(m, s - peak, 0.0)), 0.0), 0, keepdims=True)
        for m, s in zip(members, column)
    )
    label_total = sum(
        jnp.sum(jnp.where(m, w, 0.0), 0, keepdims=True) for m, w in zip(members, heavy)
    )
    log_norm = peak + jnp.log(total)
    own = members[0]
    log_prob = column[0][:, :1] - jnp.sum(jnp.where(own, log_norm, 0.0), 1, keepdims=True)
    target = heavy[0][:, :1] / jnp.sum(jnp.where(own, label_total, 0.0), 1, keepdims=True)
    loss = -loss_scale * jnp.sum((target * log_prob)[:passages], 0, keepdims=True)
    d_score = loss_scale * (jnp.exp(log_prob) - target)
    unit = unit_ref[...]
    d_unit = d_score * (ws_ref[...] * final_ref[...])
    mean = jnp.mean(d_unit * unit, -1, keepdims=True)
    d_pooled = inverse_ref[:, :1] * (d_unit - unit * mean)
    depth, part = pieces[0].shape
    half = d_pooled.shape[1] // 2
    own = jnp.where(core == 0, d_pooled[:, :half], d_pooled[:, half:])
    far = jnp.where(core == 0, d_pooled[:, half:], d_pooled[:, :half])
    cut = [own[:, :part], own[:, part:], far[:, :part], far[:, part:]]
    cut = [(x * (1.0 / PASSAGE_LEN)).astype(BF16) for x in cut]
    for s in range(chips):
        back = sum(mm(cut[k], pieces[4 * s + k][...], ((1,), (1,))) for k in range(4))
        start = pl.multiple_of((chip ^ s) * depth, depth)
        back_ref[:, pl.ds(start, depth)] = back.astype(BF16).astype(F32)
    back = back_ref[...]
    half = back.shape[1] // 2
    d_att_ref[...] = jnp.where(core == 0, back[:, :half], back[:, half:])
    loss_ref[...] = jnp.broadcast_to(loss, loss_ref.shape)
    d_rows_ref[:, :part] = cut[0]
    d_rows_ref[:, part:] = cut[1]


def list_pass(where, places, bounds, unit, inverse, final_gain, w_score, scores, pieces,
              passages):
    count, width = unit.shape
    chips = len(pieces) // 4
    inner = chips * pieces[0].shape[0]
    vmem = pl.BlockSpec(memory_space=pltpu.VMEM)
    smem = pl.BlockSpec(memory_space=pltpu.SMEM)
    return pl.pallas_call(
        functools.partial(list_kernel, len(scores), chips, passages),
        in_specs=[smem] * 2 + [vmem] * (5 + len(scores) + len(pieces)),
        out_specs=[vmem] * 3,
        out_shape=[
            jax.ShapeDtypeStruct((count, inner // 2), F32),
            jax.ShapeDtypeStruct((count, width // 2), BF16),
            jax.ShapeDtypeStruct((8, 128), F32),
        ],
        scratch_shapes=[pltpu.VMEM((count, inner), F32)],
        compiler_params=pltpu.CompilerParams(vmem_limit_bytes=SMALL),
        cost_estimate=cost(2.5),
        name="list_grad",
    )(where, places, bounds, unit, inverse, final_gain[None], w_score[None], *scores,
      *pieces)


def payload_kernel(passages, where_ref, attn_ref, d_rows_ref, loss_ref, out_ref):
    core = where_ref[1]
    attn = attn_ref[...].astype(F32)
    half = attn.shape[1] // 2
    columns = [jnp.where(core == 0, attn[:, :half], attn[:, half:]), d_rows_ref[...].astype(F32)]
    rest = jnp.broadcast_to(loss_ref[:1], (attn.shape[0], 128))
    for _ in range(3):
        columns.append(rest.astype(BF16).astype(F32))
        rest = rest - columns[-1]
    columns = jnp.concatenate(columns, 1)
    turned = jnp.concatenate([columns[passages:], columns[:passages]], 0)
    out_ref[...] = jnp.where(core == 0, columns, turned).astype(BF16)


def payload_pass(where, attn, d_rows, loss):
    count = attn.shape[0]
    vmem = pl.BlockSpec(memory_space=pltpu.VMEM)
    return pl.pallas_call(
        functools.partial(payload_kernel, count // 2),
        in_specs=[pl.BlockSpec(memory_space=pltpu.SMEM)] + [vmem] * 3,
        out_specs=vmem,
        out_shape=jax.ShapeDtypeStruct(
            (count, attn.shape[1] // 2 + d_rows.shape[1] + 3 * 128), BF16
        ),
        compiler_params=pltpu.CompilerParams(vmem_limit_bytes=SMALL),
        cost_estimate=cost(1),
        name="out_payload",
    )(where, attn, d_rows, loss)


EXTRA = 16


def out_kernel(chips, where_ref, left_ref, *refs):
    near, far, out_ref = refs[:chips], refs[chips], refs[chips + 1]
    core = where_ref[1]
    cols = out_ref.shape[1] // 2
    own_rows = out_ref.shape[0] - EXTRA
    lead = far.shape[1] - 3 * 128 - cols
    mine = jnp.concatenate([ref[...] for ref in near], 0)
    other = far[...]
    down = ((0,), (0,))
    products = [mm(left_ref[...], x[:, lead : lead + cols], down) for x in (mine, other)]
    out_ref[:own_rows, :cols] = jnp.where(core == 0, *products).astype(BF16)
    out_ref[:own_rows, cols:] = jnp.where(core == 0, *products[::-1]).astype(BF16)

    count = mine.shape[0] // chips
    losses = []
    for s in range(chips):
        total = 0.0
        for x in (mine, other):
            row = x[s * count : s * count + EXTRA, lead + cols :].astype(F32)
            total = total + (row[:, :128] + row[:, 128:256] + row[:, 256:])
        losses.append(total)
    while len(losses) > 1:
        losses = [a + b for a, b in zip(losses[0::2], losses[1::2])]
    rest = losses[0]
    parts = []
    for _ in range(3):
        parts.append(rest.astype(BF16).astype(F32))
        rest = rest - parts[-1]
    index = lax.broadcasted_iota(jnp.int32, rest.shape, 0)
    row = jnp.where(index == 0, parts[0], jnp.where(index == 1, parts[1], parts[2])).astype(BF16)
    out_ref[own_rows:] = jnp.concatenate([row] * (2 * cols // row.shape[1]), 1)


def total_kernel(*refs):
    blocks, (out_ref, loss_ref) = refs[:-2], refs[-2:]
    own_rows = out_ref.shape[0]
    out_ref[...] = sum(ref[:own_rows].astype(F32) for ref in blocks)
    losses = []
    for ref in blocks:
        rows = ref[own_rows:].astype(F32)
        losses.append(rows[0:1] + rows[1:2] + rows[2:3])
    while len(losses) > 1:
        losses = [a + b for a, b in zip(losses[0::2], losses[1::2])]
    loss_ref[...] = jnp.broadcast_to(losses[0][:, :128], loss_ref.shape)


def total_pass(blocks):
    vmem = pl.BlockSpec(memory_space=pltpu.VMEM)
    rows, width = blocks[0].shape
    return pl.pallas_call(
        total_kernel,
        in_specs=[vmem] * len(blocks),
        out_specs=[vmem] * 2,
        out_shape=[
            jax.ShapeDtypeStruct((rows - EXTRA, width), F32),
            jax.ShapeDtypeStruct((8, 128), F32),
        ],
        compiler_params=pltpu.CompilerParams(vmem_limit_bytes=SMALL),
        cost_estimate=cost(1),
        name="out_total",
    )(*blocks)


def out_pass(where, left, near, far, cols):
    vmem = pl.BlockSpec(memory_space=pltpu.VMEM)
    return pl.pallas_call(
        functools.partial(out_kernel, len(near)),
        in_specs=[pl.BlockSpec(memory_space=pltpu.SMEM)] + [vmem] * (2 + len(near)),
        out_specs=vmem,
        out_shape=jax.ShapeDtypeStruct((left.shape[1] + EXTRA, 2 * cols), BF16),
        compiler_params=pltpu.CompilerParams(vmem_limit_bytes=SMALL),
        cost_estimate=cost(1),
        name="out_rows",
    )(where, left, *near, far)


def grad_kernel(blocks, where_ref, own_ref, sib_ref, d_own_ref, d_sib_ref, *out):
    depth, part = out[0].shape
    tile = min(depth, 256)
    down = ((0,), (0,))
    for n, s in enumerate(blocks):
        for i in range(depth // tile):
            start = pl.multiple_of((where_ref[0] ^ s) * depth + i * tile, tile)
            cols = pl.ds(start, tile)
            total = mm(own_ref[:, cols], d_own_ref[...], down)
            total = (total + mm(sib_ref[:, cols], d_sib_ref[...], down)).astype(BF16)
            out[2 * n][i * tile : (i + 1) * tile] = total[:, :part]
            out[2 * n + 1][i * tile : (i + 1) * tile] = total[:, part:]


def grad_blocks(where, blocks, own, sib, d_own, d_sib, depth):
    part = d_own.shape[1] // 2
    return local_call(
        functools.partial(grad_kernel, tuple(blocks)),
        "grad_rows",
        2.5 * len(blocks),
        where,
        [own, sib, d_own, d_sib],
        [jax.ShapeDtypeStruct((depth, part), BF16)] * (2 * len(blocks)),
    )


def pick_kernel(starts, sizes, where_ref, mine_ref, come_ref, a_ref, b_ref):
    core = where_ref[1]
    mine, come = mine_ref[...].astype(F32), come_ref[...].astype(F32)
    rows = mine.shape[0]
    halves = []
    for h in range(2):
        spans = [slice(a + h * n, a + (h + 1) * n) for a, n in zip(starts, sizes)]
        halves.append([jnp.concatenate([x[:, t] for t in spans], 1) for x in (mine, come)])
    first = jnp.where(core == 0, halves[0][0], halves[1][1]).astype(BF16)
    second = jnp.where(core == 0, halves[0][1], halves[1][0]).astype(BF16)
    part = a_ref.shape[1]
    a_ref[:rows], b_ref[:rows] = first[:, :part], first[:, part:]
    a_ref[rows:], b_ref[rows:] = second[:, :part], second[:, part:]


def pick(where, mine, come, starts, sizes):
    rows = mine.shape[0]
    vmem = pl.BlockSpec(memory_space=pltpu.VMEM)
    return pl.pallas_call(
        functools.partial(pick_kernel, starts, sizes),
        in_specs=[pl.BlockSpec(memory_space=pltpu.SMEM), vmem, vmem],
        out_specs=[vmem] * 2,
        out_shape=[jax.ShapeDtypeStruct((2 * rows, sum(sizes) // 2), BF16)] * 2,
        compiler_params=pltpu.CompilerParams(vmem_limit_bytes=SMALL),
        cost_estimate=cost(1),
        name="pick_columns",
    )(where, mine, come)


def solution(mesh):
    n_list, n_fsdp = mesh.shape["list"], mesh.shape["fsdp"]
    bits = [1 << k for k in range(1, n_fsdp.bit_length() - 1)]
    pairs = n_list * n_fsdp // 2

    def across(value, distance):
        return lax.ppermute(value, "fsdp", [(i, i ^ distance) for i in range(n_fsdp)])

    def along(value, distance):
        return lax.ppermute(value, "list", [(i, i ^ distance) for i in range(n_list)])

    def partner(kind, pair):
        return (
            pair ^ 1,
            ((pair + 1) ^ 1) - 1,
            pair ^ 2,
            ((pair + 2) ^ 2) - 2,
        )[kind]

    def neighbour(value, kind):
        moves = []
        for pair in range(pairs):
            for core in (0, 1):
                other = partner(kind + core, pair)
                if 0 <= other < pairs:
                    moves.append((2 * pair + core, 2 * other + core))
        return lax.ppermute(value, ("list", "fsdp"), moves)

    def after(value, *others):
        return lax.optimization_barrier((value, others))[0]

    def gathered(value, order, far=(), wait=True):
        have = {0: value}
        for bit in order:
            first = [part for s, part in have.items() if s]
            ready = dict(have)
            if first:
                ready = {
                    s: after(part, far, first) if s else after(part, first) if wait else part
                    for s, part in have.items()
                }
            have.update({s ^ (bit >> 1): across(part, bit) for s, part in ready.items()})
        return have

    def joined(parts, come, bit):
        return {
            s: (parts[s].astype(F32) + come[s].astype(F32)).astype(BF16)
            for s in parts
            if not s & (bit >> 1)
        }

    def sent(parts, bit):
        flag = bit >> 1
        return {s ^ flag: across(parts[s], bit) for s in sorted(parts)[::-1] if s & flag}

    def local(hidden, norm_gain, w_qkv, w_out, final_gain, w_score, prior, labels, lengths):
        passages, _, width = hidden.shape
        assert 4 * passages >= LONGEST - 1
        groups = KV_HEADS // 2
        width_q, width_k = groups * GROUP, groups * HEAD_DIM
        index = lax.axis_index("fsdp")
        core = index % 2
        chip = index // 2
        where = jnp.stack([chip, core]).astype(jnp.int32)
        first_core = core == 0

        def ordered(mine, other, axis):
            return jnp.where(
                first_core,
                jnp.concatenate([mine, other], axis),
                jnp.concatenate([other, mine], axis),
            )

        starts = (0, 2 * width_q, 2 * (width_q + width_k))
        sizes = (width_q, width_k, width_k)
        come = across(w_qkv, 1)
        pair_a, pair_b = pick(where, w_qkv, come, starts, sizes)
        w_out = after(w_out, come)
        out_come = across(w_out, 1)
        hidden_sib = across(after(hidden, come), 1)

        normal, sums, before_own = norm(where, hidden, norm_gain, (pair_a, pair_b))
        prior, labels, lengths, out_come = after((prior, labels, lengths, out_come), before_own)
        lanes = -(-lengths.shape[0] // 128) * 128
        label_weight = jnp.exp(labels.astype(F32))
        small = jnp.concatenate(
            [jnp.broadcast_to(x[:, None], (passages, 64)) for x in (prior, label_weight)], 1
        )
        small_sib = across(small, 1)
        pair = lax.axis_index("list") * (n_fsdp // 2) + chip
        places = [pair] + [
            jnp.where(first_core == near, partner(2 * kind, pair), partner(2 * kind + 1, pair))
            for near in (True, False)
            for kind in range(2)
        ]
        places = jnp.stack(places).astype(jnp.int32)
        bounds = jnp.broadcast_to(
            jnp.pad(lengths, (0, lanes - lengths.shape[0]))[None], (8, lanes)
        )

        cols = w_out.shape[1] // 2
        both = ordered(w_out, out_come, 0)
        out_pair = jnp.where(first_core, both[:, :cols], both[:, cols:])
        normal_sib, sums_sib, before_sib = norm(
            where,
            after(hidden_sib, before_own, places, bounds, small_sib, out_pair),
            norm_gain,
            (pair_a, pair_b),
        )
        part_a = gathered(pair_a, bits, far=before_own)
        part_b = gathered(pair_b, bits[::-1], far=before_own)
        chips = n_fsdp // 2
        last = max(bin(s).count("1") for s in range(chips))
        weights = [{}, {}, {}]
        for s in range(chips):
            ones = bin(s).count("1")
            weights[2 if ones == last else 1 if ones else 0][s] = (part_a[s], part_b[s])

        out_pair = after(out_pair, weights[1], before_sib)
        if weights[1]:
            normal_first = after(normal, before_sib)
            before_own = partial_project(where, normal_first, weights[1], before_own)
            before_sib = partial_project(
                where, after(normal_sib, before_own), weights[1], before_sib
            )
        before_own, before_sib, weights[2] = after(
            (before_own, before_sib, weights[2]), before_sib
        )
        proj_sib, probs_sib, attn_sib = forward(where, normal_sib, weights[2], groups, before_sib)
        attn_sib = attn_sib.reshape(passages, -1)
        attn_sib_other = across(attn_sib, 1)
        normal_last = after(normal, probs_sib)
        proj_own, probs_own, attn_own = forward(where, normal_last, weights[2], groups, before_own)
        attn_own = attn_own.reshape(passages, -1)
        attn_own_other = across(attn_own, 1)
        out_a = gathered(out_pair[:, : cols // 2], bits, before_sib, False)
        out_b = gathered(out_pair[:, cols // 2 :], bits[::-1], before_sib, False)
        pieces = []
        for s in range(chips):
            pieces += [out_a[s], out_b[s]]
            gate = probs_own
            pieces += [across(after(x, gate), 1) for x in (out_a[s], out_b[s])]
        unit, inverse, score, attn = score_pass(
            where,
            (attn_own, attn_sib, attn_sib_other, attn_own_other),
            (sums, sums_sib),
            final_gain,
            w_score,
            (small, small_sib),
            pieces,
        )
        near = [neighbour(score, kind) for kind in (0, 2)]
        scores = [score] + near + [across(x, 1) for x in near]
        d_attended, d_rows, loss_part = list_pass(
            where, places, bounds, unit, inverse, final_gain, w_score, scores, pieces, passages
        )

        d_own = backward(where, probs_own, proj_own, d_attended[:passages], groups)
        payload = payload_pass(where, attn, d_rows, loss_part)
        d_sib = backward(
            where, after(probs_sib, d_own), proj_sib, d_attended[passages:], groups
        )
        depth = pair_a.shape[0]
        flag_a, flag_b = bits[0] >> 1, bits[-1] >> 1
        lead = [s for s in range(chips) if s & flag_a and s & flag_b]
        rest = [s for s in range(1, chips) if s not in lead]

        def grads(blocks, *gate):
            out = grad_blocks(where, blocks, normal, normal_sib, d_own, after(d_sib, gate), depth)
            return dict(zip(blocks, out[0::2])), dict(zip(blocks, out[1::2]))

        parts_a, parts_b = grads(lead)
        first_a = {s ^ flag_a: across(parts_a[s], bits[0]) for s in lead}
        first_b = {s ^ flag_b: across(parts_b[s], bits[-1]) for s in lead}
        plane = gathered(payload, bits)
        plane = [plane[s] for s in range(chips)]
        more_a, more_b = grads(rest, parts_a, plane)
        far = across(jnp.concatenate(plane, 0), 1)
        for s in rest:
            if s & flag_a:
                first_a[s ^ flag_a] = across(more_a[s], bits[0])
            if s & flag_b:
                first_b[s ^ flag_b] = across(more_b[s], bits[-1])
        own_a, own_b = grads([0], more_a, first_a, first_b)
        parts_a.update(more_a)
        parts_b.update(more_b)
        parts_a.update(own_a)
        parts_b.update(own_b)
        left_a, left_b = joined(parts_a, first_a, bits[0]), joined(parts_b, first_b, bits[-1])
        place = lax.axis_index("list")
        inner = 2 * width_q
        left = ordered(
            jnp.concatenate([x[:, :width_q] for x in plane], 0), far[:, :width_q], 1
        )
        own_rows = inner // n_fsdp
        left = lax.dynamic_slice_in_dim(left, index * own_rows, own_rows, 1)
        rows = out_pass(where, left, plane, far, cols)
        blocks = rows.shape[1] // n_list
        block = lambda which: lax.dynamic_slice_in_dim(rows, which * blocks, blocks, 1)
        come_out = [block(place)]
        come_out += [along(block(place ^ distance), distance) for distance in range(1, n_list)]
        for bit_a, bit_b in zip(bits[1:], bits[::-1][1:]):
            far_a, far_b = after((sent(left_a, bit_a), sent(left_b, bit_b)), come_out)
            left_a, left_b = joined(left_a, far_a, bit_a), joined(left_b, far_b, bit_b)
        sum_a, sum_b = left_a[0], left_b[0]
        chip_sum = jnp.concatenate([sum_a, sum_b], 1)
        upper, lower = chip_sum[: depth // 2], chip_sum[depth // 2 :]
        keep = jnp.where(first_core, upper, lower)
        come = across(jnp.where(first_core, lower, upper), 1)
        columns = []
        at = 0
        for n in sizes:
            columns.append(ordered(keep[:, at : at + n], come[:, at : at + n], 1))
            at += n
        rows_sum = jnp.concatenate(columns, 1)
        place = lax.axis_index("list")

        def list_scatter(value):
            n = value.shape[1] // n_list
            block = lambda which: lax.dynamic_slice_in_dim(value, which * n, n, 1)
            total = block(place).astype(F32)
            for distance in range(1, n_list):
                total = total + along(block(place ^ distance).astype(BF16), distance).astype(F32)
            return total

        grad_qkv = list_scatter(rows_sum)

        grad_out, losses = total_pass(come_out)
        return (losses[0, 0], grad_qkv, grad_out)

    placed = (
        P(("list", "fsdp"), None, None),
        P(),
        P("fsdp", None),
        P("fsdp", None),
        P(),
        P(),
        P(("list", "fsdp")),
        P(("list", "fsdp")),
        P(),
    )
    return jax.shard_map(
        local,
        mesh=mesh,
        in_specs=placed,
        out_specs=(P(), P("fsdp", "list"), P("fsdp", "list")),
        check_vma=False,
    )
```

```python
import functools

import jax
import jax.numpy as jnp
from jax import lax
from jax.experimental import pallas as pl
from jax.experimental.pallas import tpu as pltpu
from jax.sharding import PartitionSpec as P

HEADS = 16
KV_HEADS = 4
HEAD_DIM = 64
PASSAGE_LEN = 64
LONGEST = 48
RATIO = HEADS // KV_HEADS
GROUP = RATIO * HEAD_DIM

epsilon = 1e-05
loss_scale = 64.0
scale = HEAD_DIM ** (-0.5)
VMEM = 10 * 1024 * 1024
SMALL = 6 * 1024 * 1024


def cost(micros):
    return pl.CostEstimate(flops=int(micros * 5e8), bytes_accessed=int(micros * 3.5e6), transcendentals=0)

BF16 = jnp.bfloat16
F32 = jnp.float32


def params(grid=1):
    return pltpu.CompilerParams(
        vmem_limit_bytes=VMEM, dimension_semantics=("arbitrary",) * grid
    )


def held(space, *values):
    return [pltpu.with_memory_space_constraint(x, space) for x in values]


def mm(a, b, dims=((1,), (0,))):
    return lax.dot_general(a, b, (dims, ((), ())), preferred_element_type=F32)


def norm_kernel(where_ref, hidden_ref, gain_ref, a_ref, b_ref, normal_ref, sum_ref, out_ref):
    values = hidden_ref[...].astype(F32)
    mean_square = jnp.mean(values * values, -1, keepdims=True)
    out = values * lax.rsqrt(mean_square + epsilon) * gain_ref[...][None]
    normal_ref[...] = out.reshape(normal_ref.shape).astype(BF16)
    sum_ref[0] = jnp.sum(values, 1)
    depth, part = a_ref.shape
    start = pl.multiple_of(where_ref[0] * depth, depth)
    block = normal_ref[:, pl.ds(start, depth)]
    out_ref[:, :part] = mm(block, a_ref[...])
    out_ref[:, part:] = mm(block, b_ref[...])


def norm(where, hidden, gain, weights):
    passages, length, width = hidden.shape
    depth, part = weights[0].shape
    step = 4 if passages % 4 == 0 else 1
    steps = passages // step
    whole = lambda i, w: (0, 0)
    normal, sums, product = pl.pallas_call(
        norm_kernel,
        grid_spec=pltpu.PrefetchScalarGridSpec(
            num_scalar_prefetch=1,
            grid=(steps,),
            in_specs=[
                pl.BlockSpec((step, length, width), lambda i, w: (i, 0, 0)),
                pl.BlockSpec((1, width), whole),
                pl.BlockSpec((depth, part), whole),
                pl.BlockSpec((depth, part), whole),
            ],
            out_specs=[
                pl.BlockSpec((step * length, width), lambda i, w: (i, 0)),
                pl.BlockSpec((1, step, width), lambda i, w: (i, 0, 0)),
                pl.BlockSpec((step * length, 2 * part), lambda i, w: (i, 0)),
            ],
        ),
        out_shape=[
            pltpu.VMEM((passages * length, width), BF16),
            jax.ShapeDtypeStruct((steps, step, width), F32),
            pltpu.VMEM((passages * length, 2 * part), F32),
        ],
        compiler_params=params(),
        cost_estimate=cost(7),
        name="norm_project",
    )(where, *held(pltpu.HBM, hidden), gain[None], *weights)
    return normal, sums, product


WIDE = 2 * HEAD_DIM
BATCH = 8


def low_lanes(rows):
    return lax.broadcasted_iota(jnp.int32, (rows, WIDE), 1) < HEAD_DIM


def ones_block(repeat):
    row = lax.broadcasted_iota(jnp.int32, (repeat * WIDE, WIDE), 0) // HEAD_DIM % 2
    col = lax.broadcasted_iota(jnp.int32, (repeat * WIDE, WIDE), 1) // HEAD_DIM
    return jnp.where(row == col, 1.0, 0.0).astype(BF16)


def diagonals(pair, factor):
    low = low_lanes(HEAD_DIM)
    wide = pair.astype(F32) * factor
    turned = pltpu.roll(wide, HEAD_DIM, 1)
    out = []
    for first, second in ((wide, turned), (turned, wide)):
        block = [jnp.where(low, first, 0.0), jnp.where(low, 0.0, second)]
        out.append(jnp.concatenate(block, 0).astype(BF16))
    return out


def segment_max(scores):
    low = low_lanes(scores.shape[0])
    first = jnp.max(jnp.where(low, scores, -jnp.inf), 1, keepdims=True)
    second = jnp.max(jnp.where(low, -jnp.inf, scores), 1, keepdims=True)
    return jnp.where(low, first, second)


def stacked(ref, rows, g):
    at = g * GROUP
    return jnp.concatenate([ref[rows, at : at + WIDE], ref[rows, at + WIDE : at + GROUP]], 0)


def product_of(chip, rows_ref, rows, shifts, weights):
    depth = weights[0].shape[0]
    out = []
    for part in range(2):
        total = None
        for k, s in enumerate(shifts):
            start = pl.multiple_of((chip ^ s) * depth, depth)
            x = mm(rows_ref[rows, pl.ds(start, depth)], weights[2 * k + part][...])
            total = x if total is None else total + x
        out.append(total)
    return out


def partial_kernel(shifts, step, where_ref, rows_ref, before_ref, *refs):
    weights, out_ref = refs[:-1], refs[-1]
    part = weights[0].shape[1]
    for i in range(rows_ref.shape[0] // step):
        rows = slice(i * step, (i + 1) * step)
        a, b = product_of(where_ref[0], rows_ref, rows, shifts, weights)
        out_ref[rows, :part] = a + before_ref[rows, :part]
        out_ref[rows, part:] = b + before_ref[rows, part:]


def forward_kernel(shifts, groups, batch, where_ref, rows_ref, before_ref, *refs):
    weights, refs = refs[: 2 * len(shifts)], refs[2 * len(shifts) :]
    projected_ref, probs_ref, sum_ref = refs
    part = weights[0].shape[1]
    ones = ones_block(1)
    width_q = groups * GROUP
    width_k = groups * HEAD_DIM
    step = batch * PASSAGE_LEN
    for n in range(rows_ref.shape[0] // step):
        rows = slice(n * step, (n + 1) * step)
        a, b = product_of(where_ref[0], rows_ref, rows, shifts, weights)
        projected_ref[rows, :part] = (a + before_ref[rows, :part]).astype(BF16)
        projected_ref[rows, part:] = (b + before_ref[rows, part:]).astype(BF16)
        spans = [
            slice(n * step + i * PASSAGE_LEN, n * step + (i + 1) * PASSAGE_LEN)
            for i in range(batch)
        ]
        keys = [diagonals(projected_ref[r, width_q : width_q + width_k], scale) for r in spans]
        values = [diagonals(projected_ref[r, width_q + width_k :], 1.0) for r in spans]
        for g in range(groups):
            scores = [
                mm(stacked(projected_ref, r, g), keys[i][g], ((1,), (1,)))
                for i, r in enumerate(spans)
            ]
            scores = jnp.concatenate(scores, 0)
            expo = jnp.exp(scores - segment_max(scores))
            total = mm(expo.astype(BF16), ones)
            probs = (expo / total).astype(BF16)
            probs_ref[n, g] = probs
            for i in range(batch):
                attended = mm(probs[i * WIDE : (i + 1) * WIDE], values[i][g])
                attended = attended.astype(BF16).astype(F32)
                for j in range(2):
                    at = g * GROUP + j * WIDE
                    sum_ref[n, i : i + 1, at : at + WIDE] = jnp.sum(
                        attended[j * HEAD_DIM : (j + 1) * HEAD_DIM], 0, keepdims=True
                    )


def row_step(total, batch):
    batch = batch if total % (batch * PASSAGE_LEN) == 0 else 1
    return batch, batch * PASSAGE_LEN


def local_call(kernel, name, micros, where, operands, out_shape):
    vmem = pl.BlockSpec(memory_space=pltpu.VMEM)
    return pl.pallas_call(
        kernel,
        in_specs=[pl.BlockSpec(memory_space=pltpu.SMEM)] + [vmem] * len(operands),
        out_specs=jax.tree.map(lambda _: vmem, out_shape),
        out_shape=out_shape,
        compiler_params=pltpu.CompilerParams(vmem_limit_bytes=VMEM),
        cost_estimate=cost(micros),
        name=name,
    )(where, *operands)


def partial_project(where, rows, weights, before):
    _, step = row_step(rows.shape[0], BATCH)
    return local_call(
        functools.partial(partial_kernel, tuple(weights), step),
        "project_more",
        4.5,
        where,
        [rows, before] + [x for s in weights for x in weights[s]],
        jax.ShapeDtypeStruct(before.shape, F32),
    )


def forward(where, rows, weights, groups, before):
    total = rows.shape[0]
    batch, step = row_step(total, BATCH)
    steps = total // step
    heads = groups * GROUP
    return local_call(
        functools.partial(forward_kernel, tuple(weights), groups, batch),
        "project_attend",
        6.5,
        where,
        [rows, before] + [x for s in weights for x in weights[s]],
        [
            jax.ShapeDtypeStruct(before.shape, BF16),
            jax.ShapeDtypeStruct((steps, groups, batch * WIDE, WIDE), BF16),
            jax.ShapeDtypeStruct((steps, batch, heads), F32),
        ],
    )


def backward_kernel(groups, where_ref, probs_ref, projected_ref, d_ref, out_ref):
    for n in range(probs_ref.shape[0]):
        backward_step(groups, n, probs_ref, projected_ref, d_ref, out_ref)


def backward_step(groups, n, probs_ref, projected_ref, d_ref, out_ref):
    low = low_lanes(HEAD_DIM)
    ones = ones_block(2)
    width_q = groups * GROUP
    width_k = groups * HEAD_DIM
    count = d_ref.shape[1]
    at = n * count
    spans = [slice((at + i) * PASSAGE_LEN, (at + i + 1) * PASSAGE_LEN) for i in range(count)]
    keys = [diagonals(projected_ref[r, width_q : width_q + width_k], scale) for r in spans]
    values = [diagonals(projected_ref[r, width_q + width_k :], 1.0) for r in spans]
    down = ((0,), (0,))
    d_keys = [[] for _ in spans]
    d_values = [[] for _ in spans]

    def fold(product):
        kept = jnp.where(low, product[:HEAD_DIM], product[HEAD_DIM:])
        return kept + pltpu.roll(kept, HEAD_DIM, 1)

    for g in range(groups):
        probs = probs_ref[n, g]
        d_rows = []
        for i in range(count):
            row = [
                d_ref[n, i : i + 1, g * GROUP + j * WIDE : g * GROUP + (j + 1) * WIDE]
                for j in range(2)
            ]
            d_rows.append(
                jnp.concatenate(
                    [jnp.broadcast_to(x, (HEAD_DIM, WIDE)) for x in row], 0
                ).astype(BF16)
            )
        d_probs = jnp.concatenate(
            [mm(d_rows[i], values[i][g], ((1,), (1,))) for i in range(count)], 0
        )
        probs_f = probs.astype(F32)
        product = probs_f * d_probs
        upper = product.astype(BF16)
        lower = (product - upper.astype(F32)).astype(BF16)
        inner = mm(jnp.concatenate([upper, lower], 1), ones)
        d_scores = (probs_f * (d_probs - inner)).astype(BF16)
        for i, r in enumerate(spans):
            block = slice(i * WIDE, (i + 1) * WIDE)
            d_query = mm(d_scores[block], keys[i][g]).astype(BF16)
            at = g * GROUP
            out_ref[r, at : at + WIDE] = d_query[:HEAD_DIM]
            out_ref[r, at + WIDE : at + GROUP] = d_query[HEAD_DIM:]
            d_keys[i].append(fold(mm(d_scores[block], stacked(projected_ref, r, g), down)) * scale)
            d_values[i].append(fold(mm(probs[block], d_rows[i], down)))
    for i, r in enumerate(spans):
        out_ref[r, width_q : width_q + width_k] = jnp.where(low, *d_keys[i]).astype(BF16)
        out_ref[r, width_q + width_k :] = jnp.where(low, *d_values[i]).astype(BF16)


def backward(where, probs, projected, d_attended, groups):
    steps = probs.shape[0]
    batch = probs.shape[2] // WIDE
    return local_call(
        functools.partial(backward_kernel, groups),
        "attend_back",
        3.4,
        where,
        [probs, projected, d_attended.reshape(steps, batch, groups * GROUP)],
        jax.ShapeDtypeStruct(projected.shape, BF16),
    )


def score_kernel(chips, where_ref, own_ref, sib_ref, own_far_ref, sib_far_ref, sum_ref, sib_sum_ref,
                 final_ref, ws_ref, prior_ref, prior_sib_ref, *refs):
    pieces, refs = refs[: 4 * chips], refs[4 * chips :]
    score_ref, attn_ref, d_att_ref, d_rows_ref, product_ref = refs
    chip, core = where_ref[0], where_ref[1]
    mine = jnp.concatenate([own_ref[...], sib_ref[...]], 0)
    other = jnp.concatenate([own_far_ref[...], sib_far_ref[...]], 0)
    sums = [ref[k] for ref in (sum_ref, sib_sum_ref) for k in range(ref.shape[0])]
    attn = jnp.concatenate(
        [jnp.where(core == 0, mine, other), jnp.where(core == 0, other, mine)], 1
    )
    count = attn.shape[0]
    upper = attn.astype(BF16)
    attn_ref[...] = upper
    both = jnp.concatenate([upper.astype(F32), attn - upper.astype(F32)], 0)
    product_ref[...] = both
    depth, part = pieces[0].shape
    out = [None] * 4
    for s in range(chips):
        start = pl.multiple_of((chip ^ s) * depth, depth)
        block = product_ref[:, pl.ds(start, depth)].astype(BF16)
        for k in range(4):
            x = mm(block, pieces[4 * s + k][...])
            out[k] = x if out[k] is None else out[k] + x
    out = [x[:count] + x[count:] for x in out]
    own, far = jnp.concatenate(out[:2], 1), jnp.concatenate(out[2:], 1)
    product = jnp.concatenate(
        [jnp.where(core == 0, own, far), jnp.where(core == 0, far, own)], 1
    )
    pooled = (jnp.concatenate(sums, 0) + product) * (1.0 / PASSAGE_LEN)
    inverse = lax.rsqrt(jnp.mean(pooled * pooled, -1, keepdims=True) + epsilon)
    unit = pooled * inverse
    direction = final_ref[...] * ws_ref[...]
    score = jnp.sum(unit * direction, -1, keepdims=True)
    lane = lax.broadcasted_iota(jnp.int32, score_ref.shape, 1)
    half = score_ref.shape[1] // 2
    prior = jnp.concatenate([prior_ref[...], prior_sib_ref[...]], 0)
    score_ref[...] = jnp.where(lane < half, score, 0.0) + prior

    mean = jnp.mean(unit * direction, -1, keepdims=True)
    d_rows = inverse * (direction - unit * mean) * (1.0 / PASSAGE_LEN)
    half = d_rows.shape[1] // 2
    own = jnp.where(core == 0, d_rows[:, :half], d_rows[:, half:])
    far = jnp.where(core == 0, d_rows[:, half:], d_rows[:, :half])
    d_rows_ref[...] = own
    cut = [x.astype(BF16) for x in (own[:, :part], own[:, part:], far[:, :part], far[:, part:])]
    for s in range(chips):
        back = sum(mm(cut[k], pieces[4 * s + k][...], ((1,), (1,))) for k in range(4))
        start = pl.multiple_of((chip ^ s) * depth, depth)
        product_ref[:count, pl.ds(start, depth)] = back.astype(BF16).astype(F32)
    back = product_ref[:count]
    half = back.shape[1] // 2
    d_att_ref[...] = jnp.where(core == 0, back[:, :half], back[:, half:])


def score_pass(where, attn, sums, final_gain, w_score, priors, pieces):
    count, width = 2 * attn[0].shape[0], sums[0].shape[2]
    lanes = priors[0].shape[1]
    inner = 2 * attn[0].shape[1]
    vmem = pl.BlockSpec(memory_space=pltpu.VMEM)
    return pl.pallas_call(
        functools.partial(score_kernel, len(pieces) // 4),
        in_specs=[pl.BlockSpec(memory_space=pltpu.SMEM)] + [vmem] * (10 + len(pieces)),
        out_specs=[vmem] * 4,
        out_shape=[
            jax.ShapeDtypeStruct((count, lanes), F32),
            jax.ShapeDtypeStruct((count, inner), BF16),
            jax.ShapeDtypeStruct((count, inner // 2), F32),
            jax.ShapeDtypeStruct((count, width // 2), F32),
        ],
        scratch_shapes=[pltpu.VMEM((2 * count, inner), F32)],
        compiler_params=pltpu.CompilerParams(vmem_limit_bytes=SMALL),
        cost_estimate=cost(2),
        name="pool_score",
    )(where, *attn, *sums, final_gain[None], w_score[None], *priors, *pieces)


def list_kernel(blocks, passages, where_ref, place_ref, bounds_ref, rows_ref, own_ref, sib_ref,
                *refs):
    scores = [ref[...] for ref in refs[:blocks]]
    d_rows_ref, loss_ref, d_own_ref, d_sib_ref = refs[blocks:]
    core = where_ref[1]
    pair = 2 * passages
    lanes = bounds_ref.shape[1]
    lane = lax.broadcasted_iota(jnp.int32, bounds_ref.shape, 1)
    ends, reach = bounds_ref[...], 1
    while reach < lanes:
        ends = ends + jnp.where(lane >= reach, pltpu.roll(ends, reach, 1), 0)
        reach *= 2
    starts, ends = (ends - bounds_ref[...])[:1], ends[:1]
    row = lax.broadcasted_iota(jnp.int32, (pair, lanes), 0)
    near = jnp.where(row < passages, core * passages + row, (1 - core) * passages + row - passages)
    far = jnp.where(row < passages, (1 - core) * passages + row, core * passages + row - passages)
    members = []
    for j in range(blocks):
        place = place_ref[j] * pair + (near if j <= blocks // 2 else far)
        members.append((place >= starts) & (place < ends))
    high = scores[0].shape[1] // 2
    column = [jnp.broadcast_to(score[:, :1], (pair, lanes)) for score in scores]
    heavy = [jnp.broadcast_to(score[:, high : high + 1], (pair, lanes)) for score in scores]
    peak = functools.reduce(
        jnp.maximum,
        [jnp.max(jnp.where(m, s, -1e30), 0, keepdims=True) for m, s in zip(members, column)],
    )
    total = sum(
        jnp.sum(jnp.where(m, jnp.exp(jnp.where(m, s - peak, 0.0)), 0.0), 0, keepdims=True)
        for m, s in zip(members, column)
    )
    label_total = sum(
        jnp.sum(jnp.where(m, w, 0.0), 0, keepdims=True) for m, w in zip(members, heavy)
    )
    log_norm = peak + jnp.log(total)
    own = members[0]
    log_prob = column[0][:, :1] - jnp.sum(jnp.where(own, log_norm, 0.0), 1, keepdims=True)
    target = heavy[0][:, :1] / jnp.sum(jnp.where(own, label_total, 0.0), 1, keepdims=True)
    loss = -loss_scale * jnp.sum((target * log_prob)[:passages], 0, keepdims=True)
    d_score = loss_scale * (jnp.exp(log_prob) - target)
    loss_ref[...] = jnp.broadcast_to(loss, loss_ref.shape)
    d_rows_ref[...] = (rows_ref[...] * d_score).astype(BF16)
    for k, (ref, out_ref) in enumerate(((own_ref, d_own_ref), (sib_ref, d_sib_ref))):
        for i in range(passages):
            rows = slice(i * PASSAGE_LEN, (i + 1) * PASSAGE_LEN)
            at = k * passages + i
            out_ref[rows] = (ref[rows].astype(F32) * d_score[at : at + 1]).astype(BF16)


def list_pass(where, places, bounds, rows, d_own, d_sib, scores):
    vmem = pl.BlockSpec(memory_space=pltpu.VMEM)
    smem = pl.BlockSpec(memory_space=pltpu.SMEM)
    return pl.pallas_call(
        functools.partial(list_kernel, len(scores), rows.shape[0] // 2),
        in_specs=[smem] * 2 + [vmem] * (4 + len(scores)),
        out_specs=[vmem] * 4,
        out_shape=[
            jax.ShapeDtypeStruct(rows.shape, BF16),
            jax.ShapeDtypeStruct((8, 128), F32),
            jax.ShapeDtypeStruct(d_own.shape, BF16),
            jax.ShapeDtypeStruct(d_sib.shape, BF16),
        ],
        compiler_params=pltpu.CompilerParams(vmem_limit_bytes=SMALL),
        cost_estimate=cost(2.5),
        name="list_grad",
    )(where, places, bounds, rows, d_own, d_sib, *scores)


def payload_kernel(passages, where_ref, attn_ref, d_rows_ref, loss_ref, out_ref):
    core = where_ref[1]
    attn = attn_ref[...].astype(F32)
    half = attn.shape[1] // 2
    columns = [jnp.where(core == 0, attn[:, :half], attn[:, half:]), d_rows_ref[...].astype(F32)]
    rest = jnp.broadcast_to(loss_ref[:1], (attn.shape[0], 128))
    for _ in range(3):
        columns.append(rest.astype(BF16).astype(F32))
        rest = rest - columns[-1]
    columns = jnp.concatenate(columns, 1)
    turned = jnp.concatenate([columns[passages:], columns[:passages]], 0)
    out_ref[...] = jnp.where(core == 0, columns, turned).astype(BF16)


def payload_pass(where, attn, d_rows, loss):
    count = attn.shape[0]
    vmem = pl.BlockSpec(memory_space=pltpu.VMEM)
    return pl.pallas_call(
        functools.partial(payload_kernel, count // 2),
        in_specs=[pl.BlockSpec(memory_space=pltpu.SMEM)] + [vmem] * 3,
        out_specs=vmem,
        out_shape=jax.ShapeDtypeStruct(
            (count, attn.shape[1] // 2 + d_rows.shape[1] + 3 * 128), BF16
        ),
        compiler_params=pltpu.CompilerParams(vmem_limit_bytes=SMALL),
        cost_estimate=cost(1),
        name="out_payload",
    )(where, attn, d_rows, loss)


EXTRA = 16


def out_kernel(chips, where_ref, left_ref, *refs):
    near, far, out_ref = refs[:chips], refs[chips], refs[chips + 1]
    core = where_ref[1]
    cols = out_ref.shape[1] // 2
    own_rows = out_ref.shape[0] - EXTRA
    lead = far.shape[1] - 3 * 128 - cols
    mine = jnp.concatenate([ref[...] for ref in near], 0)
    other = far[...]
    down = ((0,), (0,))
    products = [mm(left_ref[...], x[:, lead : lead + cols], down) for x in (mine, other)]
    out_ref[:own_rows, :cols] = jnp.where(core == 0, *products).astype(BF16)
    out_ref[:own_rows, cols:] = jnp.where(core == 0, *products[::-1]).astype(BF16)

    count = mine.shape[0] // chips
    losses = []
    for s in range(chips):
        total = 0.0
        for x in (mine, other):
            row = x[s * count : s * count + EXTRA, lead + cols :].astype(F32)
            total = total + (row[:, :128] + row[:, 128:256] + row[:, 256:])
        losses.append(total)
    while len(losses) > 1:
        losses = [a + b for a, b in zip(losses[0::2], losses[1::2])]
    rest = losses[0]
    parts = []
    for _ in range(3):
        parts.append(rest.astype(BF16).astype(F32))
        rest = rest - parts[-1]
    index = lax.broadcasted_iota(jnp.int32, rest.shape, 0)
    row = jnp.where(index == 0, parts[0], jnp.where(index == 1, parts[1], parts[2])).astype(BF16)
    out_ref[own_rows:] = jnp.concatenate([row] * (2 * cols // row.shape[1]), 1)


def total_kernel(*refs):
    blocks, (out_ref, loss_ref) = refs[:-2], refs[-2:]
    own_rows = out_ref.shape[0]
    out_ref[...] = sum(ref[:own_rows].astype(F32) for ref in blocks)
    losses = []
    for ref in blocks:
        rows = ref[own_rows:].astype(F32)
        losses.append(rows[0:1] + rows[1:2] + rows[2:3])
    while len(losses) > 1:
        losses = [a + b for a, b in zip(losses[0::2], losses[1::2])]
    loss_ref[...] = jnp.broadcast_to(losses[0][:, :128], loss_ref.shape)


def total_pass(blocks):
    vmem = pl.BlockSpec(memory_space=pltpu.VMEM)
    rows, width = blocks[0].shape
    return pl.pallas_call(
        total_kernel,
        in_specs=[vmem] * len(blocks),
        out_specs=[vmem] * 2,
        out_shape=[
            jax.ShapeDtypeStruct((rows - EXTRA, width), F32),
            jax.ShapeDtypeStruct((8, 128), F32),
        ],
        compiler_params=pltpu.CompilerParams(vmem_limit_bytes=SMALL),
        cost_estimate=cost(1),
        name="out_total",
    )(*blocks)


def out_pass(where, left, near, far, cols):
    vmem = pl.BlockSpec(memory_space=pltpu.VMEM)
    return pl.pallas_call(
        functools.partial(out_kernel, len(near)),
        in_specs=[pl.BlockSpec(memory_space=pltpu.SMEM)] + [vmem] * (2 + len(near)),
        out_specs=vmem,
        out_shape=jax.ShapeDtypeStruct((left.shape[1] + EXTRA, 2 * cols), BF16),
        compiler_params=pltpu.CompilerParams(vmem_limit_bytes=SMALL),
        cost_estimate=cost(1),
        name="out_rows",
    )(where, left, *near, far)


def grad_kernel(blocks, where_ref, own_ref, sib_ref, d_own_ref, d_sib_ref, *out):
    depth, part = out[0].shape
    tile = min(depth, 256)
    down = ((0,), (0,))
    for n, s in enumerate(blocks):
        for i in range(depth // tile):
            start = pl.multiple_of((where_ref[0] ^ s) * depth + i * tile, tile)
            cols = pl.ds(start, tile)
            total = mm(own_ref[:, cols], d_own_ref[...], down)
            total = (total + mm(sib_ref[:, cols], d_sib_ref[...], down)).astype(BF16)
            out[2 * n][i * tile : (i + 1) * tile] = total[:, :part]
            out[2 * n + 1][i * tile : (i + 1) * tile] = total[:, part:]


def grad_blocks(where, blocks, own, sib, d_own, d_sib, depth):
    part = d_own.shape[1] // 2
    return local_call(
        functools.partial(grad_kernel, tuple(blocks)),
        "grad_rows",
        2.5 * len(blocks),
        where,
        [own, sib, d_own, d_sib],
        [jax.ShapeDtypeStruct((depth, part), BF16)] * (2 * len(blocks)),
    )


def pick_kernel(starts, sizes, where_ref, mine_ref, come_ref, a_ref, b_ref):
    core = where_ref[1]
    mine, come = mine_ref[...].astype(F32), come_ref[...].astype(F32)
    rows = mine.shape[0]
    halves = []
    for h in range(2):
        spans = [slice(a + h * n, a + (h + 1) * n) for a, n in zip(starts, sizes)]
        halves.append([jnp.concatenate([x[:, t] for t in spans], 1) for x in (mine, come)])
    first = jnp.where(core == 0, halves[0][0], halves[1][1]).astype(BF16)
    second = jnp.where(core == 0, halves[0][1], halves[1][0]).astype(BF16)
    part = a_ref.shape[1]
    a_ref[:rows], b_ref[:rows] = first[:, :part], first[:, part:]
    a_ref[rows:], b_ref[rows:] = second[:, :part], second[:, part:]


def pick(where, mine, come, starts, sizes):
    rows = mine.shape[0]
    vmem = pl.BlockSpec(memory_space=pltpu.VMEM)
    return pl.pallas_call(
        functools.partial(pick_kernel, starts, sizes),
        in_specs=[pl.BlockSpec(memory_space=pltpu.SMEM), vmem, vmem],
        out_specs=[vmem] * 2,
        out_shape=[jax.ShapeDtypeStruct((2 * rows, sum(sizes) // 2), BF16)] * 2,
        compiler_params=pltpu.CompilerParams(vmem_limit_bytes=SMALL),
        cost_estimate=cost(1),
        name="pick_columns",
    )(where, mine, come)


def solution(mesh):
    n_list, n_fsdp = mesh.shape["list"], mesh.shape["fsdp"]
    bits = [1 << k for k in range(1, n_fsdp.bit_length() - 1)]
    pairs = n_list * n_fsdp // 2

    def across(value, distance):
        return lax.ppermute(value, "fsdp", [(i, i ^ distance) for i in range(n_fsdp)])

    def along(value, distance):
        return lax.ppermute(value, "list", [(i, i ^ distance) for i in range(n_list)])

    def partner(kind, pair):
        return (
            pair ^ 1,
            ((pair + 1) ^ 1) - 1,
            pair ^ 2,
            ((pair + 2) ^ 2) - 2,
        )[kind]

    def neighbour(value, kind):
        moves = []
        for pair in range(pairs):
            for core in (0, 1):
                other = partner(kind + core, pair)
                if 0 <= other < pairs:
                    moves.append((2 * pair + core, 2 * other + core))
        return lax.ppermute(value, ("list", "fsdp"), moves)

    def after(value, *others):
        return lax.optimization_barrier((value, others))[0]

    def gathered(value, order, far=(), wait=True):
        have = {0: value}
        for bit in order:
            first = [part for s, part in have.items() if s]
            ready = dict(have)
            if first:
                ready = {
                    s: after(part, far, first) if s else after(part, first) if wait else part
                    for s, part in have.items()
                }
            have.update({s ^ (bit >> 1): across(part, bit) for s, part in ready.items()})
        return have

    def joined(parts, come, bit):
        return {
            s: (parts[s].astype(F32) + come[s].astype(F32)).astype(BF16)
            for s in parts
            if not s & (bit >> 1)
        }

    def sent(parts, bit):
        flag = bit >> 1
        return {s ^ flag: across(parts[s], bit) for s in sorted(parts)[::-1] if s & flag}

    def local(hidden, norm_gain, w_qkv, w_out, final_gain, w_score, prior, labels, lengths):
        passages, _, width = hidden.shape
        assert 4 * passages >= LONGEST - 1
        groups = KV_HEADS // 2
        width_q, width_k = groups * GROUP, groups * HEAD_DIM
        index = lax.axis_index("fsdp")
        core = index % 2
        chip = index // 2
        where = jnp.stack([chip, core]).astype(jnp.int32)
        first_core = core == 0

        def ordered(mine, other, axis):
            return jnp.where(
                first_core,
                jnp.concatenate([mine, other], axis),
                jnp.concatenate([other, mine], axis),
            )

        starts = (0, 2 * width_q, 2 * (width_q + width_k))
        sizes = (width_q, width_k, width_k)
        come = across(w_qkv, 1)
        pair_a, pair_b = pick(where, w_qkv, come, starts, sizes)
        w_out = after(w_out, come)
        out_come = across(w_out, 1)
        hidden_sib = across(after(hidden, come), 1)

        normal, sums, before_own = norm(where, hidden, norm_gain, (pair_a, pair_b))
        prior, labels, lengths, out_come = after((prior, labels, lengths, out_come), before_own)
        lanes = -(-lengths.shape[0] // 128) * 128
        label_weight = jnp.exp(labels.astype(F32))
        small = jnp.concatenate(
            [jnp.broadcast_to(x[:, None], (passages, 64)) for x in (prior, label_weight)], 1
        )
        small_sib = across(small, 1)
        pair = lax.axis_index("list") * (n_fsdp // 2) + chip
        places = [pair] + [
            jnp.where(first_core == near, partner(2 * kind, pair), partner(2 * kind + 1, pair))
            for near in (True, False)
            for kind in range(2)
        ]
        places = jnp.stack(places).astype(jnp.int32)
        bounds = jnp.broadcast_to(
            jnp.pad(lengths, (0, lanes - lengths.shape[0]))[None], (8, lanes)
        )

        cols = w_out.shape[1] // 2
        both = ordered(w_out, out_come, 0)
        out_pair = jnp.where(first_core, both[:, :cols], both[:, cols:])
        normal_sib, sums_sib, before_sib = norm(
            where,
            after(hidden_sib, before_own, places, bounds, small_sib, out_pair),
            norm_gain,
            (pair_a, pair_b),
        )
        part_a = gathered(pair_a, bits, far=before_own)
        part_b = gathered(pair_b, bits[::-1], far=before_own)
        chips = n_fsdp // 2
        last = max(bin(s).count("1") for s in range(chips))
        weights = [{}, {}, {}]
        for s in range(chips):
            ones = bin(s).count("1")
            weights[2 if ones == last else 1 if ones else 0][s] = (part_a[s], part_b[s])

        out_pair = after(out_pair, weights[1], before_sib)
        if weights[1]:
            normal_first = after(normal, before_sib)
            before_own = partial_project(where, normal_first, weights[1], before_own)
            before_sib = partial_project(
                where, after(normal_sib, before_own), weights[1], before_sib
            )
        before_own, before_sib, weights[2] = after(
            (before_own, before_sib, weights[2]), before_sib
        )
        proj_sib, probs_sib, attn_sib = forward(where, normal_sib, weights[2], groups, before_sib)
        attn_sib = attn_sib.reshape(passages, -1)
        attn_sib_other = across(attn_sib, 1)
        normal_last = after(normal, probs_sib)
        proj_own, probs_own, attn_own = forward(where, normal_last, weights[2], groups, before_own)
        attn_own = attn_own.reshape(passages, -1)
        attn_own_other = across(attn_own, 1)
        out_a = gathered(out_pair[:, : cols // 2], bits, before_sib, False)
        out_b = gathered(out_pair[:, cols // 2 :], bits[::-1], before_sib, False)
        pieces = []
        for s in range(chips):
            pieces += [out_a[s], out_b[s]]
            gate = probs_own
            pieces += [across(after(x, gate), 1) for x in (out_a[s], out_b[s])]
        score, attn, d_attended, direction = score_pass(
            where,
            (attn_own, attn_sib, attn_sib_other, attn_own_other),
            (sums, sums_sib),
            final_gain,
            w_score,
            (small, small_sib),
            pieces,
        )
        near = [neighbour(score, kind) for kind in (0, 2)]
        scores = [score] + near + [across(x, 1) for x in near]
        d_own = backward(where, probs_own, proj_own, d_attended[:passages], groups)
        d_sib = backward(
            where, after(probs_sib, d_own), proj_sib, d_attended[passages:], groups
        )
        d_rows, loss_part, d_own, d_sib = list_pass(
            where, places, bounds, direction, d_own, d_sib, scores
        )
        inner = attn.shape[1]
        payload = payload_pass(where, attn, d_rows, loss_part)
        depth = pair_a.shape[0]
        flag_a, flag_b = bits[0] >> 1, bits[-1] >> 1
        lead = [s for s in range(chips) if s & flag_a and s & flag_b]
        rest = [s for s in range(1, chips) if s not in lead]

        def grads(blocks, *gate):
            out = grad_blocks(where, blocks, normal, normal_sib, d_own, after(d_sib, gate), depth)
            return dict(zip(blocks, out[0::2])), dict(zip(blocks, out[1::2]))

        parts_a, parts_b = grads(lead)
        first_a = {s ^ flag_a: across(parts_a[s], bits[0]) for s in lead}
        first_b = {s ^ flag_b: across(parts_b[s], bits[-1]) for s in lead}
        plane = [payload] + [across(payload, 2 * s) for s in range(1, chips)]
        more_a, more_b = grads(rest, parts_a, plane)
        far = across(jnp.concatenate(plane, 0), 1)
        for s in rest:
            if s & flag_a:
                first_a[s ^ flag_a] = across(more_a[s], bits[0])
            if s & flag_b:
                first_b[s ^ flag_b] = across(more_b[s], bits[-1])
        own_a, own_b = grads([0], more_a, first_a, first_b, far)
        parts_a.update(more_a)
        parts_b.update(more_b)
        parts_a.update(own_a)
        parts_b.update(own_b)
        left_a, left_b = joined(parts_a, first_a, bits[0]), joined(parts_b, first_b, bits[-1])
        place = lax.axis_index("list")
        inner = 2 * width_q
        left = ordered(
            jnp.concatenate([x[:, :width_q] for x in plane], 0), far[:, :width_q], 1
        )
        own_rows = inner // n_fsdp
        left = lax.dynamic_slice_in_dim(left, index * own_rows, own_rows, 1)
        rows = out_pass(where, left, plane, far, cols)
        blocks = rows.shape[1] // n_list
        block = lambda which: lax.dynamic_slice_in_dim(rows, which * blocks, blocks, 1)
        come_out = [block(place)]
        come_out += [along(block(place ^ distance), distance) for distance in range(1, n_list)]
        for bit_a, bit_b in zip(bits[1:], bits[::-1][1:]):
            far_a, far_b = after((sent(left_a, bit_a), sent(left_b, bit_b)), come_out)
            left_a, left_b = joined(left_a, far_a, bit_a), joined(left_b, far_b, bit_b)
        sum_a, sum_b = left_a[0], left_b[0]
        chip_sum = jnp.concatenate([sum_a, sum_b], 1)
        upper, lower = chip_sum[: depth // 2], chip_sum[depth // 2 :]
        keep = jnp.where(first_core, upper, lower)
        come = across(jnp.where(first_core, lower, upper), 1)
        columns = []
        at = 0
        for n in sizes:
            columns.append(ordered(keep[:, at : at + n], come[:, at : at + n], 1))
            at += n
        rows_sum = jnp.concatenate(columns, 1)
        place = lax.axis_index("list")

        def list_scatter(value):
            n = value.shape[1] // n_list
            block = lambda which: lax.dynamic_slice_in_dim(value, which * n, n, 1)
            total = block(place).astype(F32)
            for distance in range(1, n_list):
                total = total + along(block(place ^ distance).astype(BF16), distance).astype(F32)
            return total

        grad_qkv = list_scatter(rows_sum)

        grad_out, losses = total_pass(come_out)
        return (losses[0, 0], grad_qkv, grad_out)

    placed = (
        P(("list", "fsdp"), None, None),
        P(),
        P("fsdp", None),
        P("fsdp", None),
        P(),
        P(),
        P(("list", "fsdp")),
        P(("list", "fsdp")),
        P(),
    )
    return jax.shard_map(
        local,
        mesh=mesh,
        in_specs=placed,
        out_specs=(P(), P("fsdp", "list"), P("fsdp", "list")),
        check_vma=False,
    )
```

```python
import functools

import jax
import jax.numpy as jnp
from jax import lax
from jax.experimental import pallas as pl
from jax.experimental.pallas import tpu as pltpu
from jax.sharding import PartitionSpec as P

HEADS = 16
KV_HEADS = 4
HEAD_DIM = 64
PASSAGE_LEN = 64
LONGEST = 48
RATIO = HEADS // KV_HEADS
GROUP = RATIO * HEAD_DIM

epsilon = 1e-05
loss_scale = 64.0
scale = HEAD_DIM ** (-0.5)
VMEM = 14 * 1024 * 1024
SMALL = 6 * 1024 * 1024


def cost(micros):
    return pl.CostEstimate(flops=int(micros * 5e8), bytes_accessed=int(micros * 3.5e6), transcendentals=0)

BF16 = jnp.bfloat16
F32 = jnp.float32


def params(grid=1):
    return pltpu.CompilerParams(
        vmem_limit_bytes=VMEM, dimension_semantics=("arbitrary",) * grid
    )


def held(space, *values):
    return [pltpu.with_memory_space_constraint(x, space) for x in values]


def mm(a, b, dims=((1,), (0,))):
    return lax.dot_general(a, b, (dims, ((), ())), preferred_element_type=F32)


def norm_kernel(where_ref, hidden_ref, gain_ref, a_ref, b_ref, normal_ref, sum_ref, out_ref):
    values = hidden_ref[...].astype(F32)
    mean_square = jnp.mean(values * values, -1, keepdims=True)
    out = values * lax.rsqrt(mean_square + epsilon) * gain_ref[...][None]
    normal_ref[...] = out.reshape(normal_ref.shape).astype(BF16)
    sum_ref[0] = jnp.sum(values, 1)
    depth, part = a_ref.shape
    start = pl.multiple_of(where_ref[0] * depth, depth)
    block = normal_ref[:, pl.ds(start, depth)]
    out_ref[:, :part] = mm(block, a_ref[...])
    out_ref[:, part:] = mm(block, b_ref[...])


def norm(where, hidden, gain, weights):
    passages, length, width = hidden.shape
    depth, part = weights[0].shape
    step = 4 if passages % 4 == 0 else 1
    steps = passages // step
    whole = lambda i, w: (0, 0)
    normal, sums, product = pl.pallas_call(
        norm_kernel,
        grid_spec=pltpu.PrefetchScalarGridSpec(
            num_scalar_prefetch=1,
            grid=(steps,),
            in_specs=[
                pl.BlockSpec((step, length, width), lambda i, w: (i, 0, 0)),
                pl.BlockSpec((1, width), whole),
                pl.BlockSpec((depth, part), whole),
                pl.BlockSpec((depth, part), whole),
            ],
            out_specs=[
                pl.BlockSpec((step * length, width), lambda i, w: (i, 0)),
                pl.BlockSpec((1, step, width), lambda i, w: (i, 0, 0)),
                pl.BlockSpec((step * length, 2 * part), lambda i, w: (i, 0)),
            ],
        ),
        out_shape=[
            pltpu.VMEM((passages * length, width), BF16),
            jax.ShapeDtypeStruct((steps, step, width), F32),
            pltpu.VMEM((passages * length, 2 * part), F32),
        ],
        compiler_params=params(),
        cost_estimate=cost(7),
        name="norm_project",
    )(where, *held(pltpu.HBM, hidden), gain[None], *weights)
    return normal, sums, product


WIDE = 2 * HEAD_DIM
BATCH = 8


def low_lanes(rows):
    return lax.broadcasted_iota(jnp.int32, (rows, WIDE), 1) < HEAD_DIM


def ones_block(repeat):
    row = lax.broadcasted_iota(jnp.int32, (repeat * WIDE, WIDE), 0) // HEAD_DIM % 2
    col = lax.broadcasted_iota(jnp.int32, (repeat * WIDE, WIDE), 1) // HEAD_DIM
    return jnp.where(row == col, 1.0, 0.0).astype(BF16)


def diagonals(pair, factor):
    low = low_lanes(HEAD_DIM)
    wide = pair.astype(F32) * factor
    turned = pltpu.roll(wide, HEAD_DIM, 1)
    out = []
    for first, second in ((wide, turned), (turned, wide)):
        block = [jnp.where(low, first, 0.0), jnp.where(low, 0.0, second)]
        out.append(jnp.concatenate(block, 0).astype(BF16))
    return out


def segment_max(scores):
    low = low_lanes(scores.shape[0])
    first = jnp.max(jnp.where(low, scores, -jnp.inf), 1, keepdims=True)
    second = jnp.max(jnp.where(low, -jnp.inf, scores), 1, keepdims=True)
    return jnp.where(low, first, second)


def stacked(ref, rows, g):
    at = g * GROUP
    return jnp.concatenate([ref[rows, at : at + WIDE], ref[rows, at + WIDE : at + GROUP]], 0)


def product_of(chip, rows_ref, rows, shifts, weights):
    depth = weights[0].shape[0]
    out = []
    for part in range(2):
        total = None
        for k, s in enumerate(shifts):
            start = pl.multiple_of((chip ^ s) * depth, depth)
            x = mm(rows_ref[rows, pl.ds(start, depth)], weights[2 * k + part][...])
            total = x if total is None else total + x
        out.append(total)
    return out


def partial_kernel(shifts, step, where_ref, rows_ref, before_ref, *refs):
    weights, out_ref = refs[:-1], refs[-1]
    part = weights[0].shape[1]
    for i in range(rows_ref.shape[0] // step):
        rows = slice(i * step, (i + 1) * step)
        a, b = product_of(where_ref[0], rows_ref, rows, shifts, weights)
        out_ref[rows, :part] = a + before_ref[rows, :part]
        out_ref[rows, part:] = b + before_ref[rows, part:]


def forward_kernel(shifts, groups, batch, where_ref, rows_ref, before_ref, *refs):
    weights, refs = refs[: 2 * len(shifts)], refs[2 * len(shifts) :]
    projected_ref, probs_ref, sum_ref = refs
    part = weights[0].shape[1]
    ones = ones_block(1)
    width_q = groups * GROUP
    width_k = groups * HEAD_DIM
    step = batch * PASSAGE_LEN
    for n in range(rows_ref.shape[0] // step):
        rows = slice(n * step, (n + 1) * step)
        a, b = product_of(where_ref[0], rows_ref, rows, shifts, weights)
        projected_ref[rows, :part] = (a + before_ref[rows, :part]).astype(BF16)
        projected_ref[rows, part:] = (b + before_ref[rows, part:]).astype(BF16)
        spans = [
            slice(n * step + i * PASSAGE_LEN, n * step + (i + 1) * PASSAGE_LEN)
            for i in range(batch)
        ]
        keys = [diagonals(projected_ref[r, width_q : width_q + width_k], scale) for r in spans]
        values = [diagonals(projected_ref[r, width_q + width_k :], 1.0) for r in spans]
        for g in range(groups):
            scores = [
                mm(stacked(projected_ref, r, g), keys[i][g], ((1,), (1,)))
                for i, r in enumerate(spans)
            ]
            scores = jnp.concatenate(scores, 0)
            expo = jnp.exp(scores - segment_max(scores))
            total = mm(expo.astype(BF16), ones)
            probs = (expo / total).astype(BF16)
            probs_ref[n, g] = probs
            for i in range(batch):
                attended = mm(probs[i * WIDE : (i + 1) * WIDE], values[i][g])
                attended = attended.astype(BF16).astype(F32)
                for j in range(2):
                    at = g * GROUP + j * WIDE
                    sum_ref[n, i : i + 1, at : at + WIDE] = jnp.sum(
                        attended[j * HEAD_DIM : (j + 1) * HEAD_DIM], 0, keepdims=True
                    )


def row_step(total, batch):
    batch = batch if total % (batch * PASSAGE_LEN) == 0 else 1
    return batch, batch * PASSAGE_LEN


def local_call(kernel, name, micros, where, operands, out_shape):
    vmem = pl.BlockSpec(memory_space=pltpu.VMEM)
    return pl.pallas_call(
        kernel,
        in_specs=[pl.BlockSpec(memory_space=pltpu.SMEM)] + [vmem] * len(operands),
        out_specs=jax.tree.map(lambda _: vmem, out_shape),
        out_shape=out_shape,
        compiler_params=pltpu.CompilerParams(vmem_limit_bytes=VMEM),
        cost_estimate=cost(micros),
        name=name,
    )(where, *operands)


def partial_project(where, rows, weights, before):
    _, step = row_step(rows.shape[0], BATCH)
    return local_call(
        functools.partial(partial_kernel, tuple(weights), step),
        "project_more",
        4.5,
        where,
        [rows, before] + [x for s in weights for x in weights[s]],
        jax.ShapeDtypeStruct(before.shape, F32),
    )


def forward(where, rows, weights, groups, before):
    total = rows.shape[0]
    batch, step = row_step(total, BATCH)
    steps = total // step
    heads = groups * GROUP
    return local_call(
        functools.partial(forward_kernel, tuple(weights), groups, batch),
        "project_attend",
        6.5,
        where,
        [rows, before] + [x for s in weights for x in weights[s]],
        [
            jax.ShapeDtypeStruct(before.shape, BF16),
            jax.ShapeDtypeStruct((steps, groups, batch * WIDE, WIDE), BF16),
            jax.ShapeDtypeStruct((steps, batch, heads), F32),
        ],
    )


def backward_kernel(groups, where_ref, probs_ref, projected_ref, d_ref, out_ref):
    for n in range(probs_ref.shape[0]):
        backward_step(groups, n, probs_ref, projected_ref, d_ref, out_ref)


def backward_step(groups, n, probs_ref, projected_ref, d_ref, out_ref):
    low = low_lanes(HEAD_DIM)
    ones = ones_block(2)
    width_q = groups * GROUP
    width_k = groups * HEAD_DIM
    count = d_ref.shape[1]
    at = n * count
    spans = [slice((at + i) * PASSAGE_LEN, (at + i + 1) * PASSAGE_LEN) for i in range(count)]
    keys = [diagonals(projected_ref[r, width_q : width_q + width_k], scale) for r in spans]
    values = [diagonals(projected_ref[r, width_q + width_k :], 1.0) for r in spans]
    down = ((0,), (0,))
    d_keys = [[] for _ in spans]
    d_values = [[] for _ in spans]

    def fold(product):
        kept = jnp.where(low, product[:HEAD_DIM], product[HEAD_DIM:])
        return kept + pltpu.roll(kept, HEAD_DIM, 1)

    for g in range(groups):
        probs = probs_ref[n, g]
        d_rows = []
        for i in range(count):
            row = [
                d_ref[n, i : i + 1, g * GROUP + j * WIDE : g * GROUP + (j + 1) * WIDE]
                for j in range(2)
            ]
            d_rows.append(
                jnp.concatenate(
                    [jnp.broadcast_to(x, (HEAD_DIM, WIDE)) for x in row], 0
                ).astype(BF16)
            )
        d_probs = jnp.concatenate(
            [mm(d_rows[i], values[i][g], ((1,), (1,))) for i in range(count)], 0
        )
        probs_f = probs.astype(F32)
        product = probs_f * d_probs
        upper = product.astype(BF16)
        lower = (product - upper.astype(F32)).astype(BF16)
        inner = mm(jnp.concatenate([upper, lower], 1), ones)
        d_scores = (probs_f * (d_probs - inner)).astype(BF16)
        for i, r in enumerate(spans):
            block = slice(i * WIDE, (i + 1) * WIDE)
            d_query = mm(d_scores[block], keys[i][g]).astype(BF16)
            at = g * GROUP
            out_ref[r, at : at + WIDE] = d_query[:HEAD_DIM]
            out_ref[r, at + WIDE : at + GROUP] = d_query[HEAD_DIM:]
            d_keys[i].append(fold(mm(d_scores[block], stacked(projected_ref, r, g), down)) * scale)
            d_values[i].append(fold(mm(probs[block], d_rows[i], down)))
    for i, r in enumerate(spans):
        out_ref[r, width_q : width_q + width_k] = jnp.where(low, *d_keys[i]).astype(BF16)
        out_ref[r, width_q + width_k :] = jnp.where(low, *d_values[i]).astype(BF16)


def backward(where, probs, projected, d_attended, groups):
    steps = probs.shape[0]
    batch = probs.shape[2] // WIDE
    return local_call(
        functools.partial(backward_kernel, groups),
        "attend_back",
        3.4,
        where,
        [probs, projected, d_attended.reshape(steps, batch, groups * GROUP)],
        jax.ShapeDtypeStruct(projected.shape, BF16),
    )


def score_kernel(chips, where_ref, own_ref, sib_ref, own_far_ref, sib_far_ref, sum_ref, sib_sum_ref,
                 final_ref, ws_ref, prior_ref, prior_sib_ref, *refs):
    pieces, refs = refs[: 4 * chips], refs[4 * chips :]
    score_ref, attn_ref, d_att_ref, d_rows_ref, product_ref = refs
    chip, core = where_ref[0], where_ref[1]
    mine = jnp.concatenate([own_ref[...], sib_ref[...]], 0)
    other = jnp.concatenate([own_far_ref[...], sib_far_ref[...]], 0)
    sums = [ref[k] for ref in (sum_ref, sib_sum_ref) for k in range(ref.shape[0])]
    attn = jnp.concatenate(
        [jnp.where(core == 0, mine, other), jnp.where(core == 0, other, mine)], 1
    )
    count = attn.shape[0]
    upper = attn.astype(BF16)
    attn_ref[...] = upper
    both = jnp.concatenate([upper.astype(F32), attn - upper.astype(F32)], 0)
    product_ref[...] = both
    depth, part = pieces[0].shape
    out = [None] * 4
    for s in range(chips):
        start = pl.multiple_of((chip ^ s) * depth, depth)
        block = product_ref[:, pl.ds(start, depth)].astype(BF16)
        for k in range(4):
            x = mm(block, pieces[4 * s + k][...])
            out[k] = x if out[k] is None else out[k] + x
    out = [x[:count] + x[count:] for x in out]
    own, far = jnp.concatenate(out[:2], 1), jnp.concatenate(out[2:], 1)
    product = jnp.concatenate(
        [jnp.where(core == 0, own, far), jnp.where(core == 0, far, own)], 1
    )
    pooled = (jnp.concatenate(sums, 0) + product) * (1.0 / PASSAGE_LEN)
    inverse = lax.rsqrt(jnp.mean(pooled * pooled, -1, keepdims=True) + epsilon)
    unit = pooled * inverse
    direction = final_ref[...] * ws_ref[...]
    score = jnp.sum(unit * direction, -1, keepdims=True)
    lane = lax.broadcasted_iota(jnp.int32, score_ref.shape, 1)
    half = score_ref.shape[1] // 2
    prior = jnp.concatenate([prior_ref[...], prior_sib_ref[...]], 0)
    score_ref[...] = jnp.where(lane < half, score, 0.0) + prior

    mean = jnp.mean(unit * direction, -1, keepdims=True)
    d_rows = inverse * (direction - unit * mean) * (1.0 / PASSAGE_LEN)
    half = d_rows.shape[1] // 2
    own = jnp.where(core == 0, d_rows[:, :half], d_rows[:, half:])
    far = jnp.where(core == 0, d_rows[:, half:], d_rows[:, :half])
    d_rows_ref[...] = own
    cut = [x.astype(BF16) for x in (own[:, :part], own[:, part:], far[:, :part], far[:, part:])]
    for s in range(chips):
        back = sum(mm(cut[k], pieces[4 * s + k][...], ((1,), (1,))) for k in range(4))
        start = pl.multiple_of((chip ^ s) * depth, depth)
        product_ref[:count, pl.ds(start, depth)] = back.astype(BF16).astype(F32)
    back = product_ref[:count]
    half = back.shape[1] // 2
    d_att_ref[...] = jnp.where(core == 0, back[:, :half], back[:, half:])


def score_pass(where, attn, sums, final_gain, w_score, priors, pieces):
    count, width = 2 * attn[0].shape[0], sums[0].shape[2]
    lanes = priors[0].shape[1]
    inner = 2 * attn[0].shape[1]
    vmem = pl.BlockSpec(memory_space=pltpu.VMEM)
    return pl.pallas_call(
        functools.partial(score_kernel, len(pieces) // 4),
        in_specs=[pl.BlockSpec(memory_space=pltpu.SMEM)] + [vmem] * (10 + len(pieces)),
        out_specs=[vmem] * 4,
        out_shape=[
            jax.ShapeDtypeStruct((count, lanes), F32),
            jax.ShapeDtypeStruct((count, inner), BF16),
            jax.ShapeDtypeStruct((count, inner // 2), F32),
            jax.ShapeDtypeStruct((count, width // 2), F32),
        ],
        scratch_shapes=[pltpu.VMEM((2 * count, inner), F32)],
        compiler_params=pltpu.CompilerParams(vmem_limit_bytes=SMALL),
        cost_estimate=cost(2),
        name="pool_score",
    )(where, *attn, *sums, final_gain[None], w_score[None], *priors, *pieces)


def list_kernel(blocks, passages, where_ref, place_ref, bounds_ref, rows_ref, own_ref, sib_ref,
                *refs):
    scores = [ref[...] for ref in refs[:blocks]]
    d_rows_ref, loss_ref, d_own_ref, d_sib_ref = refs[blocks:]
    core = where_ref[1]
    pair = 2 * passages
    lanes = bounds_ref.shape[1]
    lane = lax.broadcasted_iota(jnp.int32, bounds_ref.shape, 1)
    ends, reach = bounds_ref[...], 1
    while reach < lanes:
        ends = ends + jnp.where(lane >= reach, pltpu.roll(ends, reach, 1), 0)
        reach *= 2
    starts, ends = (ends - bounds_ref[...])[:1], ends[:1]
    row = lax.broadcasted_iota(jnp.int32, (pair, lanes), 0)
    near = jnp.where(row < passages, core * passages + row, (1 - core) * passages + row - passages)
    far = jnp.where(row < passages, (1 - core) * passages + row, core * passages + row - passages)
    members = []
    for j in range(blocks):
        place = place_ref[j] * pair + (near if j <= blocks // 2 else far)
        members.append((place >= starts) & (place < ends))
    high = scores[0].shape[1] // 2
    column = [jnp.broadcast_to(score[:, :1], (pair, lanes)) for score in scores]
    heavy = [jnp.broadcast_to(score[:, high : high + 1], (pair, lanes)) for score in scores]
    peak = functools.reduce(
        jnp.maximum,
        [jnp.max(jnp.where(m, s, -1e30), 0, keepdims=True) for m, s in zip(members, column)],
    )
    total = sum(
        jnp.sum(jnp.where(m, jnp.exp(jnp.where(m, s - peak, 0.0)), 0.0), 0, keepdims=True)
        for m, s in zip(members, column)
    )
    label_total = sum(
        jnp.sum(jnp.where(m, w, 0.0), 0, keepdims=True) for m, w in zip(members, heavy)
    )
    log_norm = peak + jnp.log(total)
    own = members[0]
    log_prob = column[0][:, :1] - jnp.sum(jnp.where(own, log_norm, 0.0), 1, keepdims=True)
    target = heavy[0][:, :1] / jnp.sum(jnp.where(own, label_total, 0.0), 1, keepdims=True)
    loss = -loss_scale * jnp.sum((target * log_prob)[:passages], 0, keepdims=True)
    d_score = loss_scale * (jnp.exp(log_prob) - target)
    loss_ref[...] = jnp.broadcast_to(loss, loss_ref.shape)
    d_rows_ref[...] = (rows_ref[...] * d_score).astype(BF16)
    for k, (ref, out_ref) in enumerate(((own_ref, d_own_ref), (sib_ref, d_sib_ref))):
        for i in range(passages):
            rows = slice(i * PASSAGE_LEN, (i + 1) * PASSAGE_LEN)
            at = k * passages + i
            out_ref[rows] = (ref[rows].astype(F32) * d_score[at : at + 1]).astype(BF16)


def list_pass(where, places, bounds, rows, d_own, d_sib, scores):
    vmem = pl.BlockSpec(memory_space=pltpu.VMEM)
    smem = pl.BlockSpec(memory_space=pltpu.SMEM)
    return pl.pallas_call(
        functools.partial(list_kernel, len(scores), rows.shape[0] // 2),
        in_specs=[smem] * 2 + [vmem] * (4 + len(scores)),
        out_specs=[vmem] * 4,
        out_shape=[
            jax.ShapeDtypeStruct(rows.shape, BF16),
            jax.ShapeDtypeStruct((8, 128), F32),
            jax.ShapeDtypeStruct(d_own.shape, BF16),
            jax.ShapeDtypeStruct(d_sib.shape, BF16),
        ],
        compiler_params=pltpu.CompilerParams(vmem_limit_bytes=SMALL),
        cost_estimate=cost(2.5),
        name="list_grad",
    )(where, places, bounds, rows, d_own, d_sib, *scores)


def payload_kernel(passages, where_ref, attn_ref, d_rows_ref, loss_ref, out_ref):
    core = where_ref[1]
    attn = attn_ref[...].astype(F32)
    half = attn.shape[1] // 2
    columns = [jnp.where(core == 0, attn[:, :half], attn[:, half:]), d_rows_ref[...].astype(F32)]
    rest = jnp.broadcast_to(loss_ref[:1], (attn.shape[0], 128))
    for _ in range(3):
        columns.append(rest.astype(BF16).astype(F32))
        rest = rest - columns[-1]
    columns = jnp.concatenate(columns, 1)
    turned = jnp.concatenate([columns[passages:], columns[:passages]], 0)
    out_ref[...] = jnp.where(core == 0, columns, turned).astype(BF16)


def payload_pass(where, attn, d_rows, loss):
    count = attn.shape[0]
    vmem = pl.BlockSpec(memory_space=pltpu.VMEM)
    return pl.pallas_call(
        functools.partial(payload_kernel, count // 2),
        in_specs=[pl.BlockSpec(memory_space=pltpu.SMEM)] + [vmem] * 3,
        out_specs=vmem,
        out_shape=jax.ShapeDtypeStruct(
            (count, attn.shape[1] // 2 + d_rows.shape[1] + 3 * 128), BF16
        ),
        compiler_params=pltpu.CompilerParams(vmem_limit_bytes=SMALL),
        cost_estimate=cost(1),
        name="out_payload",
    )(where, attn, d_rows, loss)


EXTRA = 16


def out_kernel(chips, where_ref, left_ref, *refs):
    near, far, out_ref = refs[:chips], refs[chips], refs[chips + 1]
    core = where_ref[1]
    cols = out_ref.shape[1] // 2
    own_rows = out_ref.shape[0] - EXTRA
    lead = far.shape[1] - 3 * 128 - cols
    mine = jnp.concatenate([ref[...] for ref in near], 0)
    other = far[...]
    down = ((0,), (0,))
    products = [mm(left_ref[...], x[:, lead : lead + cols], down) for x in (mine, other)]
    out_ref[:own_rows, :cols] = jnp.where(core == 0, *products).astype(BF16)
    out_ref[:own_rows, cols:] = jnp.where(core == 0, *products[::-1]).astype(BF16)

    count = mine.shape[0] // chips
    losses = []
    for s in range(chips):
        total = 0.0
        for x in (mine, other):
            row = x[s * count : s * count + EXTRA, lead + cols :].astype(F32)
            total = total + (row[:, :128] + row[:, 128:256] + row[:, 256:])
        losses.append(total)
    while len(losses) > 1:
        losses = [a + b for a, b in zip(losses[0::2], losses[1::2])]
    rest = losses[0]
    parts = []
    for _ in range(3):
        parts.append(rest.astype(BF16).astype(F32))
        rest = rest - parts[-1]
    index = lax.broadcasted_iota(jnp.int32, rest.shape, 0)
    row = jnp.where(index == 0, parts[0], jnp.where(index == 1, parts[1], parts[2])).astype(BF16)
    out_ref[own_rows:] = jnp.concatenate([row] * (2 * cols // row.shape[1]), 1)


def total_kernel(*refs):
    blocks, (out_ref, loss_ref) = refs[:-2], refs[-2:]
    own_rows = out_ref.shape[0]
    out_ref[...] = sum(ref[:own_rows].astype(F32) for ref in blocks)
    losses = []
    for ref in blocks:
        rows = ref[own_rows:].astype(F32)
        losses.append(rows[0:1] + rows[1:2] + rows[2:3])
    while len(losses) > 1:
        losses = [a + b for a, b in zip(losses[0::2], losses[1::2])]
    loss_ref[...] = jnp.broadcast_to(losses[0][:, :128], loss_ref.shape)


def total_pass(blocks):
    vmem = pl.BlockSpec(memory_space=pltpu.VMEM)
    rows, width = blocks[0].shape
    return pl.pallas_call(
        total_kernel,
        in_specs=[vmem] * len(blocks),
        out_specs=[vmem] * 2,
        out_shape=[
            jax.ShapeDtypeStruct((rows - EXTRA, width), F32),
            jax.ShapeDtypeStruct((8, 128), F32),
        ],
        compiler_params=pltpu.CompilerParams(vmem_limit_bytes=SMALL),
        cost_estimate=cost(1),
        name="out_total",
    )(*blocks)


def out_pass(where, left, near, far, cols):
    vmem = pl.BlockSpec(memory_space=pltpu.VMEM)
    return pl.pallas_call(
        functools.partial(out_kernel, len(near)),
        in_specs=[pl.BlockSpec(memory_space=pltpu.SMEM)] + [vmem] * (2 + len(near)),
        out_specs=vmem,
        out_shape=jax.ShapeDtypeStruct((left.shape[1] + EXTRA, 2 * cols), BF16),
        compiler_params=pltpu.CompilerParams(vmem_limit_bytes=SMALL),
        cost_estimate=cost(1),
        name="out_rows",
    )(where, left, *near, far)


def grad_kernel(blocks, where_ref, own_ref, sib_ref, d_own_ref, d_sib_ref, *refs):
    out, (rows_ref, done) = refs[:-2], refs[-2:]
    depth, part = out[0].shape
    tile = min(depth, 256)
    down = ((0,), (0,))
    copies = []
    for n, s in enumerate(blocks):
        start = pl.multiple_of((where_ref[0] ^ s) * depth, depth)
        for k, ref in enumerate((own_ref, sib_ref)):
            copy = pltpu.make_async_copy(
                ref.at[:, pl.ds(start, depth)], rows_ref.at[n, k], done.at[n, k]
            )
            copy.start()
            copies.append(copy)
    for n in range(len(blocks)):
        copies[2 * n].wait()
        copies[2 * n + 1].wait()
        for i in range(depth // tile):
            cols = slice(i * tile, (i + 1) * tile)
            total = mm(rows_ref[n, 0, :, cols], d_own_ref[...], down)
            total = (total + mm(rows_ref[n, 1, :, cols], d_sib_ref[...], down)).astype(BF16)
            out[2 * n][cols] = total[:, :part]
            out[2 * n + 1][cols] = total[:, part:]


def grad_blocks(where, blocks, own, sib, d_own, d_sib, depth):
    part = d_own.shape[1] // 2
    count = len(blocks)
    vmem = pl.BlockSpec(memory_space=pltpu.VMEM)
    hbm = pl.BlockSpec(memory_space=pltpu.HBM)
    return pl.pallas_call(
        functools.partial(grad_kernel, tuple(blocks)),
        in_specs=[pl.BlockSpec(memory_space=pltpu.SMEM), hbm, hbm, vmem, vmem],
        out_specs=[vmem] * (2 * count),
        out_shape=[jax.ShapeDtypeStruct((depth, part), BF16)] * (2 * count),
        scratch_shapes=[
            pltpu.VMEM((count, 2, own.shape[0], depth), BF16),
            pltpu.SemaphoreType.DMA((count, 2)),
        ],
        compiler_params=pltpu.CompilerParams(vmem_limit_bytes=VMEM),
        cost_estimate=cost(2.5 * count),
        name="grad_rows",
    )(where, *held(pltpu.HBM, own, sib), d_own, d_sib)


def pick_kernel(starts, sizes, where_ref, mine_ref, come_ref, a_ref, b_ref):
    core = where_ref[1]
    mine, come = mine_ref[...].astype(F32), come_ref[...].astype(F32)
    rows = mine.shape[0]
    halves = []
    for h in range(2):
        spans = [slice(a + h * n, a + (h + 1) * n) for a, n in zip(starts, sizes)]
        halves.append([jnp.concatenate([x[:, t] for t in spans], 1) for x in (mine, come)])
    first = jnp.where(core == 0, halves[0][0], halves[1][1]).astype(BF16)
    second = jnp.where(core == 0, halves[0][1], halves[1][0]).astype(BF16)
    part = a_ref.shape[1]
    a_ref[:rows], b_ref[:rows] = first[:, :part], first[:, part:]
    a_ref[rows:], b_ref[rows:] = second[:, :part], second[:, part:]


def pick(where, mine, come, starts, sizes):
    rows = mine.shape[0]
    vmem = pl.BlockSpec(memory_space=pltpu.VMEM)
    return pl.pallas_call(
        functools.partial(pick_kernel, starts, sizes),
        in_specs=[pl.BlockSpec(memory_space=pltpu.SMEM), vmem, vmem],
        out_specs=[vmem] * 2,
        out_shape=[jax.ShapeDtypeStruct((2 * rows, sum(sizes) // 2), BF16)] * 2,
        compiler_params=pltpu.CompilerParams(vmem_limit_bytes=SMALL),
        cost_estimate=cost(1),
        name="pick_columns",
    )(where, mine, come)


def solution(mesh):
    n_list, n_fsdp = mesh.shape["list"], mesh.shape["fsdp"]
    bits = [1 << k for k in range(1, n_fsdp.bit_length() - 1)]
    pairs = n_list * n_fsdp // 2

    def across(value, distance):
        return lax.ppermute(value, "fsdp", [(i, i ^ distance) for i in range(n_fsdp)])

    def along(value, distance):
        return lax.ppermute(value, "list", [(i, i ^ distance) for i in range(n_list)])

    def partner(kind, pair):
        return (
            pair ^ 1,
            ((pair + 1) ^ 1) - 1,
            pair ^ 2,
            ((pair + 2) ^ 2) - 2,
        )[kind]

    def neighbour(value, kind):
        moves = []
        for pair in range(pairs):
            for core in (0, 1):
                other = partner(kind + core, pair)
                if 0 <= other < pairs:
                    moves.append((2 * pair + core, 2 * other + core))
        return lax.ppermute(value, ("list", "fsdp"), moves)

    def after(value, *others):
        return lax.optimization_barrier((value, others))[0]

    def gathered(value, order, far=(), wait=True):
        have = {0: value}
        for bit in order:
            first = [part for s, part in have.items() if s]
            ready = dict(have)
            if first:
                ready = {
                    s: after(part, far, first) if s else after(part, first) if wait else part
                    for s, part in have.items()
                }
            have.update({s ^ (bit >> 1): across(part, bit) for s, part in ready.items()})
        return have

    def joined(parts, come, bit):
        return {
            s: (parts[s].astype(F32) + come[s].astype(F32)).astype(BF16)
            for s in parts
            if not s & (bit >> 1)
        }

    def sent(parts, bit):
        flag = bit >> 1
        return {s ^ flag: across(parts[s], bit) for s in sorted(parts)[::-1] if s & flag}

    def local(hidden, norm_gain, w_qkv, w_out, final_gain, w_score, prior, labels, lengths):
        passages, _, width = hidden.shape
        assert 4 * passages >= LONGEST - 1
        groups = KV_HEADS // 2
        width_q, width_k = groups * GROUP, groups * HEAD_DIM
        index = lax.axis_index("fsdp")
        core = index % 2
        chip = index // 2
        where = jnp.stack([chip, core]).astype(jnp.int32)
        first_core = core == 0

        def ordered(mine, other, axis):
            return jnp.where(
                first_core,
                jnp.concatenate([mine, other], axis),
                jnp.concatenate([other, mine], axis),
            )

        starts = (0, 2 * width_q, 2 * (width_q + width_k))
        sizes = (width_q, width_k, width_k)
        come = across(w_qkv, 1)
        pair_a, pair_b = pick(where, w_qkv, come, starts, sizes)
        w_out = after(w_out, come)
        out_come = across(w_out, 1)
        hidden_sib = across(after(hidden, come), 1)

        normal, sums, before_own = norm(where, hidden, norm_gain, (pair_a, pair_b))
        prior, labels, lengths, out_come = after((prior, labels, lengths, out_come), before_own)
        lanes = -(-lengths.shape[0] // 128) * 128
        label_weight = jnp.exp(labels.astype(F32))
        small = jnp.concatenate(
            [jnp.broadcast_to(x[:, None], (passages, 64)) for x in (prior, label_weight)], 1
        )
        small_sib = across(small, 1)
        pair = lax.axis_index("list") * (n_fsdp // 2) + chip
        places = [pair] + [
            jnp.where(first_core == near, partner(2 * kind, pair), partner(2 * kind + 1, pair))
            for near in (True, False)
            for kind in range(2)
        ]
        places = jnp.stack(places).astype(jnp.int32)
        bounds = jnp.broadcast_to(
            jnp.pad(lengths, (0, lanes - lengths.shape[0]))[None], (8, lanes)
        )

        cols = w_out.shape[1] // 2
        both = ordered(w_out, out_come, 0)
        out_pair = jnp.where(first_core, both[:, :cols], both[:, cols:])
        normal_sib, sums_sib, before_sib = norm(
            where,
            after(hidden_sib, before_own, places, bounds, small_sib, out_pair),
            norm_gain,
            (pair_a, pair_b),
        )
        part_a = gathered(pair_a, bits, far=before_own)
        part_b = gathered(pair_b, bits[::-1], far=before_own)
        chips = n_fsdp // 2
        last = max(bin(s).count("1") for s in range(chips))
        weights = [{}, {}, {}]
        for s in range(chips):
            ones = bin(s).count("1")
            weights[2 if ones == last else 1 if ones else 0][s] = (part_a[s], part_b[s])

        out_pair = after(out_pair, weights[1], before_sib)
        if weights[1]:
            normal_first = after(normal, before_sib)
            before_own = partial_project(where, normal_first, weights[1], before_own)
            before_sib = partial_project(
                where, after(normal_sib, before_own), weights[1], before_sib
            )
        before_own, before_sib, weights[2] = after(
            (before_own, before_sib, weights[2]), before_sib
        )
        proj_sib, probs_sib, attn_sib = forward(where, normal_sib, weights[2], groups, before_sib)
        attn_sib = attn_sib.reshape(passages, -1)
        attn_sib_other = across(attn_sib, 1)
        normal_last = after(normal, probs_sib)
        proj_own, probs_own, attn_own = forward(where, normal_last, weights[2], groups, before_own)
        attn_own = attn_own.reshape(passages, -1)
        attn_own_other = across(attn_own, 1)
        out_a = gathered(out_pair[:, : cols // 2], bits, before_sib, False)
        out_b = gathered(out_pair[:, cols // 2 :], bits[::-1], before_sib, False)
        pieces = []
        for s in range(chips):
            pieces += [out_a[s], out_b[s]]
            gate = probs_own
            pieces += [across(after(x, gate), 1) for x in (out_a[s], out_b[s])]
        score, attn, d_attended, direction = score_pass(
            where,
            (attn_own, attn_sib, attn_sib_other, attn_own_other),
            (sums, sums_sib),
            final_gain,
            w_score,
            (small, small_sib),
            pieces,
        )
        near = [neighbour(score, kind) for kind in (0, 2)]
        scores = [score] + near + [across(x, 1) for x in near]
        d_own = backward(where, probs_own, proj_own, d_attended[:passages], groups)
        d_sib = backward(
            where, after(probs_sib, d_own), proj_sib, d_attended[passages:], groups
        )
        d_rows, loss_part, d_own, d_sib = list_pass(
            where, places, bounds, direction, d_own, d_sib, scores
        )
        inner = attn.shape[1]
        payload = payload_pass(where, attn, d_rows, loss_part)
        depth = pair_a.shape[0]
        flag_a, flag_b = bits[0] >> 1, bits[-1] >> 1
        lead = [s for s in range(chips) if s & flag_a and s & flag_b]
        rest = [s for s in range(1, chips) if s not in lead]

        def grads(blocks, *gate):
            out = grad_blocks(where, blocks, normal, normal_sib, d_own, after(d_sib, gate), depth)
            return dict(zip(blocks, out[0::2])), dict(zip(blocks, out[1::2]))

        parts_a, parts_b = grads(lead)
        first_a = {s ^ flag_a: across(parts_a[s], bits[0]) for s in lead}
        first_b = {s ^ flag_b: across(parts_b[s], bits[-1]) for s in lead}
        plane = [payload] + [across(payload, 2 * s) for s in range(1, chips)]
        more_a, more_b = grads(rest, parts_a, plane)
        far = across(jnp.concatenate(plane, 0), 1)
        for s in rest:
            if s & flag_a:
                first_a[s ^ flag_a] = across(more_a[s], bits[0])
            if s & flag_b:
                first_b[s ^ flag_b] = across(more_b[s], bits[-1])
        own_a, own_b = grads([0], more_a, first_a, first_b, far)
        parts_a.update(more_a)
        parts_b.update(more_b)
        parts_a.update(own_a)
        parts_b.update(own_b)
        left_a, left_b = joined(parts_a, first_a, bits[0]), joined(parts_b, first_b, bits[-1])
        place = lax.axis_index("list")
        inner = 2 * width_q
        left = ordered(
            jnp.concatenate([x[:, :width_q] for x in plane], 0), far[:, :width_q], 1
        )
        own_rows = inner // n_fsdp
        left = lax.dynamic_slice_in_dim(left, index * own_rows, own_rows, 1)
        rows = out_pass(where, left, plane, far, cols)
        blocks = rows.shape[1] // n_list
        block = lambda which: lax.dynamic_slice_in_dim(rows, which * blocks, blocks, 1)
        come_out = [block(place)]
        come_out += [along(block(place ^ distance), distance) for distance in range(1, n_list)]
        for bit_a, bit_b in zip(bits[1:], bits[::-1][1:]):
            far_a, far_b = after((sent(left_a, bit_a), sent(left_b, bit_b)), come_out)
            left_a, left_b = joined(left_a, far_a, bit_a), joined(left_b, far_b, bit_b)
        sum_a, sum_b = left_a[0], left_b[0]
        chip_sum = jnp.concatenate([sum_a, sum_b], 1)
        upper, lower = chip_sum[: depth // 2], chip_sum[depth // 2 :]
        keep = jnp.where(first_core, upper, lower)
        come = across(jnp.where(first_core, lower, upper), 1)
        columns = []
        at = 0
        for n in sizes:
            columns.append(ordered(keep[:, at : at + n], come[:, at : at + n], 1))
            at += n
        rows_sum = jnp.concatenate(columns, 1)
        place = lax.axis_index("list")

        def list_scatter(value):
            n = value.shape[1] // n_list
            block = lambda which: lax.dynamic_slice_in_dim(value, which * n, n, 1)
            total = block(place).astype(F32)
            for distance in range(1, n_list):
                total = total + along(block(place ^ distance).astype(BF16), distance).astype(F32)
            return total

        grad_qkv = list_scatter(rows_sum)

        grad_out, losses = total_pass(come_out)
        return (losses[0, 0], grad_qkv, grad_out)

    placed = (
        P(("list", "fsdp"), None, None),
        P(),
        P("fsdp", None),
        P("fsdp", None),
        P(),
        P(),
        P(("list", "fsdp")),
        P(("list", "fsdp")),
        P(),
    )
    return jax.shard_map(
        local,
        mesh=mesh,
        in_specs=placed,
        out_specs=(P(), P("fsdp", "list"), P("fsdp", "list")),
        check_vma=False,
    )
```

```python
import functools

import jax
import jax.numpy as jnp
from jax import lax
from jax.experimental import pallas as pl
from jax.experimental.pallas import tpu as pltpu
from jax.sharding import PartitionSpec as P

HEADS = 16
KV_HEADS = 4
HEAD_DIM = 64
PASSAGE_LEN = 64
LONGEST = 48
RATIO = HEADS // KV_HEADS
GROUP = RATIO * HEAD_DIM

epsilon = 1e-05
loss_scale = 64.0
scale = HEAD_DIM ** (-0.5)
VMEM = 14 * 1024 * 1024
SMALL = 6 * 1024 * 1024


def cost(micros):
    return pl.CostEstimate(flops=int(micros * 5e8), bytes_accessed=int(micros * 3.5e6), transcendentals=0)

BF16 = jnp.bfloat16
F32 = jnp.float32


def params(grid=1):
    return pltpu.CompilerParams(
        vmem_limit_bytes=VMEM, dimension_semantics=("arbitrary",) * grid
    )


def held(space, *values):
    return [pltpu.with_memory_space_constraint(x, space) for x in values]


def mm(a, b, dims=((1,), (0,))):
    return lax.dot_general(a, b, (dims, ((), ())), preferred_element_type=F32)


def norm_kernel(where_ref, hidden_ref, gain_ref, a_ref, b_ref, normal_ref, sum_ref, out_ref):
    values = hidden_ref[...].astype(F32)
    mean_square = jnp.mean(values * values, -1, keepdims=True)
    out = values * lax.rsqrt(mean_square + epsilon) * gain_ref[...][None]
    normal_ref[...] = out.reshape(normal_ref.shape).astype(BF16)
    sum_ref[0] = jnp.sum(values, 1)
    depth, part = a_ref.shape
    start = pl.multiple_of(where_ref[0] * depth, depth)
    block = normal_ref[:, pl.ds(start, depth)]
    out_ref[:, :part] = mm(block, a_ref[...])
    out_ref[:, part:] = mm(block, b_ref[...])


def norm(where, hidden, gain, weights):
    passages, length, width = hidden.shape
    depth, part = weights[0].shape
    step = 4 if passages % 4 == 0 else 1
    steps = passages // step
    whole = lambda i, w: (0, 0)
    normal, sums, product = pl.pallas_call(
        norm_kernel,
        grid_spec=pltpu.PrefetchScalarGridSpec(
            num_scalar_prefetch=1,
            grid=(steps,),
            in_specs=[
                pl.BlockSpec((step, length, width), lambda i, w: (i, 0, 0)),
                pl.BlockSpec((1, width), whole),
                pl.BlockSpec((depth, part), whole),
                pl.BlockSpec((depth, part), whole),
            ],
            out_specs=[
                pl.BlockSpec((step * length, width), lambda i, w: (i, 0)),
                pl.BlockSpec((1, step, width), lambda i, w: (i, 0, 0)),
                pl.BlockSpec((step * length, 2 * part), lambda i, w: (i, 0)),
            ],
        ),
        out_shape=[
            pltpu.VMEM((passages * length, width), BF16),
            jax.ShapeDtypeStruct((steps, step, width), F32),
            pltpu.VMEM((passages * length, 2 * part), F32),
        ],
        compiler_params=params(),
        cost_estimate=cost(7),
        name="norm_project",
    )(where, *held(pltpu.HBM, hidden), gain[None], *weights)
    return normal, sums, product


WIDE = 2 * HEAD_DIM
BATCH = 8


def low_lanes(rows):
    return lax.broadcasted_iota(jnp.int32, (rows, WIDE), 1) < HEAD_DIM


def ones_block(repeat):
    row = lax.broadcasted_iota(jnp.int32, (repeat * WIDE, WIDE), 0) // HEAD_DIM % 2
    col = lax.broadcasted_iota(jnp.int32, (repeat * WIDE, WIDE), 1) // HEAD_DIM
    return jnp.where(row == col, 1.0, 0.0).astype(BF16)


def diagonals(pair, factor):
    low = low_lanes(HEAD_DIM)
    wide = pair.astype(F32) * factor
    turned = pltpu.roll(wide, HEAD_DIM, 1)
    out = []
    for first, second in ((wide, turned), (turned, wide)):
        block = [jnp.where(low, first, 0.0), jnp.where(low, 0.0, second)]
        out.append(jnp.concatenate(block, 0).astype(BF16))
    return out


def segment_max(scores):
    low = low_lanes(scores.shape[0])
    first = jnp.max(jnp.where(low, scores, -jnp.inf), 1, keepdims=True)
    second = jnp.max(jnp.where(low, -jnp.inf, scores), 1, keepdims=True)
    return jnp.where(low, first, second)


def stacked(ref, rows, g):
    at = g * GROUP
    return jnp.concatenate([ref[rows, at : at + WIDE], ref[rows, at + WIDE : at + GROUP]], 0)


def product_of(chip, rows_ref, rows, shifts, weights):
    depth = weights[0].shape[0]
    out = []
    for part in range(2):
        total = None
        for k, s in enumerate(shifts):
            start = pl.multiple_of((chip ^ s) * depth, depth)
            x = mm(rows_ref[rows, pl.ds(start, depth)], weights[2 * k + part][...])
            total = x if total is None else total + x
        out.append(total)
    return out


def partial_kernel(shifts, step, where_ref, rows_ref, before_ref, *refs):
    weights, out_ref = refs[:-1], refs[-1]
    part = weights[0].shape[1]
    for i in range(rows_ref.shape[0] // step):
        rows = slice(i * step, (i + 1) * step)
        a, b = product_of(where_ref[0], rows_ref, rows, shifts, weights)
        out_ref[rows, :part] = a + before_ref[rows, :part]
        out_ref[rows, part:] = b + before_ref[rows, part:]


def forward_kernel(shifts, groups, batch, where_ref, rows_ref, before_ref, *refs):
    weights, refs = refs[: 2 * len(shifts)], refs[2 * len(shifts) :]
    projected_ref, probs_ref, sum_ref = refs
    part = weights[0].shape[1]
    ones = ones_block(1)
    width_q = groups * GROUP
    width_k = groups * HEAD_DIM
    step = batch * PASSAGE_LEN
    for n in range(rows_ref.shape[0] // step):
        rows = slice(n * step, (n + 1) * step)
        a, b = product_of(where_ref[0], rows_ref, rows, shifts, weights)
        projected_ref[rows, :part] = (a + before_ref[rows, :part]).astype(BF16)
        projected_ref[rows, part:] = (b + before_ref[rows, part:]).astype(BF16)
        spans = [
            slice(n * step + i * PASSAGE_LEN, n * step + (i + 1) * PASSAGE_LEN)
            for i in range(batch)
        ]
        keys = [diagonals(projected_ref[r, width_q : width_q + width_k], scale) for r in spans]
        values = [diagonals(projected_ref[r, width_q + width_k :], 1.0) for r in spans]
        for g in range(groups):
            scores = [
                mm(stacked(projected_ref, r, g), keys[i][g], ((1,), (1,)))
                for i, r in enumerate(spans)
            ]
            scores = jnp.concatenate(scores, 0)
            expo = jnp.exp(scores - segment_max(scores))
            total = mm(expo.astype(BF16), ones)
            probs = (expo / total).astype(BF16)
            probs_ref[n, g] = probs
            for i in range(batch):
                attended = mm(probs[i * WIDE : (i + 1) * WIDE], values[i][g])
                attended = attended.astype(BF16).astype(F32)
                for j in range(2):
                    at = g * GROUP + j * WIDE
                    sum_ref[n, i : i + 1, at : at + WIDE] = jnp.sum(
                        attended[j * HEAD_DIM : (j + 1) * HEAD_DIM], 0, keepdims=True
                    )


def row_step(total, batch):
    batch = batch if total % (batch * PASSAGE_LEN) == 0 else 1
    return batch, batch * PASSAGE_LEN


def local_call(kernel, name, micros, where, operands, out_shape):
    vmem = pl.BlockSpec(memory_space=pltpu.VMEM)
    return pl.pallas_call(
        kernel,
        in_specs=[pl.BlockSpec(memory_space=pltpu.SMEM)] + [vmem] * len(operands),
        out_specs=jax.tree.map(lambda _: vmem, out_shape),
        out_shape=out_shape,
        compiler_params=pltpu.CompilerParams(vmem_limit_bytes=VMEM),
        cost_estimate=cost(micros),
        name=name,
    )(where, *operands)


def partial_project(where, rows, weights, before):
    _, step = row_step(rows.shape[0], BATCH)
    return local_call(
        functools.partial(partial_kernel, tuple(weights), step),
        "project_more",
        4.5,
        where,
        [rows, before] + [x for s in weights for x in weights[s]],
        jax.ShapeDtypeStruct(before.shape, F32),
    )


def forward(where, rows, weights, groups, before):
    total = rows.shape[0]
    batch, step = row_step(total, BATCH)
    steps = total // step
    heads = groups * GROUP
    return local_call(
        functools.partial(forward_kernel, tuple(weights), groups, batch),
        "project_attend",
        6.5,
        where,
        [rows, before] + [x for s in weights for x in weights[s]],
        [
            jax.ShapeDtypeStruct(before.shape, BF16),
            jax.ShapeDtypeStruct((steps, groups, batch * WIDE, WIDE), BF16),
            jax.ShapeDtypeStruct((steps, batch, heads), F32),
        ],
    )


def backward_kernel(groups, where_ref, probs_ref, projected_ref, d_ref, out_ref):
    for n in range(probs_ref.shape[0]):
        backward_step(groups, n, probs_ref, projected_ref, d_ref, out_ref)


def backward_step(groups, n, probs_ref, projected_ref, d_ref, out_ref):
    low = low_lanes(HEAD_DIM)
    ones = ones_block(2)
    width_q = groups * GROUP
    width_k = groups * HEAD_DIM
    count = d_ref.shape[1]
    at = n * count
    spans = [slice((at + i) * PASSAGE_LEN, (at + i + 1) * PASSAGE_LEN) for i in range(count)]
    keys = [diagonals(projected_ref[r, width_q : width_q + width_k], scale) for r in spans]
    values = [diagonals(projected_ref[r, width_q + width_k :], 1.0) for r in spans]
    down = ((0,), (0,))
    d_keys = [[] for _ in spans]
    d_values = [[] for _ in spans]

    def fold(product):
        kept = jnp.where(low, product[:HEAD_DIM], product[HEAD_DIM:])
        return kept + pltpu.roll(kept, HEAD_DIM, 1)

    for g in range(groups):
        probs = probs_ref[n, g]
        d_rows = []
        for i in range(count):
            row = [
                d_ref[n, i : i + 1, g * GROUP + j * WIDE : g * GROUP + (j + 1) * WIDE]
                for j in range(2)
            ]
            d_rows.append(
                jnp.concatenate(
                    [jnp.broadcast_to(x, (HEAD_DIM, WIDE)) for x in row], 0
                ).astype(BF16)
            )
        d_probs = jnp.concatenate(
            [mm(d_rows[i], values[i][g], ((1,), (1,))) for i in range(count)], 0
        )
        probs_f = probs.astype(F32)
        product = probs_f * d_probs
        upper = product.astype(BF16)
        lower = (product - upper.astype(F32)).astype(BF16)
        inner = mm(jnp.concatenate([upper, lower], 1), ones)
        d_scores = (probs_f * (d_probs - inner)).astype(BF16)
        for i, r in enumerate(spans):
            block = slice(i * WIDE, (i + 1) * WIDE)
            d_query = mm(d_scores[block], keys[i][g]).astype(BF16)
            at = g * GROUP
            out_ref[r, at : at + WIDE] = d_query[:HEAD_DIM]
            out_ref[r, at + WIDE : at + GROUP] = d_query[HEAD_DIM:]
            d_keys[i].append(fold(mm(d_scores[block], stacked(projected_ref, r, g), down)) * scale)
            d_values[i].append(fold(mm(probs[block], d_rows[i], down)))
    for i, r in enumerate(spans):
        out_ref[r, width_q : width_q + width_k] = jnp.where(low, *d_keys[i]).astype(BF16)
        out_ref[r, width_q + width_k :] = jnp.where(low, *d_values[i]).astype(BF16)


def backward(where, probs, projected, d_attended, groups):
    steps = probs.shape[0]
    batch = probs.shape[2] // WIDE
    return local_call(
        functools.partial(backward_kernel, groups),
        "attend_back",
        3.4,
        where,
        [probs, projected, d_attended.reshape(steps, batch, groups * GROUP)],
        jax.ShapeDtypeStruct(projected.shape, BF16),
    )


def score_kernel(chips, where_ref, own_ref, sib_ref, own_far_ref, sib_far_ref, sum_ref, sib_sum_ref,
                 final_ref, ws_ref, prior_ref, prior_sib_ref, *refs):
    pieces, refs = refs[: 4 * chips], refs[4 * chips :]
    score_ref, attn_ref, d_att_ref, d_rows_ref, product_ref = refs
    chip, core = where_ref[0], where_ref[1]
    mine = jnp.concatenate([own_ref[...], sib_ref[...]], 0)
    other = jnp.concatenate([own_far_ref[...], sib_far_ref[...]], 0)
    sums = [ref[k] for ref in (sum_ref, sib_sum_ref) for k in range(ref.shape[0])]
    attn = jnp.concatenate(
        [jnp.where(core == 0, mine, other), jnp.where(core == 0, other, mine)], 1
    )
    count = attn.shape[0]
    upper = attn.astype(BF16)
    attn_ref[...] = upper
    both = jnp.concatenate([upper.astype(F32), attn - upper.astype(F32)], 0)
    product_ref[...] = both
    depth, part = pieces[0].shape
    out = [None] * 4
    for s in range(chips):
        start = pl.multiple_of((chip ^ s) * depth, depth)
        block = product_ref[:, pl.ds(start, depth)].astype(BF16)
        for k in range(4):
            x = mm(block, pieces[4 * s + k][...])
            out[k] = x if out[k] is None else out[k] + x
    out = [x[:count] + x[count:] for x in out]
    own, far = jnp.concatenate(out[:2], 1), jnp.concatenate(out[2:], 1)
    product = jnp.concatenate(
        [jnp.where(core == 0, own, far), jnp.where(core == 0, far, own)], 1
    )
    pooled = (jnp.concatenate(sums, 0) + product) * (1.0 / PASSAGE_LEN)
    inverse = lax.rsqrt(jnp.mean(pooled * pooled, -1, keepdims=True) + epsilon)
    unit = pooled * inverse
    direction = final_ref[...] * ws_ref[...]
    score = jnp.sum(unit * direction, -1, keepdims=True)
    lane = lax.broadcasted_iota(jnp.int32, score_ref.shape, 1)
    half = score_ref.shape[1] // 2
    prior = jnp.concatenate([prior_ref[...], prior_sib_ref[...]], 0)
    score_ref[...] = jnp.where(lane < half, score, 0.0) + prior

    mean = jnp.mean(unit * direction, -1, keepdims=True)
    d_rows = inverse * (direction - unit * mean) * (1.0 / PASSAGE_LEN)
    half = d_rows.shape[1] // 2
    own = jnp.where(core == 0, d_rows[:, :half], d_rows[:, half:])
    far = jnp.where(core == 0, d_rows[:, half:], d_rows[:, :half])
    d_rows_ref[...] = own
    cut = [x.astype(BF16) for x in (own[:, :part], own[:, part:], far[:, :part], far[:, part:])]
    for s in range(chips):
        back = sum(mm(cut[k], pieces[4 * s + k][...], ((1,), (1,))) for k in range(4))
        start = pl.multiple_of((chip ^ s) * depth, depth)
        product_ref[:count, pl.ds(start, depth)] = back.astype(BF16).astype(F32)
    back = product_ref[:count]
    half = back.shape[1] // 2
    d_att_ref[...] = jnp.where(core == 0, back[:, :half], back[:, half:])


def score_pass(where, attn, sums, final_gain, w_score, priors, pieces):
    count, width = 2 * attn[0].shape[0], sums[0].shape[2]
    lanes = priors[0].shape[1]
    inner = 2 * attn[0].shape[1]
    vmem = pl.BlockSpec(memory_space=pltpu.VMEM)
    return pl.pallas_call(
        functools.partial(score_kernel, len(pieces) // 4),
        in_specs=[pl.BlockSpec(memory_space=pltpu.SMEM)] + [vmem] * (10 + len(pieces)),
        out_specs=[vmem] * 4,
        out_shape=[
            jax.ShapeDtypeStruct((count, lanes), F32),
            jax.ShapeDtypeStruct((count, inner), BF16),
            jax.ShapeDtypeStruct((count, inner // 2), F32),
            jax.ShapeDtypeStruct((count, width // 2), F32),
        ],
        scratch_shapes=[pltpu.VMEM((2 * count, inner), F32)],
        compiler_params=pltpu.CompilerParams(vmem_limit_bytes=SMALL),
        cost_estimate=cost(2),
        name="pool_score",
    )(where, *attn, *sums, final_gain[None], w_score[None], *priors, *pieces)


def list_kernel(blocks, passages, where_ref, place_ref, bounds_ref, rows_ref, own_ref, sib_ref,
                *refs):
    scores = [ref[...] for ref in refs[:blocks]]
    d_rows_ref, loss_ref, d_own_ref, d_sib_ref = refs[blocks:]
    core = where_ref[1]
    pair = 2 * passages
    lanes = bounds_ref.shape[1]
    lane = lax.broadcasted_iota(jnp.int32, bounds_ref.shape, 1)
    ends, reach = bounds_ref[...], 1
    while reach < lanes:
        ends = ends + jnp.where(lane >= reach, pltpu.roll(ends, reach, 1), 0)
        reach *= 2
    starts, ends = (ends - bounds_ref[...])[:1], ends[:1]
    row = lax.broadcasted_iota(jnp.int32, (pair, lanes), 0)
    near = jnp.where(row < passages, core * passages + row, (1 - core) * passages + row - passages)
    far = jnp.where(row < passages, (1 - core) * passages + row, core * passages + row - passages)
    members = []
    for j in range(blocks):
        place = place_ref[j] * pair + (near if j <= blocks // 2 else far)
        members.append((place >= starts) & (place < ends))
    high = scores[0].shape[1] // 2
    column = [jnp.broadcast_to(score[:, :1], (pair, lanes)) for score in scores]
    heavy = [jnp.broadcast_to(score[:, high : high + 1], (pair, lanes)) for score in scores]
    peak = functools.reduce(
        jnp.maximum,
        [jnp.max(jnp.where(m, s, -1e30), 0, keepdims=True) for m, s in zip(members, column)],
    )
    total = sum(
        jnp.sum(jnp.where(m, jnp.exp(jnp.where(m, s - peak, 0.0)), 0.0), 0, keepdims=True)
        for m, s in zip(members, column)
    )
    label_total = sum(
        jnp.sum(jnp.where(m, w, 0.0), 0, keepdims=True) for m, w in zip(members, heavy)
    )
    log_norm = peak + jnp.log(total)
    own = members[0]
    log_prob = column[0][:, :1] - jnp.sum(jnp.where(own, log_norm, 0.0), 1, keepdims=True)
    target = heavy[0][:, :1] / jnp.sum(jnp.where(own, label_total, 0.0), 1, keepdims=True)
    loss = -loss_scale * jnp.sum((target * log_prob)[:passages], 0, keepdims=True)
    d_score = loss_scale * (jnp.exp(log_prob) - target)
    loss_ref[...] = jnp.broadcast_to(loss, loss_ref.shape)
    d_rows_ref[...] = (rows_ref[...] * d_score).astype(BF16)
    for k, (ref, out_ref) in enumerate(((own_ref, d_own_ref), (sib_ref, d_sib_ref))):
        for i in range(passages):
            rows = slice(i * PASSAGE_LEN, (i + 1) * PASSAGE_LEN)
            at = k * passages + i
            out_ref[rows] = (ref[rows].astype(F32) * d_score[at : at + 1]).astype(BF16)


def list_pass(where, places, bounds, rows, d_own, d_sib, scores):
    vmem = pl.BlockSpec(memory_space=pltpu.VMEM)
    smem = pl.BlockSpec(memory_space=pltpu.SMEM)
    return pl.pallas_call(
        functools.partial(list_kernel, len(scores), rows.shape[0] // 2),
        in_specs=[smem] * 2 + [vmem] * (4 + len(scores)),
        out_specs=[vmem] * 4,
        out_shape=[
            jax.ShapeDtypeStruct(rows.shape, BF16),
            jax.ShapeDtypeStruct((8, 128), F32),
            jax.ShapeDtypeStruct(d_own.shape, BF16),
            jax.ShapeDtypeStruct(d_sib.shape, BF16),
        ],
        compiler_params=pltpu.CompilerParams(vmem_limit_bytes=SMALL),
        cost_estimate=cost(2.5),
        name="list_grad",
    )(where, places, bounds, rows, d_own, d_sib, *scores)


def payload_kernel(passages, where_ref, attn_ref, d_rows_ref, loss_ref, out_ref):
    core = where_ref[1]
    attn = attn_ref[...].astype(F32)
    half = attn.shape[1] // 2
    columns = [jnp.where(core == 0, attn[:, :half], attn[:, half:]), d_rows_ref[...].astype(F32)]
    rest = jnp.broadcast_to(loss_ref[:1], (attn.shape[0], 128))
    for _ in range(3):
        columns.append(rest.astype(BF16).astype(F32))
        rest = rest - columns[-1]
    columns = jnp.concatenate(columns, 1)
    turned = jnp.concatenate([columns[passages:], columns[:passages]], 0)
    out_ref[...] = jnp.where(core == 0, columns, turned).astype(BF16)


def payload_pass(where, attn, d_rows, loss):
    count = attn.shape[0]
    vmem = pl.BlockSpec(memory_space=pltpu.VMEM)
    return pl.pallas_call(
        functools.partial(payload_kernel, count // 2),
        in_specs=[pl.BlockSpec(memory_space=pltpu.SMEM)] + [vmem] * 3,
        out_specs=vmem,
        out_shape=jax.ShapeDtypeStruct(
            (count, attn.shape[1] // 2 + d_rows.shape[1] + 3 * 128), BF16
        ),
        compiler_params=pltpu.CompilerParams(vmem_limit_bytes=SMALL),
        cost_estimate=cost(1),
        name="out_payload",
    )(where, attn, d_rows, loss)


EXTRA = 16


def out_kernel(chips, where_ref, left_ref, *refs):
    near, far, out_ref = refs[:chips], refs[chips], refs[chips + 1]
    core = where_ref[1]
    cols = out_ref.shape[1] // 2
    own_rows = out_ref.shape[0] - EXTRA
    lead = far.shape[1] - 3 * 128 - cols
    mine = jnp.concatenate([ref[...] for ref in near], 0)
    other = far[...]
    down = ((0,), (0,))
    products = [mm(left_ref[...], x[:, lead : lead + cols], down) for x in (mine, other)]
    out_ref[:own_rows, :cols] = jnp.where(core == 0, *products).astype(BF16)
    out_ref[:own_rows, cols:] = jnp.where(core == 0, *products[::-1]).astype(BF16)

    count = mine.shape[0] // chips
    losses = []
    for s in range(chips):
        total = 0.0
        for x in (mine, other):
            row = x[s * count : s * count + EXTRA, lead + cols :].astype(F32)
            total = total + (row[:, :128] + row[:, 128:256] + row[:, 256:])
        losses.append(total)
    while len(losses) > 1:
        losses = [a + b for a, b in zip(losses[0::2], losses[1::2])]
    rest = losses[0]
    parts = []
    for _ in range(3):
        parts.append(rest.astype(BF16).astype(F32))
        rest = rest - parts[-1]
    index = lax.broadcasted_iota(jnp.int32, rest.shape, 0)
    row = jnp.where(index == 0, parts[0], jnp.where(index == 1, parts[1], parts[2])).astype(BF16)
    out_ref[own_rows:] = jnp.concatenate([row] * (2 * cols // row.shape[1]), 1)


def total_kernel(*refs):
    blocks, (out_ref, loss_ref) = refs[:-2], refs[-2:]
    own_rows = out_ref.shape[0]
    out_ref[...] = sum(ref[:own_rows].astype(F32) for ref in blocks)
    losses = []
    for ref in blocks:
        rows = ref[own_rows:].astype(F32)
        losses.append(rows[0:1] + rows[1:2] + rows[2:3])
    while len(losses) > 1:
        losses = [a + b for a, b in zip(losses[0::2], losses[1::2])]
    loss_ref[...] = jnp.broadcast_to(losses[0][:, :128], loss_ref.shape)


def total_pass(blocks):
    vmem = pl.BlockSpec(memory_space=pltpu.VMEM)
    rows, width = blocks[0].shape
    return pl.pallas_call(
        total_kernel,
        in_specs=[vmem] * len(blocks),
        out_specs=[vmem] * 2,
        out_shape=[
            jax.ShapeDtypeStruct((rows - EXTRA, width), F32),
            jax.ShapeDtypeStruct((8, 128), F32),
        ],
        compiler_params=pltpu.CompilerParams(vmem_limit_bytes=SMALL),
        cost_estimate=cost(1),
        name="out_total",
    )(*blocks)


def out_pass(where, left, near, far, cols):
    vmem = pl.BlockSpec(memory_space=pltpu.VMEM)
    return pl.pallas_call(
        functools.partial(out_kernel, len(near)),
        in_specs=[pl.BlockSpec(memory_space=pltpu.SMEM)] + [vmem] * (2 + len(near)),
        out_specs=vmem,
        out_shape=jax.ShapeDtypeStruct((left.shape[1] + EXTRA, 2 * cols), BF16),
        compiler_params=pltpu.CompilerParams(vmem_limit_bytes=SMALL),
        cost_estimate=cost(1),
        name="out_rows",
    )(where, left, *near, far)


def grad_kernel(blocks, where_ref, own_ref, sib_ref, d_own_ref, d_sib_ref, *refs):
    out, (rows_ref, done) = refs[:-2], refs[-2:]
    depth, part = out[0].shape
    tile = min(depth, 256)
    down = ((0,), (0,))
    copies = []
    for n, s in enumerate(blocks):
        start = pl.multiple_of((where_ref[0] ^ s) * depth, depth)
        for k, ref in enumerate((own_ref, sib_ref)):
            copy = pltpu.make_async_copy(
                ref.at[:, pl.ds(start, depth)], rows_ref.at[n, k], done.at[n, k]
            )
            copy.start()
            copies.append(copy)
    for n in range(len(blocks)):
        copies[2 * n].wait()
        copies[2 * n + 1].wait()
        for i in range(depth // tile):
            cols = slice(i * tile, (i + 1) * tile)
            total = mm(rows_ref[n, 0, :, cols], d_own_ref[...], down)
            total = (total + mm(rows_ref[n, 1, :, cols], d_sib_ref[...], down)).astype(BF16)
            out[2 * n][cols] = total[:, :part]
            out[2 * n + 1][cols] = total[:, part:]


def grad_blocks(where, blocks, own, sib, d_own, d_sib, depth):
    part = d_own.shape[1] // 2
    count = len(blocks)
    vmem = pl.BlockSpec(memory_space=pltpu.VMEM)
    hbm = pl.BlockSpec(memory_space=pltpu.HBM)
    return pl.pallas_call(
        functools.partial(grad_kernel, tuple(blocks)),
        in_specs=[pl.BlockSpec(memory_space=pltpu.SMEM), hbm, hbm, vmem, vmem],
        out_specs=[vmem] * (2 * count),
        out_shape=[jax.ShapeDtypeStruct((depth, part), BF16)] * (2 * count),
        scratch_shapes=[
            pltpu.VMEM((count, 2, own.shape[0], depth), BF16),
            pltpu.SemaphoreType.DMA((count, 2)),
        ],
        compiler_params=pltpu.CompilerParams(vmem_limit_bytes=VMEM),
        cost_estimate=cost(2.5 * count),
        name="grad_rows",
    )(where, *held(pltpu.HBM, own, sib), d_own, d_sib)


def pick_kernel(starts, sizes, where_ref, mine_ref, come_ref, a_ref, b_ref):
    core = where_ref[1]
    mine, come = mine_ref[...].astype(F32), come_ref[...].astype(F32)
    rows = mine.shape[0]
    halves = []
    for h in range(2):
        spans = [slice(a + h * n, a + (h + 1) * n) for a, n in zip(starts, sizes)]
        halves.append([jnp.concatenate([x[:, t] for t in spans], 1) for x in (mine, come)])
    first = jnp.where(core == 0, halves[0][0], halves[1][1]).astype(BF16)
    second = jnp.where(core == 0, halves[0][1], halves[1][0]).astype(BF16)
    part = a_ref.shape[1]
    a_ref[:rows], b_ref[:rows] = first[:, :part], first[:, part:]
    a_ref[rows:], b_ref[rows:] = second[:, :part], second[:, part:]


def pick(where, mine, come, starts, sizes):
    rows = mine.shape[0]
    vmem = pl.BlockSpec(memory_space=pltpu.VMEM)
    return pl.pallas_call(
        functools.partial(pick_kernel, starts, sizes),
        in_specs=[pl.BlockSpec(memory_space=pltpu.SMEM), vmem, vmem],
        out_specs=[vmem] * 2,
        out_shape=[jax.ShapeDtypeStruct((2 * rows, sum(sizes) // 2), BF16)] * 2,
        compiler_params=pltpu.CompilerParams(vmem_limit_bytes=SMALL),
        cost_estimate=cost(1),
        name="pick_columns",
    )(where, mine, come)


def solution(mesh):
    n_list, n_fsdp = mesh.shape["list"], mesh.shape["fsdp"]
    bits = [1 << k for k in range(1, n_fsdp.bit_length() - 1)]
    pairs = n_list * n_fsdp // 2

    def across(value, distance):
        return lax.ppermute(value, "fsdp", [(i, i ^ distance) for i in range(n_fsdp)])

    def along(value, distance):
        return lax.ppermute(value, "list", [(i, i ^ distance) for i in range(n_list)])

    def partner(kind, pair):
        return (
            pair ^ 1,
            ((pair + 1) ^ 1) - 1,
            pair ^ 2,
            ((pair + 2) ^ 2) - 2,
        )[kind]

    def neighbour(value, kind):
        moves = []
        for pair in range(pairs):
            for core in (0, 1):
                other = partner(kind + core, pair)
                if 0 <= other < pairs:
                    moves.append((2 * pair + core, 2 * other + core))
        return lax.ppermute(value, ("list", "fsdp"), moves)

    def after(value, *others):
        return lax.optimization_barrier((value, others))[0]

    def gathered(value, order, far=(), wait=True):
        have = {0: value}
        for bit in order:
            first = [part for s, part in have.items() if s]
            ready = dict(have)
            if first:
                ready = {
                    s: after(part, far, first) if s else after(part, first) if wait else part
                    for s, part in have.items()
                }
            have.update({s ^ (bit >> 1): across(part, bit) for s, part in ready.items()})
        return have

    def joined(parts, come, bit):
        return {
            s: (parts[s].astype(F32) + come[s].astype(F32)).astype(BF16)
            for s in parts
            if not s & (bit >> 1)
        }

    def sent(parts, bit):
        flag = bit >> 1
        return {s ^ flag: across(parts[s], bit) for s in sorted(parts)[::-1] if s & flag}

    def local(hidden, norm_gain, w_qkv, w_out, final_gain, w_score, prior, labels, lengths):
        passages, _, width = hidden.shape
        assert 4 * passages >= LONGEST - 1
        groups = KV_HEADS // 2
        width_q, width_k = groups * GROUP, groups * HEAD_DIM
        index = lax.axis_index("fsdp")
        core = index % 2
        chip = index // 2
        where = jnp.stack([chip, core]).astype(jnp.int32)
        first_core = core == 0

        def ordered(mine, other, axis):
            return jnp.where(
                first_core,
                jnp.concatenate([mine, other], axis),
                jnp.concatenate([other, mine], axis),
            )

        starts = (0, 2 * width_q, 2 * (width_q + width_k))
        sizes = (width_q, width_k, width_k)
        come = across(w_qkv, 1)
        pair_a, pair_b = pick(where, w_qkv, come, starts, sizes)
        w_out = after(w_out, come)
        out_come = across(w_out, 1)
        hidden_sib = across(after(hidden, come), 1)

        normal, sums, before_own = norm(where, hidden, norm_gain, (pair_a, pair_b))
        prior, labels, lengths, out_come = after((prior, labels, lengths, out_come), before_own)
        lanes = -(-lengths.shape[0] // 128) * 128
        label_weight = jnp.exp(labels.astype(F32))
        small = jnp.concatenate(
            [jnp.broadcast_to(x[:, None], (passages, 64)) for x in (prior, label_weight)], 1
        )
        small_sib = across(small, 1)
        pair = lax.axis_index("list") * (n_fsdp // 2) + chip
        places = [pair] + [
            jnp.where(first_core == near, partner(2 * kind, pair), partner(2 * kind + 1, pair))
            for near in (True, False)
            for kind in range(2)
        ]
        places = jnp.stack(places).astype(jnp.int32)
        bounds = jnp.broadcast_to(
            jnp.pad(lengths, (0, lanes - lengths.shape[0]))[None], (8, lanes)
        )

        cols = w_out.shape[1] // 2
        both = ordered(w_out, out_come, 0)
        out_pair = jnp.where(first_core, both[:, :cols], both[:, cols:])
        normal_sib, sums_sib, before_sib = norm(
            where,
            after(hidden_sib, before_own, places, bounds, small_sib, out_pair),
            norm_gain,
            (pair_a, pair_b),
        )
        part_a = gathered(pair_a, bits, far=before_own)
        part_b = gathered(pair_b, bits[::-1], far=before_own)
        chips = n_fsdp // 2
        last = max(bin(s).count("1") for s in range(chips))
        weights = [{}, {}, {}]
        for s in range(chips):
            ones = bin(s).count("1")
            weights[2 if ones == last else 1 if ones else 0][s] = (part_a[s], part_b[s])

        out_pair = after(out_pair, weights[1], before_sib)
        if weights[1]:
            normal_first = after(normal, before_sib)
            before_own = partial_project(where, normal_first, weights[1], before_own)
            before_sib = partial_project(
                where, after(normal_sib, before_own), weights[1], before_sib
            )
        before_own, before_sib, weights[2] = after(
            (before_own, before_sib, weights[2]), before_sib
        )
        proj_sib, probs_sib, attn_sib = forward(where, normal_sib, weights[2], groups, before_sib)
        attn_sib = attn_sib.reshape(passages, -1)
        attn_sib_other = across(attn_sib, 1)
        normal_last = after(normal, probs_sib)
        proj_own, probs_own, attn_own = forward(where, normal_last, weights[2], groups, before_own)
        attn_own = attn_own.reshape(passages, -1)
        attn_own_other = across(attn_own, 1)
        out_a = gathered(out_pair[:, : cols // 2], bits, before_sib, False)
        out_b = gathered(out_pair[:, cols // 2 :], bits[::-1], before_sib, False)
        pieces = []
        for s in range(chips):
            pieces += [out_a[s], out_b[s]]
            gate = probs_own
            pieces += [across(after(x, gate), 1) for x in (out_a[s], out_b[s])]
        score, attn, d_attended, direction = score_pass(
            where,
            (attn_own, attn_sib, attn_sib_other, attn_own_other),
            (sums, sums_sib),
            final_gain,
            w_score,
            (small, small_sib),
            pieces,
        )
        near = [neighbour(score, kind) for kind in (0, 2)]
        scores = [score] + near + [across(x, 1) for x in near]
        d_own = backward(where, probs_own, proj_own, d_attended[:passages], groups)
        d_sib = backward(
            where, after(probs_sib, d_own), proj_sib, d_attended[passages:], groups
        )
        d_rows, loss_part, d_own, d_sib = list_pass(
            where, places, bounds, direction, d_own, d_sib, scores
        )
        inner = attn.shape[1]
        payload = payload_pass(where, attn, d_rows, loss_part)
        depth = pair_a.shape[0]
        flag_a, flag_b = bits[0] >> 1, bits[-1] >> 1
        lead = [s for s in range(chips) if s & flag_a and s & flag_b]
        rest = [s for s in range(1, chips) if s not in lead]

        def grads(blocks, *gate):
            out = grad_blocks(where, blocks, normal, normal_sib, d_own, after(d_sib, gate), depth)
            return dict(zip(blocks, out[0::2])), dict(zip(blocks, out[1::2]))

        parts_a, parts_b = grads(lead)
        first_a = {s ^ flag_a: across(parts_a[s], bits[0]) for s in lead}
        first_b = {s ^ flag_b: across(parts_b[s], bits[-1]) for s in lead}
        plane = [payload] + [across(payload, 2 * s) for s in range(1, chips)]
        more_a, more_b = {}, {}
        for s in rest:
            block_a, block_b = grads([s], parts_a, plane, more_a)
            more_a.update(block_a)
            more_b.update(block_b)
        far = across(jnp.concatenate(plane, 0), 1)
        for s in rest:
            if s & flag_a:
                first_a[s ^ flag_a] = across(more_a[s], bits[0])
            if s & flag_b:
                first_b[s ^ flag_b] = across(more_b[s], bits[-1])
        own_a, own_b = grads([0], more_a, first_a, first_b, far)
        parts_a.update(more_a)
        parts_b.update(more_b)
        parts_a.update(own_a)
        parts_b.update(own_b)
        left_a, left_b = joined(parts_a, first_a, bits[0]), joined(parts_b, first_b, bits[-1])
        place = lax.axis_index("list")
        inner = 2 * width_q
        left = ordered(
            jnp.concatenate([x[:, :width_q] for x in plane], 0), far[:, :width_q], 1
        )
        own_rows = inner // n_fsdp
        left = lax.dynamic_slice_in_dim(left, index * own_rows, own_rows, 1)
        rows = out_pass(where, left, plane, far, cols)
        blocks = rows.shape[1] // n_list
        block = lambda which: lax.dynamic_slice_in_dim(rows, which * blocks, blocks, 1)
        come_out = [block(place)]
        come_out += [along(block(place ^ distance), distance) for distance in range(1, n_list)]
        for bit_a, bit_b in zip(bits[1:], bits[::-1][1:]):
            far_a, far_b = after((sent(left_a, bit_a), sent(left_b, bit_b)), come_out)
            left_a, left_b = joined(left_a, far_a, bit_a), joined(left_b, far_b, bit_b)
        sum_a, sum_b = left_a[0], left_b[0]
        chip_sum = jnp.concatenate([sum_a, sum_b], 1)
        upper, lower = chip_sum[: depth // 2], chip_sum[depth // 2 :]
        keep = jnp.where(first_core, upper, lower)
        come = across(jnp.where(first_core, lower, upper), 1)
        columns = []
        at = 0
        for n in sizes:
            columns.append(ordered(keep[:, at : at + n], come[:, at : at + n], 1))
            at += n
        rows_sum = jnp.concatenate(columns, 1)
        place = lax.axis_index("list")

        def list_scatter(value):
            n = value.shape[1] // n_list
            block = lambda which: lax.dynamic_slice_in_dim(value, which * n, n, 1)
            total = block(place).astype(F32)
            for distance in range(1, n_list):
                total = total + along(block(place ^ distance).astype(BF16), distance).astype(F32)
            return total

        grad_qkv = list_scatter(rows_sum)

        grad_out, losses = total_pass(come_out)
        return (losses[0, 0], grad_qkv, grad_out)

    placed = (
        P(("list", "fsdp"), None, None),
        P(),
        P("fsdp", None),
        P("fsdp", None),
        P(),
        P(),
        P(("list", "fsdp")),
        P(("list", "fsdp")),
        P(),
    )
    return jax.shard_map(
        local,
        mesh=mesh,
        in_specs=placed,
        out_specs=(P(), P("fsdp", "list"), P("fsdp", "list")),
        check_vma=False,
    )
```
